32 devices in a mesh: dp: 4 (over y, x), fsdp: 8 (over z, core).
Axes of the slice: x: 2, y: 2, z: 4, core: 2. Of those that a mesh axis runs over, the one named last changes fastest.
Arguments:
- stream_in: bfloat16 [65536, 512], P(('dp', 'fsdp')), may hold values from -6 to 6
- dual_in: float32 [65536, 512], P(('dp', 'fsdp')), may hold values from -6 to 6
- segment_ids: int32 [64, 1024], P(('dp', 'fsdp')), may hold values from 0 to 8, as said below
- qkv_weight: float32 [512, 1536], P(('dp', 'fsdp')), may hold values from -0.25 to 0.25
- proj_weight: float32 [512, 512], P(('dp', 'fsdp')), may hold values from -1 to 1
- up_weight: float32 [512, 2048], P(('dp', 'fsdp')), may hold values from -0.25 to 0.25
- down_weight: float32 [2048, 512], P(('dp', 'fsdp')), may hold values from -0.1875 to 0.1875
- vectors: float32 [6144], P(('dp', 'fsdp')), may hold values from -1.2 to 2.2
- qkv_first: float32 [512, 1536], P(('dp', 'fsdp')), may hold values from -768 to 768
- proj_first: float32 [512, 512], P(('dp', 'fsdp')), may hold values from -320 to 320
- up_first: float32 [512, 2048], P(('dp', 'fsdp')), may hold values from -640 to 640
- down_first: float32 [2048, 512], P(('dp', 'fsdp')), may hold values from -1280 to 1280
- vec_first: float32 [6144], P(('dp', 'fsdp')), may hold values from -1024 to 1024
- qkv_second: float32 [512, 1536], P(('dp', 'fsdp')), may hold values from 16384 to 65536
- proj_second: float32 [512, 512], P(('dp', 'fsdp')), may hold values from 2621.44 to 10485.76
- up_second: float32 [512, 2048], P(('dp', 'fsdp')), may hold values from 10485.76 to 41943.04
- down_second: float32 [2048, 512], P(('dp', 'fsdp')), may hold values from 41943.04 to 167772.16
- vec_second: float32 [6144], P(('dp', 'fsdp')), may hold values from 6553.6 to 7864320
- cot_stream: bfloat16 [65536, 512], P(('dp', 'fsdp')), may hold values from -6 to 6
- cot_dual: bfloat16 [65536, 512], P(('dp', 'fsdp')), may hold values from -6 to 6
Outputs:
- stream_out: bfloat16 [65536, 512], P(('dp', 'fsdp'))
- dual_out: float32 [65536, 512], P(('dp', 'fsdp'))
- stream_grad: float32 [65536, 512], P(('dp', 'fsdp'))
- root_means: float32 [3], replicated
- qkv_grad: float32 [512, 1536], P(('dp', 'fsdp'))
- proj_grad: float32 [512, 512], P(('dp', 'fsdp'))
- up_grad: float32 [512, 2048], P(('dp', 'fsdp'))
- down_grad: float32 [2048, 512], P(('dp', 'fsdp'))
- vec_grad: float32 [6144], P(('dp', 'fsdp'))
- qkv_renewed: float32 [512, 1536], P(('dp', 'fsdp'))
- proj_renewed: float32 [512, 512], P(('dp', 'fsdp'))
- up_renewed: float32 [512, 2048], P(('dp', 'fsdp'))
- down_renewed: float32 [2048, 512], P(('dp', 'fsdp'))
- vec_renewed: float32 [6144], P(('dp', 'fsdp'))
- qkv_updated: float32 [512, 1536], P(('dp', 'fsdp'))
- proj_updated: float32 [512, 512], P(('dp', 'fsdp'))
- up_updated: float32 [512, 2048], P(('dp', 'fsdp'))
- down_updated: float32 [2048, 512], P(('dp', 'fsdp'))
- vec_updated: float32 [6144], P(('dp', 'fsdp'))
The draws below stay inside these ranges and needn't reach their ends.
Inputs may be any that keep to these rules, and one draw needn't show every extreme that they name: `segment_ids`: in each row the nonzero ids start at 1 and never fall; padding (id 0) fills the row's tail; at least 256 positions of every row are nonzero; ids are at most min(8, 256), documents beyond that sharing the last number.
All inputs are finite; a program needn't handle non-finite values.
Results may differ from the reference program's by a relative error of at most 0.013.
The reference program's roundings to bfloat16 on the way count: a program that leaves them out, or rounds other values in their place, can miss the bound.
Values may be sent and summed in bfloat16 or wider, within the bound.
A program may use at most 256 MiB of HBM per device.

```python
import math
import jax
import jax.numpy as jnp
from jax import lax

D = 512
FF = 2048
HEADS = 8
HEAD = 64
SEQ = 1024
ROWS_DEV = 2
STEP = 10
ROWS = 64
TOKENS = 65536
NVEC = 6144
N_DP = 4
N_FSDP = 8


def draw_segment_ids(key, part):
    key = jax.random.fold_in(key, 17)
    cut_key, jitter_key = jax.random.split(key)
    row_index = jnp.arange(ROWS, dtype=jnp.int32)
    device = row_index // ROWS_DEV
    outer = device // N_FSDP
    inner = device % N_FSDP
    quarter = SEQ // 4
    reach = 3 * SEQ // 8
    doc_limit = min(8, SEQ // 4)
    valid_len = quarter + reach * outer // max(N_DP - 1, 1) + reach * inner // max(N_FSDP - 1, 1)
    jitter = jax.random.randint(jitter_key, (ROWS,), 0, SEQ // 8 + 1)
    valid_len = jnp.maximum(valid_len - jitter, quarter)
    position = jnp.arange(SEQ, dtype=jnp.int32)[None, :]
    breaks = (jax.random.randint(cut_key, (ROWS, SEQ), 0, max(SEQ // 4, 2)) == 0).astype(jnp.int32)
    spacing = SEQ // (2 * doc_limit)
    forced = ((row_index[:, None] == ROWS - 1) & (position % spacing == 0) & (position > 0) & (position < SEQ // 2)).astype(jnp.int32)
    breaks = jnp.maximum(breaks, forced)
    breaks = jnp.where(position == 0, 0, breaks)
    numbers = jnp.minimum(1 + jnp.cumsum(breaks, axis=1), doc_limit)
    return jnp.where(position < valid_len[:, None], numbers, 0).astype(jnp.int32)


def draw_vectors(key, part):
    key = jax.random.fold_in(key, 23)
    position = jnp.arange(NVEC)
    is_gain = (position < D) | (position >= 2 * D) & (position < 3 * D)
    base = jnp.clip(jax.random.normal(key, (NVEC,), jnp.float32) * 0.3, -1.2, 1.2)
    return jnp.where(is_gain, 1.0 + base, 0.4 * base).astype(jnp.float32)


def draw_vec_second(key, part):
    key = jax.random.fold_in(key, 29)
    low_end = 0.1 * TOKENS
    high_end = 2.0 * TOKENS
    fraction = jax.random.uniform(key, (NVEC,), jnp.float32, 0.0, 1.0)
    spread = math.log(high_end) - math.log(low_end)
    return (low_end * jnp.exp(fraction * spread)).astype(jnp.float32)


def shard_levels(rng, dims, cuts, low, top_value):
    level, own = 1.0, jax.random.fold_in(rng, 6)
    for dim, parts in cuts:
        steps = jnp.exp(jax.random.uniform(jax.random.fold_in(own, dim), (parts,), jnp.float32, low / len(cuts), top_value / len(cuts)))
        level = level * jnp.repeat(steps, dims[dim] // parts).reshape([-1 if axis == dim else 1 for axis in range(len(dims))])
    return level


def noise(own_key, dims, width, most, shards=(), kind=jnp.bfloat16):
    drawn = width * jax.random.normal(own_key, dims, jnp.float32)
    if shards:
        drawn = drawn * shard_levels(own_key, dims, shards, -0.22, 0.18)
    return jnp.clip(drawn, -most, most).astype(kind)


def setup_inputs(seed: int = 0) -> dict:
    streams_of = jax.random.split(jax.random.key(seed), 21)
    return {
        "stream_in": noise(streams_of[0], (TOKENS, D), 1.0, 6.0, ((0, 32),)),
        "dual_in": noise(streams_of[1], (TOKENS, D), 1.0, 6.0, ((0, 32),), jnp.float32),
        "segment_ids": draw_segment_ids(jax.random.fold_in(streams_of[20], 71), 0),
        "qkv_weight": noise(streams_of[3], (D, 3 * D), D ** -0.5, 0.25, ((0, 32),), jnp.float32),
        "proj_weight": noise(streams_of[4], (D, D), (D // 16) ** -0.5, 1.0, ((0, 32),), jnp.float32),
        "up_weight": noise(streams_of[5], (D, FF), D ** -0.5, 0.25, ((0, 32),), jnp.float32),
        "down_weight": noise(streams_of[6], (FF, D), (FF // 2) ** -0.5, 0.1875, ((0, 32),), jnp.float32),
        "vectors": draw_vectors(jax.random.fold_in(streams_of[20], 71), 0),
        "qkv_first": noise(streams_of[8], (D, 3 * D), (0.5 * TOKENS ** 0.5), 768.0, ((0, 32),), jnp.float32),
        "proj_first": noise(streams_of[9], (D, D), (0.2 * TOKENS ** 0.5), 320.0, ((0, 32),), jnp.float32),
        "up_first": noise(streams_of[10], (D, FF), (0.4 * TOKENS ** 0.5), 640.0, ((0, 32),), jnp.float32),
        "down_first": noise(streams_of[11], (FF, D), (0.8 * TOKENS ** 0.5), 1280.0, ((0, 32),), jnp.float32),
        "vec_first": noise(streams_of[12], (NVEC,), (0.7 * TOKENS ** 0.5), 1024.0, ((0, 32),), jnp.float32),
        "qkv_second": jnp.clip(jnp.exp(math.log(65536.0) - 1.3862944 * jax.random.uniform(streams_of[13], (D, 3 * D), jnp.float32) ** shard_levels(streams_of[13], (D, 3 * D), ((0, 32),), -0.2, 0.2)), 16384.0, 65536.0),
        "proj_second": jnp.clip(jnp.exp(math.log(10485.76) - 1.3862944 * jax.random.uniform(streams_of[14], (D, D), jnp.float32) ** shard_levels(streams_of[14], (D, D), ((0, 32),), -0.2, 0.2)), 2621.44, 10485.76),
        "up_second": jnp.clip(jnp.exp(math.log(41943.04) - 1.3862944 * jax.random.uniform(streams_of[15], (D, FF), jnp.float32) ** shard_levels(streams_of[15], (D, FF), ((0, 32),), -0.2, 0.2)), 10485.76, 41943.04),
        "down_second": jnp.clip(jnp.exp(math.log(167772.16) - 1.3862944 * jax.random.uniform(streams_of[16], (FF, D), jnp.float32) ** shard_levels(streams_of[16], (FF, D), ((0, 32),), -0.2, 0.2)), 41943.04, 167772.16),
        "vec_second": draw_vec_second(jax.random.fold_in(streams_of[20], 71), 0),
        "cot_stream": noise(streams_of[18], (TOKENS, D), 1.0, 6.0, ((0, 32),)),
        "cot_dual": noise(streams_of[19], (TOKENS, D), 1.0, 6.0, ((0, 32),)),
    }


@jax.custom_vjp
def low(v):
    return lax.optimization_barrier(v.astype(jnp.bfloat16)).astype(jnp.float32)

@jax.custom_vjp
def low_back(v):
    return v

def low_keep(v):
    return (low(v), None)

def low_pass(kept, grad):
    return (grad,)

def back_keep(v):
    return (v, None)

def back_low(kept, grad):
    return (low(grad),)
low.defvjp(low_keep, low_pass)
low_back.defvjp(back_keep, back_low)
NORM_EPS = 1e-05
BETA_FIRST = 0.5
BETA_SECOND = 0.5
ADAM_EPS = 1e-08
HIGH = lax.Precision.HIGHEST

def layer_norm(summed, gain_vec, shift_vec):
    row_mean = lax.optimization_barrier(jnp.mean(summed, axis=-1, keepdims=True))
    centred = summed - row_mean
    spread = lax.optimization_barrier(jnp.mean(centred * centred, axis=-1, keepdims=True))
    return centred * lax.rsqrt(spread + NORM_EPS) * gain_vec + shift_vec

def group_forward(params, streams, duals, segments):
    qkv_w, proj_w, up_w, down_w, vec_all = params
    row_count = streams.shape[0]
    gain_one = vec_all[0:D]
    shift_one = vec_all[D:2 * D]
    gain_two = vec_all[2 * D:3 * D]
    shift_two = vec_all[3 * D:4 * D]
    bias_q = vec_all[4 * D:5 * D]
    bias_v = vec_all[5 * D:6 * D]
    bias_o = vec_all[6 * D:7 * D]
    bias_d = vec_all[7 * D:8 * D]
    bias_u = vec_all[8 * D:]
    qkv_bias = jnp.concatenate([bias_q, jnp.zeros((D,), jnp.float32), bias_v])
    qkv_lin = jnp.einsum('rsd,de->rse', streams, qkv_w, precision=HIGH) + qkv_bias
    qkv_lin = low(low_back(qkv_lin)).reshape(row_count, SEQ, 3, HEADS, HEAD)
    queries = qkv_lin[:, :, 0]
    key_rows = qkv_lin[:, :, 1]
    value_rows = qkv_lin[:, :, 2]
    scores = jnp.einsum('rqhe,rkhe->rhqk', queries, key_rows, precision=HIGH) * HEAD ** (-0.5)
    scores = low_back(scores)
    matches = segments[:, None, :, None] == segments[:, None, None, :]
    scores = jnp.where(matches, scores, -1e+30)
    row_peak = lax.optimization_barrier(jnp.max(scores, axis=-1, keepdims=True))
    row_exp = jnp.exp(scores - row_peak)
    weights_soft = low(row_exp / lax.optimization_barrier(jnp.sum(row_exp, axis=-1, keepdims=True)))
    mixed_all = jnp.einsum('rhqk,rkhe->rqhe', weights_soft, value_rows, precision=HIGH).reshape(row_count, SEQ, D)
    mixed_all = low(low_back(mixed_all))
    attn_out = low_back(jnp.einsum('rsd,de->rse', mixed_all, proj_w, precision=HIGH) + bias_o)
    first_norm = layer_norm(streams + attn_out, gain_one, shift_one)
    dual_mid = duals + attn_out
    first_low = low(first_norm)
    upper_lin = low_back(jnp.einsum('rsd,df->rsf', first_low, up_w, precision=HIGH) + bias_u)
    hidden = low(jax.nn.gelu(upper_lin, approximate=True))
    ffn_out = low_back(jnp.einsum('rsf,fd->rsd', hidden, down_w, precision=HIGH) + bias_d)
    second = layer_norm(first_norm + ffn_out, gain_two, shift_two)
    return (second, dual_mid + ffn_out, attn_out, ffn_out)

def forward(params, stream, dual_val, segment_ids):
    row_total = segment_ids.shape[0]
    per_group = math.gcd(row_total, max(1, 4096 // SEQ))
    groups = row_total // per_group
    streams = stream.reshape(groups, per_group, SEQ, D)
    duals = dual_val.reshape(groups, per_group, SEQ, D)
    segments = segment_ids.reshape(groups, per_group, SEQ)

    def visit(carry, pieces):
        return (carry, group_forward(params, pieces[0], pieces[1], pieces[2]))
    _, results = lax.scan(jax.checkpoint(visit), jnp.zeros((), jnp.float32), (streams, duals, segments))
    return tuple((member.reshape(-1, D) for member in results))

def adam_step(weight, gradient, first_old, second, step_rate, decay_rate):
    first_new = BETA_FIRST * first_old + (1.0 - BETA_FIRST) * gradient
    second_new = BETA_SECOND * second + (1.0 - BETA_SECOND) * gradient * gradient
    first_hat = first_new / (1.0 - BETA_FIRST ** STEP)
    second_hat = second_new / (1.0 - BETA_SECOND ** STEP)
    updated = weight - step_rate * (first_hat / (jnp.sqrt(second_hat) + ADAM_EPS) + decay_rate * weight)
    return (second_new, updated)

def reference(stream_in, dual_in, segment_ids, qkv_weight, proj_weight, up_weight, down_weight, vectors, qkv_first, proj_first, up_first, down_first, vec_first, qkv_second, proj_second, up_second, down_second, vec_second, cot_stream, cot_dual):
    masters = (qkv_weight, proj_weight, up_weight, down_weight, vectors)
    compute = tuple((lax.optimization_barrier(master.astype(jnp.bfloat16)).astype(jnp.float32) for master in masters))
    stream_f = stream_in.astype(jnp.float32)

    def wrapped(params, stream, dual_val):
        return forward(params, stream, dual_val, segment_ids)
    outputs, pull_back = jax.vjp(wrapped, compute, stream_f, dual_in)
    second, dual_out, attn_out, ffn_out = outputs
    weight_grads, stream_grad, dual_back = pull_back((cot_stream.astype(jnp.float32), cot_dual.astype(jnp.float32), jnp.zeros_like(attn_out), jnp.zeros_like(ffn_out)))
    valid_mask = (segment_ids.reshape(-1, 1) != 0).astype(jnp.float32)
    count = jnp.sum(valid_mask) * D
    root_means = jnp.sqrt(jnp.stack([jnp.sum(valid_mask * second * second), jnp.sum(valid_mask * attn_out * attn_out), jnp.sum(valid_mask * ffn_out * ffn_out)]) / count)
    qkv_renewed, qkv_updated = adam_step(qkv_weight, weight_grads[0], qkv_first, qkv_second, 0.04, 0.1)
    proj_renewed, proj_updated = adam_step(proj_weight, weight_grads[1], proj_first, proj_second, 0.15, 0.1)
    up_renewed, up_updated = adam_step(up_weight, weight_grads[2], up_first, up_second, 0.04, 0.1)
    down_renewed, down_updated = adam_step(down_weight, weight_grads[3], down_first, down_second, 0.03, 0.1)
    vec_renewed, vec_updated = adam_step(vectors, weight_grads[4], vec_first, vec_second, 0.2, 0.0)
    return (second.astype(jnp.bfloat16), dual_out, stream_grad, root_means, weight_grads[0], weight_grads[1], weight_grads[2], weight_grads[3], weight_grads[4], qkv_renewed, proj_renewed, up_renewed, down_renewed, vec_renewed, qkv_updated, proj_updated, up_updated, down_updated, vec_updated)
```

```python
import functools

import jax
import jax.numpy as jnp
from jax import lax
from jax.experimental import pallas as pl
from jax.experimental.pallas import tpu as pltpu
from jax.sharding import PartitionSpec as P

HEAD = 64
STEP = 10
NORM_EPS = 1e-05
BETA_FIRST = 0.5
BETA_SECOND = 0.5
ADAM_EPS = 1e-08
RATES = ((0.04, 0.1), (0.15, 0.1), (0.04, 0.1), (0.03, 0.1), (0.2, 0.0))

AXES = ("dp", "fsdp")
MESH = pl.DeviceIdType.MESH
bf16 = jnp.bfloat16
f32 = jnp.float32
ANY = pl.BlockSpec(memory_space=pl.ANY)
VMEM = pl.BlockSpec(memory_space=pltpu.VMEM)

SLOTS = 32
NEG = -1e30
QB = 256
LANES = 128


def nn(a, b):
    return jnp.dot(a, b, preferred_element_type=f32)


def nt(a, b):
    return lax.dot_general(a, b, (((1,), (1,)), ((), ())), preferred_element_type=f32)


def tn(a, b):
    return lax.dot_general(a, b, (((0,), (0,)), ((), ())), preferred_element_type=f32)


def merged(packed):
    return packed.reshape(-1, packed.shape[-1])


def half_rows():
    lane = lax.broadcasted_iota(jnp.int32, (1, LANES), 1)
    low = jnp.where(lane < HEAD, 1.0, 0.0)
    return low.astype(bf16), (1.0 - low).astype(bf16)


def segment_columns(seg_row):
    length = seg_row.shape[-1]
    place = lax.rem(lax.broadcasted_iota(jnp.int32, (LANES, length), 0), HEAD)
    ids = jnp.broadcast_to(seg_row, (LANES, length))
    same = (place == ids) & (place < 16)
    ones = jnp.where(same, 1.0, 0.0)
    against = jnp.where(place < 16, jnp.where(same, 0.0, NEG), jnp.where(place < 19, 1.0, 0.0))
    return jnp.transpose(ones).astype(bf16), jnp.transpose(against).astype(bf16)


def in_parts(value):
    first = value.astype(bf16).astype(f32)
    rest = value - first
    second = rest.astype(bf16).astype(f32)
    return first, second, rest - second


def part_columns(value, other):
    first, second, third = in_parts(value)
    lane = lax.rem(lax.broadcasted_iota(jnp.int32, value.shape, 1), HEAD)
    return jnp.where(
        lane == 16, first, jnp.where(lane == 17, second, jnp.where(lane == 18, third, other))
    )


class Place:
    def __init__(self):
        self.dp = lax.axis_index("dp")
        self.fs = lax.axis_index("fsdp")
        self.c = lax.rem(self.fs, 2)
        self.z = self.fs // 2
        x = lax.rem(self.dp, 2)
        y = self.dp // 2
        self.dpx = 2 * y + 1 - x
        self.dpy = 2 - 2 * y + x
        self.a = self.dpx + self.c * (self.dpy - self.dpx)
        self.b = self.dpy + self.c * (self.dpx - self.dpy)
        self.ab = 3 - self.dp
        self.zs = [lax.rem(self.z + k, 4) for k in range(4)]
        self.to_a = (self.a, self.fs)
        self.to_b = (self.b, self.fs)
        self.to_x = (self.dpx, self.fs)
        self.to_y = (self.dpy, self.fs)
        self.to_core = (self.dp, self.fs + 1 - 2 * self.c)
        self.to_z = [None] + [(self.dp, 2 * self.zs[k] + self.c) for k in range(1, 4)]

    def greet(self):
        barrier = pltpu.get_barrier_semaphore()
        friends = [self.to_a, self.to_b, self.to_core] + self.to_z[1:]
        for friend in friends:
            pl.semaphore_signal(barrier, inc=1, device_id=friend, device_id_type=MESH)
        pl.semaphore_wait(barrier, len(friends))


def remote(src, dst, send_sem, recv_sem, device):
    return pltpu.make_async_remote_copy(
        src_ref=src,
        dst_ref=dst,
        send_sem=send_sem,
        recv_sem=recv_sem,
        device_id=device,
        device_id_type=MESH,
    )


class Gather:
    def __init__(self, here, buf, send_sem, recv_sem):
        self.here, self.buf, self.send_sem, self.recv_sem = here, buf, send_sem, recv_sem
        self.sent = []

    def copy(self, number, d, z, c, device):
        slot = self.buf.at[d, z, c]
        return remote(slot, slot, self.send_sem.at[number], self.recv_sem.at[d, z, c], device)

    def send(self, d, z, device):
        number = len(self.sent)
        self.sent.append((number, d, z, device))
        self.copy(number, d, z, self.here.c, device).start()

    def arrive(self, d, z, c):
        self.copy(0, d, z, c, self.here.to_core).wait_recv()

    def step(self, number):
        me = self.here
        if number == 0:
            for k in range(1, 4):
                self.send(me.dp, me.z, me.to_z[k])
            for device in (me.to_a, me.to_b, me.to_core):
                self.send(me.dp, me.z, device)
        elif number < 4:
            self.arrive(me.dp, me.zs[number], me.c)
            for device in (me.to_b, me.to_a, me.to_core):
                self.send(me.dp, me.zs[number], device)
        elif number < 8:
            self.arrive(me.a, me.zs[number - 4], me.c)
            self.send(me.a, me.zs[number - 4], me.to_b)
            self.send(me.a, me.zs[number - 4], me.to_core)
        elif number < 12:
            self.arrive(me.b, me.zs[number - 8], me.c)
            self.send(me.b, me.zs[number - 8], me.to_core)
        elif number < 16:
            self.arrive(me.ab, me.zs[number - 12], me.c)
            self.send(me.ab, me.zs[number - 12], me.to_core)
        else:
            for d in range(4):
                for z in range(4):
                    self.arrive(d, z, 1 - me.c)

    def finish(self):
        for number, d, z, device in self.sent:
            self.copy(number, d, z, self.here.c, device).wait_send()


def forward_kernel(comm, scale, *refs):
    if comm:
        (x_hbm, seg, wqkv, wp, wu, wd, vec, qkv_o, mix_o, feat_o, vec_o, ga_o, gb_o, gc_o) = refs[:14]
        (x_v, qkv_v, mix_v, feat_v, fq, fk, ga, gb, gc) = refs[14:23]
        (loc, sa, ra, sb, rb, sc, rc) = refs[23:]
    else:
        (x_hbm, seg, ga_hbm, qkv_o, mix_o, feat_o, vec_o) = refs[:7]
        (x_v, qkv_v, mix_v, feat_v, fq, fk, ga) = refs[7:14]
        (loc,) = refs[14:]
    rows, length = seg.shape
    width = x_v.shape[1]
    pairs = width // LANES
    step_rows = width // SLOTS

    x_copy = pltpu.make_async_copy(x_hbm, x_v, loc.at[0])
    if comm:
        here = Place()
        here.greet()
        x_copy.start()
        own = (here.dp, here.z, here.c)
        for j in range(3):
            ga[own + (slice(j * step_rows, (j + 1) * step_rows),)] = wqkv[
                :, j * width : (j + 1) * width
            ].astype(bf16)
        index = here.dp * 8 + here.fs
        count = vec.shape[1]
        begin = index * count
        top = begin // width
        shift = begin - top * width
        line = jnp.concatenate([vec[...], jnp.zeros((1, width - count), f32)], axis=1)
        line = pltpu.roll(jnp.broadcast_to(line, (8, width)), shift, 1)
        line = jnp.concatenate([line, line], axis=0)
        row = lax.broadcasted_iota(jnp.int32, (16, width), 0)
        lane = lax.broadcasted_iota(jnp.int32, (16, width), 1)
        kept = ((row == top) & (lane >= shift)) | ((row == top + 1) & (lane < shift))
        ga[own + (slice(48, 64),)] = jnp.where(kept, line, 0.0).astype(bf16)
        first = Gather(here, ga, sa, ra)
        first.step(0)
        gb[own + (slice(0, step_rows),)] = wp[...].astype(bf16)
        for j in range(4):
            gb[own + (slice((j + 1) * step_rows, (j + 2) * step_rows),)] = wu[
                :, j * width : (j + 1) * width
            ].astype(bf16)
        gc[own] = wd[...].astype(bf16)
    else:
        x_copy.start()
        ga_copy = pltpu.make_async_copy(ga_hbm, ga, loc.at[1])
        ga_copy.start()

    for r in range(rows):
        ones, against = segment_columns(seg[r : r + 1, :])
        fq[r] = ones
        fk[r] = against

    if comm:
        for number in range(1, 17):
            first.step(number)
        second = Gather(here, gb, sb, rb)
        third = Gather(here, gc, sc, rc)
        second.step(0)
        third.step(0)
    else:
        ga_copy.wait()
    x_copy.wait()

    vec_sum = jnp.sum(ga[:, :, :, 48:64, :].astype(f32).reshape(SLOTS, 16, width), axis=0)
    vec_o[...] = vec_sum

    def project(t, carry):
        span = pl.ds(pl.multiple_of(t * 512, 512), 512)
        tile = x_v[span, :]
        for j in range(3):
            lin = nn(tile, merged(ga[:, :, :, j * step_rows : (j + 1) * step_rows, :]))
            if j == 0:
                lin = (lin + vec_sum[4:5]).astype(bf16).astype(f32) * scale
            if j == 2:
                lin = lin + vec_sum[5:6]
            low = lin.astype(bf16)
            for p in range(pairs):
                qkv_v[pairs * j + p, span, :] = low[:, p * LANES : (p + 1) * LANES]
        return carry

    lax.fori_loop(0, x_v.shape[0] // 512, project, 0)
    qkv_copy = pltpu.make_async_copy(qkv_v, qkv_o, loc.at[2])
    qkv_copy.start()
    low_half, high_half = half_rows()
    half = lax.broadcasted_iota(jnp.int32, (QB, LANES), 1) < HEAD

    def out_copies(r):
        span = pl.ds(pl.multiple_of(r * length, length), length)
        return (
            pltpu.make_async_copy(mix_v.at[span, :], mix_o.at[span, :], loc.at[3 + 2 * r]),
            pltpu.make_async_copy(feat_v.at[span, :], feat_o.at[span, :], loc.at[4 + 2 * r]),
        )

    def attend(i, carry):
        r = i // pairs
        p = lax.rem(i, pairs)
        span = pl.ds(pl.multiple_of(r * length, length), length)
        keys = qkv_v[pairs + p, span, :]
        values = qkv_v[2 * pairs + p, span, :]
        keys_in = (keys * low_half + fk[r] * high_half, keys * high_half + fk[r] * low_half)
        one_low = jnp.broadcast_to(low_half, values.shape)
        one_high = jnp.broadcast_to(high_half, values.shape)
        values_in = (
            jnp.concatenate([values * low_half, one_low], axis=1),
            jnp.concatenate([values * high_half, one_high], axis=1),
        )

        def scores(j, h):
            part = pl.ds(pl.multiple_of(r * length + j * QB, QB), QB)
            query = qkv_v[p, part, :]
            marks = fq[r, j * QB : (j + 1) * QB, :]
            mine, other = (low_half, high_half) if h == 0 else (high_half, low_half)
            return nt(query * mine + marks * other, keys_in[h])

        blocks = [(j, h) for j in range(length // QB) for h in range(2)]
        following = scores(*blocks[0])
        kept = []
        for number, (j, h) in enumerate(blocks):
            current = following
            if number + 1 < len(blocks):
                following = scores(*blocks[number + 1])
            peak = jnp.max(current, axis=1, keepdims=True)
            soft = jnp.exp(current - peak).astype(bf16)
            kept.append((peak, nn(soft, values_in[h])))
            if h == 1:
                both = kept[0][1] + kept[1][1]
                total = both[:, LANES:]
                part = pl.ds(pl.multiple_of(r * length + j * QB, QB), QB)
                columns = pl.ds(pl.multiple_of(p * LANES, LANES), LANES)
                mix_v[part, columns] = (both[:, :LANES] / total).astype(bf16)
                logs = jnp.where(half, kept[0][0], kept[1][0]) + jnp.log(total)
                logs = pltpu.roll(logs, HEAD, 1)
                marks = fq[r, j * QB : (j + 1) * QB, :].astype(f32)
                feat_v[part, columns] = part_columns(-logs, marks).astype(bf16)
                kept = []
        if comm:
            for number in range(16):
                pl.when(i == number // 2)(functools.partial(second.step, number + 1))
                pl.when(i == number // 2)(functools.partial(third.step, number + 1))
        for r_done in range(rows):

            @pl.when(i == (r_done + 1) * pairs - 1)
            def _():
                for copy in out_copies(r_done):
                    copy.start()

        return carry

    lax.fori_loop(0, rows * pairs, attend, 0)
    if comm:
        first.finish()
        second.finish()
        third.finish()
        copies = [
            pltpu.make_async_copy(src, dst, loc.at[3 + 2 * rows + k])
            for k, (src, dst) in enumerate(((ga, ga_o), (gb, gb_o), (gc, gc_o)))
        ]
        for copy in copies:
            copy.start()
        for copy in copies:
            copy.wait()
    qkv_copy.wait()
    for r in range(rows):
        for copy in out_copies(r):
            copy.wait()


def row_mean(value):
    return jnp.mean(value, axis=-1, keepdims=True)


def column_sum(value):
    return jnp.sum(value, axis=0, keepdims=True)


def middle_kernel(
    seg, vec, x_hbm, mix_hbm, dual_hbm, cs_hbm, cd_hbm, gb_hbm, gc_hbm,
    so_o, do_o, one_o, gm_o, pg_o, vg_o,
    x_v, mix_v, dual_v, cs_v, cd_v, gb, gc, low_v, spread_v, two_v, ffn_v, hid_v, slope_v, up_v, pg_v,
    in_sem, out_sem, w_sem,
):
    rows, length = seg.shape
    tokens, width = x_v.shape
    blocks = hid_v.shape[0]
    step_rows = width // SLOTS
    tile = 256
    tiles = tokens // tile
    per_row = length // tile

    def rows_of(t, size=tile):
        return pl.ds(pl.multiple_of(t * size, size), size)

    w_copies = [
        pltpu.make_async_copy(gb_hbm, gb, w_sem.at[0]),
        pltpu.make_async_copy(gc_hbm, gc, w_sem.at[1]),
    ]
    pairs_in = ((mix_hbm, mix_v), (x_hbm, x_v), (cs_hbm, cs_v), (cd_hbm, cd_v), (dual_hbm, dual_v))

    def in_copy(k, t):
        src, dst = pairs_in[k]
        return pltpu.make_async_copy(src.at[rows_of(t)], dst.at[rows_of(t)], in_sem.at[k, t])

    w_copies[0].start()
    for k in range(5):
        in_copy(k, 0).start()
    w_copies[1].start()
    for t in range(1, tiles):
        for k in range(5):
            in_copy(k, t).start()
    pairs_out = ((cs_v, so_o), (dual_v, do_o), (two_v, one_o), (ffn_v, gm_o))

    def out_copy(k, t):
        src, dst = pairs_out[k]
        return pltpu.make_async_copy(src.at[rows_of(t)], dst.at[rows_of(t)], out_sem.at[k, t])

    vg_o[...] = jnp.zeros_like(vg_o)
    gain_one, shift_one, gain_two, shift_two = (vec[k : k + 1, :] for k in range(4))
    bias_o, bias_d = vec[6:7, :], vec[7:8, :]
    w_copies[0].wait()
    w_copies[1].wait()
    lane = lax.broadcasted_iota(jnp.int32, (1, width), 1)

    def proj_weight():
        return merged(gb[:, :, :, 0:step_rows, :])

    def up_weight(f):
        return merged(gb[:, :, :, (f + 1) * step_rows : (f + 2) * step_rows, :])

    def down_weight(f):
        return merged(gc[f])

    def forward(t, carry):
        here = rows_of(t)
        for k in range(5):
            in_copy(k, t).wait()
        attn = nn(mix_v[here, :], proj_weight()) + bias_o
        first_sum = x_v[here, :].astype(f32) + attn
        centred = first_sum - row_mean(first_sum)
        spread = lax.rsqrt(row_mean(centred * centred) + NORM_EPS)
        hat = centred * spread
        x_v[here, :] = hat.astype(bf16)
        spread_v[here, :] = jnp.broadcast_to(spread, (tile, LANES))
        first_norm = hat * gain_one + shift_one
        first_low = first_norm.astype(bf16)
        low_v[here, :] = first_low
        ffn = bias_d
        for f in range(blocks):
            u = nn(first_low, up_weight(f)) + vec[8 + f : 9 + f, :]
            square = u * u
            inner = jnp.tanh(u * (0.7978845608028654 + 0.035677408136300125 * square))
            share = 0.5 + 0.5 * inner
            hidden = (u * share).astype(bf16)
            slope = share + 0.5 * u * (1.0 - inner * inner) * (
                0.7978845608028654 + 0.10703222440890037 * square
            )
            hid_v[f, here, :] = hidden
            slope_v[f, here, :] = slope.astype(bf16)
            ffn = ffn + nn(hidden, down_weight(f))
        dual_v[here, :] = dual_v[here, :] + attn + ffn
        second_sum = first_norm + ffn
        centred = second_sum - row_mean(second_sum)
        spread = lax.rsqrt(row_mean(centred * centred) + NORM_EPS)
        hat = centred * spread
        second_norm = hat * gain_two + shift_two
        cot = cs_v[here, :].astype(f32)
        cs_v[here, :] = second_norm.astype(bf16)
        out_copy(0, t).start()
        out_copy(1, t).start()
        r = t // per_row
        ids = seg[pl.ds(r, 1), pl.ds(pl.multiple_of((t - r * per_row) * tile, tile), tile)]
        valid = jnp.where(ids != 0, 1.0, 0.0)
        valid = jnp.transpose(jnp.broadcast_to(valid, (LANES, tile)))[:, 0:1]
        counts = column_sum(valid) * width
        squares = [
            jnp.sum(column_sum(valid * v * v), axis=1, keepdims=True)
            for v in (second_norm, attn, ffn)
        ]
        line = jnp.where(lane == 0, counts, 0.0)
        for k in range(3):
            line = jnp.where(lane == k + 1, squares[k], line)
        vg_o[12:13, :] += line
        scaled = cot * gain_two
        grad = (scaled - row_mean(scaled) - hat * row_mean(scaled * hat)) * spread
        two_v[here, :] = grad
        vg_o[2:3, :] += column_sum(cot * hat)
        vg_o[3:4, :] += column_sum(cot)
        grad_low = (grad + cd_v[here, :].astype(f32)).astype(bf16)
        ffn_v[here, :] = grad_low
        vg_o[7:8, :] += column_sum(grad_low.astype(f32))
        return carry

    lax.fori_loop(0, tiles, forward, 0)

    for f in range(blocks):

        def back(t, carry, f=f):
            here = rows_of(t, 512)
            grad = nt(ffn_v[here, :], down_weight(f))
            grad_up = (slope_v[f, here, :].astype(f32) * grad).astype(bf16)
            up_v[here, :] = grad_up
            vg_o[8 + f : 9 + f, :] += column_sum(grad_up.astype(f32))
            two_v[here, :] += nt(grad_up, up_weight(f))
            return carry

        lax.fori_loop(0, tokens // 512, back, 0)
        down = tn(hid_v[f], ffn_v[...])
        pg_v[f, :, :, 5 * step_rows :, :] = down.astype(bf16).reshape(4, 2, 4 * step_rows, width)
        up = tn(low_v[...], up_v[...])
        pg_v[:, :, :, (f + 1) * step_rows : (f + 2) * step_rows, :] = up.astype(bf16).reshape(
            4, 4, 2, step_rows, width
        )

    def back_first(t, carry):
        here = rows_of(t)
        grad = two_v[here, :]
        hat = x_v[here, :].astype(f32)
        vg_o[0:1, :] += column_sum(grad * hat)
        vg_o[1:2, :] += column_sum(grad)
        scaled = grad * gain_one
        spread = spread_v[here, 0:1]
        grad_one = (scaled - row_mean(scaled) - hat * row_mean(scaled * hat)) * spread
        two_v[here, :] = grad_one
        out_copy(2, t).start()
        grad_low = (grad_one + cd_v[here, :].astype(f32)).astype(bf16)
        low_v[here, :] = grad_low
        vg_o[6:7, :] += column_sum(grad_low.astype(f32))
        ffn_v[here, :] = nt(grad_low, proj_weight()).astype(bf16)
        out_copy(3, t).start()
        return carry

    lax.fori_loop(0, tiles, back_first, 0)
    proj = tn(mix_v[...], low_v[...])
    pg_v[:, :, :, 0:step_rows, :] = proj.astype(bf16).reshape(4, 4, 2, step_rows, width)
    pg_copy = pltpu.make_async_copy(pg_v, pg_o, w_sem.at[2])
    pg_copy.start()
    for t in range(tiles):
        for k in range(4):
            out_copy(k, t).wait()
    pg_copy.wait()


class Scatter:
    def __init__(self, here, send, mine, bufs, send_sem, recv_sem):
        self.here, self.source, self.mine = here, send, mine
        self.from_core, self.from_b, self.from_a, self.from_z = bufs
        self.send_sem, self.recv_sem = send_sem, recv_sem

    def copies(self, phase):
        me, mine = self.here, self.mine
        if phase == 0:
            found = [(self.source, self.from_core, me.to_core)]
        elif phase == 1:
            found = [
                (mine.at[me.b], self.from_b.at[0], me.to_b),
                (mine.at[me.ab], self.from_b.at[1], me.to_b),
            ]
        elif phase == 2:
            found = [(mine.at[me.a], self.from_a, me.to_a)]
        else:
            found = [
                (mine.at[me.dp, me.zs[k]], self.from_z.at[k - 1], me.to_z[k]) for k in range(1, 4)
            ]
        base = (0, 1, 3, 4)[phase]
        return [
            remote(src, dst, self.send_sem.at[base + k], self.recv_sem.at[base + k], device)
            for k, (src, dst, device) in enumerate(found)
        ]

    def start(self, phase):
        for copy in self.copies(phase):
            copy.start()

    def add(self, phase):
        me, mine = self.here, self.mine
        for copy in self.copies(phase):
            copy.wait_recv()

        def into(where, part):
            mine[where] = (mine[where].astype(f32) + part.astype(f32)).astype(bf16)

        if phase == 0:
            for d in range(4):
                for z in range(4):
                    into((d, z), self.from_core[d, z])
        elif phase == 1:
            for z in range(4):
                into((me.dp, z), self.from_b[0, z])
                into((me.a, z), self.from_b[1, z])
        elif phase == 2:
            for z in range(4):
                into((me.dp, z), self.from_a[z])

    def result(self):
        for copy in self.copies(3):
            copy.wait_recv()
        total = self.mine[self.here.dp, self.here.z].astype(f32)
        for k in range(3):
            total = total + self.from_z[k].astype(f32)
        return total

    def finish(self):
        for phase in range(4):
            for copy in self.copies(phase):
                copy.wait_send()


class Total:
    def __init__(self, here, parts, bufs, send_sem, recv_sem):
        self.here, self.parts, self.bufs = here, parts, bufs
        self.send_sem, self.recv_sem = send_sem, recv_sem

    def copies(self, phase):
        me, parts, bufs = self.here, self.parts, self.bufs
        if phase < 3:
            device = (me.to_core, me.to_y, me.to_x)[phase]
            found = [(parts.at[phase], bufs.at[phase], device)]
        else:
            found = [(bufs.at[3 + me.z], bufs.at[3 + me.z], me.to_z[k]) for k in range(1, 4)]
        made = []
        for k, (src, dst, device) in enumerate(found):
            recv = self.recv_sem.at[phase] if phase < 3 else self.recv_sem.at[3 + me.z]
            made.append(remote(src, dst, self.send_sem.at[phase + k], recv, device))
        return made

    def start(self, phase):
        for copy in self.copies(phase):
            copy.start()

    def add(self, phase):
        for copy in self.copies(phase):
            copy.wait_recv()
        total = self.parts[phase] + self.bufs[phase]
        if phase < 2:
            self.parts[phase + 1] = total
        else:
            self.bufs[3 + self.here.z] = total

    def result(self):
        me = self.here
        for k in range(1, 4):
            slot = self.bufs.at[3 + me.zs[k]]
            remote(slot, slot, self.send_sem.at[0], self.recv_sem.at[3 + me.zs[k]], me.to_core).wait_recv()
        return self.bufs[3] + self.bufs[4] + self.bufs[5] + self.bufs[6]

    def finish(self):
        for phase in range(4):
            for copy in self.copies(phase):
                copy.wait_send()


def backward_kernel(comm, scale, *refs):
    (seg, vg, qkv_hbm, feat_hbm, mix_hbm, gm_hbm, one_hbm, x_hbm, ga_hbm) = refs[:9]
    if comm:
        (pg_hbm, sg_o, tot_o, totq_o, vg_o) = refs[9:14]
        refs = refs[14:]
    else:
        (sg_o, pq_o, vg_o) = refs[9:12]
        refs = refs[12:]
    (qkv_v, feat_v, mix_v, gm_v, one_v, x_v, ga, gq_v, fk, pq_v, in_sem, w_sem, out_sem) = refs[:13]
    rows, length = seg.shape
    tokens, width = x_v.shape
    pairs = width // LANES
    step_rows = width // SLOTS

    def pair_copies(p):
        columns = pl.ds(pl.multiple_of(p * LANES, LANES), LANES)
        found = [(qkv_hbm.at[j * pairs + p], qkv_v.at[j * pairs + p]) for j in range(3)]
        found += [
            (src.at[:, columns], dst.at[:, columns])
            for src, dst in ((gm_hbm, gm_v), (mix_hbm, mix_v), (feat_hbm, feat_v))
        ]
        return [
            pltpu.make_async_copy(src, dst, in_sem.at[p, k]) for k, (src, dst) in enumerate(found)
        ]

    late = [
        pltpu.make_async_copy(src, dst, w_sem.at[k])
        for k, (src, dst) in enumerate(((x_hbm, x_v), (ga_hbm, ga), (one_hbm, one_v)))
    ]
    if comm:
        (mine, fc, fb, fa, fz, mine_q, qc, qb, qa, qz, vp, vb, s1, r1, s2, r2, s3, r3) = refs[13:]
        here = Place()
        here.greet()
        weights = Scatter(here, pg_hbm.at[:, :, 1 - here.c], mine, (fc, fb, fa, fz), s1, r1)
        columns_of = [
            Scatter(
                here,
                pq_v.at[p, :, :, 1 - here.c],
                mine_q.at[p],
                (qc.at[p], qb.at[p], qa.at[p], qz.at[p]),
                s2.at[p],
                r2.at[p],
            )
            for p in range(pairs)
        ]
        sums = Total(here, vp, vb, s3, r3)
        mine_copy = pltpu.make_async_copy(pg_hbm.at[:, :, here.c], mine, w_sem.at[3])
    for copy in pair_copies(0):
        copy.start()
    if comm:
        weights.start(0)
        mine_copy.start()
    for p in range(1, pairs):
        for copy in pair_copies(p):
            copy.start()
    for copy in late:
        copy.start()
    for r in range(rows):
        fk[r] = segment_columns(seg[r : r + 1, :])[1]
    low_half, high_half = half_rows()

    def attend(i, carry):
        p = i // rows
        r = lax.rem(i, rows)
        span = pl.ds(pl.multiple_of(r * length, length), length)
        columns = pl.ds(pl.multiple_of(p * LANES, LANES), LANES)

        @pl.when(r == 0)
        def _():
            for copy in pair_copies(p):
                copy.wait()

        queries = qkv_v[p, span, :]
        keys = qkv_v[pairs + p, span, :]
        values = qkv_v[2 * pairs + p, span, :]
        grads = gm_v[span, columns]
        marks = feat_v[span, columns]
        product = grads.astype(f32) * mix_v[span, columns].astype(f32)
        is_low = lax.broadcasted_iota(jnp.int32, product.shape, 1) < HEAD
        for_low = jnp.sum(jnp.where(is_low, product, 0.0), axis=1, keepdims=True)
        for_high = jnp.sum(jnp.where(is_low, 0.0, product), axis=1, keepdims=True)
        deltas = part_columns(-jnp.where(is_low, for_high, for_low), 0.0).astype(bf16)
        place = lax.rem(lax.broadcasted_iota(jnp.int32, (1, LANES), 1), HEAD)
        ones = jnp.where((place >= 16) & (place < 19), 1.0, 0.0).astype(bf16)
        queries_t = jnp.transpose(queries)
        grads_t = jnp.transpose(grads)
        key_parts, value_parts = [], []
        query_grads = [None] * (length // QB)
        for h in range(2):
            mine_h, other_h = (low_half, high_half) if h == 0 else (high_half, low_half)
            half = slice(h * HEAD, (h + 1) * HEAD)
            key_own = keys * mine_h
            key_in = key_own + fk[r] * other_h
            value_in = values * mine_h + ones * other_h
            key_sum = value_sum = None
            for j in range(length // QB):
                part = slice(j * QB, (j + 1) * QB)
                soft = jnp.exp(nt(queries[part] * mine_h + marks[part] * other_h, key_in))
                wide = nt(grads[part] * mine_h + deltas[part] * other_h, value_in)
                back = (soft * wide).astype(bf16)
                soft = soft.astype(bf16)
                moved = nn(back, key_own)
                query_grads[j] = moved if h == 0 else query_grads[j] + moved
                value_part = nn(grads_t[half, part], soft)
                key_part = nn(queries_t[half, part], back)
                value_sum = value_part if j == 0 else value_sum + value_part
                key_sum = key_part if j == 0 else key_sum + key_part
            key_parts.append(key_sum)
            value_parts.append(value_sum)
        for j in range(length // QB):
            part = pl.ds(pl.multiple_of(r * length + j * QB, QB), QB)
            gq_v[0, part, columns] = (query_grads[j] * scale).astype(bf16)
        gq_v[1, span, columns] = jnp.transpose(jnp.concatenate(key_parts, axis=0)).astype(bf16)
        gq_v[2, span, columns] = jnp.transpose(jnp.concatenate(value_parts, axis=0)).astype(bf16)

        @pl.when(r == rows - 1)
        def _():
            @pl.when(p == 0)
            def _():
                late[0].wait()

            stacked = jnp.concatenate([gq_v[j, :, columns] for j in range(3)], axis=1)
            grad = tn(x_v[...], stacked).astype(bf16).reshape(4, 4, 2, step_rows, 3 * LANES)
            for j in range(3):
                pq_v[p, :, :, :, j * step_rows : (j + 1) * step_rows, :] = grad[
                    ..., j * LANES : (j + 1) * LANES
                ]

        return carry

    lax.fori_loop(0, rows * pairs, attend, 0)
    late[1].wait()
    late[2].wait()

    vg_sum = vg[...]
    row = lax.broadcasted_iota(jnp.int32, vg_sum.shape, 0)
    for k, j in ((4, 0), (5, 2)):
        vg_sum = jnp.where(row == k, column_sum(gq_v[j].astype(f32)), vg_sum)

    if comm:
        vp[0] = vg_sum
        mine_copy.wait()
        for p in range(pairs):
            mine_q[p] = pq_v[p, :, :, here.c]
        groups = columns_of + [weights]
        for group in columns_of:
            group.start(0)
        sums.start(0)
        for phase in range(3):
            for group in groups:
                group.add(phase)
                group.start(phase + 1)
            sums.add(phase)
            sums.start(phase + 1)
    else:
        vg_o[...] = vg_sum
        pq_copy = pltpu.make_async_copy(pq_v, pq_o, out_sem.at[4])
        pq_copy.start()

    def out_copy(t):
        span = pl.ds(pl.multiple_of(t * 512, 512), 512)
        return pltpu.make_async_copy(one_v.at[span, :], sg_o.at[span, :], out_sem.at[t])

    def stream(t, carry):
        span = pl.ds(pl.multiple_of(t * 512, 512), 512)
        total = one_v[span, :]
        for j in range(3):
            total = total + nt(
                gq_v[j, span, :], merged(ga[:, :, :, j * step_rows : (j + 1) * step_rows, :])
            )
        one_v[span, :] = total
        out_copy(t).start()
        return carry

    lax.fori_loop(0, tokens // 512, stream, 0)
    if comm:
        tot_o[...] = weights.result()
        for p in range(pairs):
            totq_o[p] = columns_of[p].result()
        vg_o[...] = sums.result()
        for group in groups + [sums]:
            group.finish()
    else:
        pq_copy.wait()
    for t in range(tokens // 512):
        out_copy(t).wait()


def adam(weight, gradient, first_old, second, rates):
    step_rate, decay_rate = rates
    first_new = BETA_FIRST * first_old + (1.0 - BETA_FIRST) * gradient
    second_new = BETA_SECOND * second + (1.0 - BETA_SECOND) * gradient * gradient
    first_hat = first_new / (1.0 - BETA_FIRST**STEP)
    second_hat = second_new / (1.0 - BETA_SECOND**STEP)
    updated = weight - step_rate * (
        first_hat / (jnp.sqrt(second_hat) + ADAM_EPS) + decay_rate * weight
    )
    return second_new, updated


def update_kernel(tot, totq, vg, *refs):
    weights, firsts, seconds = refs[0:5], refs[5:10], refs[10:15]
    root, grads, renewed, updated = refs[15], refs[16:21], refs[21:26], refs[26:31]
    width = tot.shape[1]
    step_rows = width // SLOTS
    pairs = width // LANES

    def apply(k, columns, gradient):
        where = (slice(None), columns)
        grads[k][where] = gradient
        renewed[k][where], updated[k][where] = adam(
            weights[k][where], gradient, firsts[k][where], seconds[k][where], RATES[k]
        )

    for j in range(3):
        for p in range(pairs):
            begin = j * width + p * LANES
            apply(0, slice(begin, begin + LANES), totq[p, j * step_rows : (j + 1) * step_rows, :])
    apply(1, slice(None), tot[0:step_rows, :])
    for j in range(4):
        apply(2, slice(j * width, (j + 1) * width), tot[(j + 1) * step_rows : (j + 2) * step_rows, :])
    apply(3, slice(None), tot[5 * step_rows :, :])
    count = weights[4].shape[1]
    begin = (lax.axis_index("dp") * 8 + lax.axis_index("fsdp")) * count
    top = begin // width
    shift = begin - top * width
    row = lax.broadcasted_iota(jnp.int32, vg.shape, 0)
    lane = lax.broadcasted_iota(jnp.int32, vg.shape, 1)
    kept = ((row == top) & (lane >= shift)) | ((row == top + 1) & (lane < shift))
    line = column_sum(jnp.where(kept, vg[...], 0.0))
    line = pltpu.roll(jnp.broadcast_to(line, (8, width)), lax.rem(width - shift, width), 1)
    apply(4, slice(None), line[0:1, :count])
    sums = vg[12:13, 0:LANES]
    root[...] = jnp.sqrt(sums / sums[:, 0:1])


def params(**more):
    return pltpu.CompilerParams(vmem_limit_bytes=62 * 2**20, **more)


def shape(dims, kind):
    return jax.ShapeDtypeStruct(dims, kind)


def pack_columns(full, blocks):
    width = full.shape[0]
    parts = full.reshape(SLOTS, width // SLOTS, blocks, width)
    return jnp.swapaxes(parts, 1, 2).reshape(SLOTS, -1, width)


def unpack_columns(packed, blocks):
    width = packed.shape[-1]
    parts = packed.reshape(SLOTS, blocks, width // SLOTS, width)
    return jnp.swapaxes(parts, 1, 2).reshape(width, blocks * width)


def per_device(comm, *args):
    (stream_in, dual_in, segment_ids) = args[:3]
    weights, firsts, seconds = args[3:8], args[8:13], args[13:18]
    cot_stream, cot_dual = args[18:]
    tokens, width = stream_in.shape
    rows, length = segment_ids.shape
    pairs = width // LANES
    hidden = weights[2].shape[1]
    blocks = hidden // width
    unit = width // SLOTS
    scale = HEAD**-0.5
    slots = (4, 4, 2)
    dma = pltpu.SemaphoreType.DMA
    sem_gather = [dma((31,)), dma(slots)]
    rows_a, rows_b, rows_c = 4 * unit, 5 * unit, 4 * unit
    ga_shape, gb_shape, gc_shape = (slots + (n, width) for n in (rows_a, rows_b, rows_c))

    def vm(dims, kind=bf16):
        return pltpu.VMEM(dims, kind)

    flat = (tokens, width)
    common_out = [
        shape((3 * pairs, tokens, LANES), bf16),
        shape(flat, bf16),
        shape(flat, bf16),
        shape((16, width), f32),
    ]
    common_scratch = [
        vm(flat),
        vm((3 * pairs, tokens, LANES)),
        vm(flat),
        vm(flat),
        vm((rows, length, LANES)),
        vm((rows, length, LANES)),
        vm(ga_shape),
    ]
    cost = pl.CostEstimate(flops=8 * 10**9, bytes_accessed=2 * 10**7, transcendentals=2 * 10**7)
    if comm:
        masters = [w if w.ndim == 2 else w.reshape(1, -1) for w in weights]
        qkv, mix, feat, vec, ga, gb, gc = pl.pallas_call(
            functools.partial(forward_kernel, True, scale),
            out_shape=common_out + [shape(s, bf16) for s in (ga_shape, gb_shape, gc_shape)],
            in_specs=[ANY] + [VMEM] * 6,
            out_specs=[ANY] * 3 + [VMEM] + [ANY] * 3,
            scratch_shapes=common_scratch
            + [vm(gb_shape), vm(gc_shape), dma((16,))]
            + sem_gather * 3,
            compiler_params=params(collective_id=0, has_side_effects=True),
            cost_estimate=cost,
            name="gather_forward",
        )(stream_in, segment_ids, *masters)
    else:
        full = [lax.all_gather(w.astype(bf16), AXES, axis=0, tiled=True) for w in weights]
        vec_pad = jnp.pad(full[4].reshape(-1, width), ((0, 4), (0, 0)))
        vec_pad = jnp.concatenate([vec_pad[None], jnp.zeros((SLOTS - 1, 16, width), bf16)], axis=0)
        ga = jnp.concatenate([pack_columns(full[0], 3), vec_pad], axis=1).reshape(ga_shape)
        gb = jnp.concatenate(
            [pack_columns(full[1], 1), pack_columns(full[2], blocks)], axis=1
        ).reshape(gb_shape)
        gc = full[3].reshape(gc_shape)
        qkv, mix, feat, vec = pl.pallas_call(
            functools.partial(forward_kernel, False, scale),
            out_shape=common_out,
            in_specs=[ANY, VMEM, ANY],
            out_specs=[ANY] * 3 + [VMEM],
            scratch_shapes=common_scratch + [dma((16,))],
            compiler_params=params(),
            cost_estimate=cost,
            name="forward",
        )(stream_in, segment_ids, ga)

    pg_shape = slots + (9 * unit, width)
    tiles = tokens // 256
    stream_out, dual_out, grad_one, grad_mixed, pg, vg = pl.pallas_call(
        middle_kernel,
        out_shape=[
            shape(flat, bf16),
            shape(flat, f32),
            shape(flat, f32),
            shape(flat, bf16),
            shape(pg_shape, bf16),
            shape((16, width), f32),
        ],
        in_specs=[VMEM, VMEM] + [ANY] * 7,
        out_specs=[ANY] * 5 + [VMEM],
        scratch_shapes=[
            vm(flat),
            vm(flat),
            vm(flat, f32),
            vm(flat),
            vm(flat),
            vm(gb_shape),
            vm(gc_shape),
            vm(flat),
            vm((tokens, LANES), f32),
            vm(flat, f32),
            vm(flat),
            vm((blocks, tokens, width)),
            vm((blocks, tokens, width)),
            vm(flat),
            vm(pg_shape),
            dma((5, tiles)),
            dma((4, tiles)),
            dma((3,)),
        ],
        compiler_params=params(),
        cost_estimate=pl.CostEstimate(
            flops=3 * 10**10, bytes_accessed=4 * 10**7, transcendentals=4 * 10**6
        ),
        name="feed_forward",
    )(segment_ids, vec, stream_in, mix, dual_in, cot_stream, cot_dual, gb, gc)

    pq_shape = (pairs,) + slots + (3 * unit, LANES)
    scratch = [
        vm((3 * pairs, tokens, LANES)),
        vm(flat),
        vm(flat),
        vm(flat),
        vm(flat, f32),
        vm(flat),
        vm(ga_shape),
        vm((3,) + flat),
        vm((rows, length, LANES)),
        vm(pq_shape),
        dma((pairs, 6)),
        dma((4,)),
        dma((8,)),
    ]
    operands = (segment_ids, vg, qkv, feat, mix, grad_mixed, grad_one, stream_in, ga)
    cost = pl.CostEstimate(flops=2 * 10**10, bytes_accessed=3 * 10**7, transcendentals=2 * 10**7)
    if comm:
        tail = (9 * unit, width)
        tail_q = (3 * unit, LANES)
        stream_grad, tot, totq, vg = pl.pallas_call(
            functools.partial(backward_kernel, True, scale),
            out_shape=[
                shape(flat, f32),
                shape(tail, f32),
                shape((pairs,) + tail_q, f32),
                shape((16, width), f32),
            ],
            in_specs=[VMEM, VMEM] + [ANY] * 8,
            out_specs=[ANY] + [VMEM] * 3,
            scratch_shapes=scratch
            + [vm(s + tail) for s in ((4, 4), (4, 4), (2, 4), (4,), (3,))]
            + [vm((pairs,) + s + tail_q) for s in ((4, 4), (4, 4), (2, 4), (4,), (3,))]
            + [vm((3, 16, width), f32), vm((7, 16, width), f32)]
            + [dma((7,)), dma((7,)), dma((pairs, 7)), dma((pairs, 7)), dma((6,)), dma((7,))],
            compiler_params=params(collective_id=1, has_side_effects=True),
            cost_estimate=cost,
            name="backward_scatter",
        )(*operands, pg)
        outs = pl.pallas_call(
            update_kernel,
            out_shape=[shape((1, LANES), f32)]
            + [shape(w.shape, f32) for _ in range(3) for w in masters],
            in_specs=[VMEM] * 18,
            out_specs=[VMEM] * 16,
            compiler_params=params(),
            name="update",
        )(tot, totq, vg, *masters, *firsts[:4], firsts[4].reshape(1, -1), *seconds[:4], seconds[4].reshape(1, -1))
        root_means = outs[0][0, 1:4]
        grads, renewed, updated = (
            [v.reshape(w.shape) for v, w in zip(outs[k : k + 5], weights)] for k in (1, 6, 11)
        )
    else:
        stream_grad, pq, vg = pl.pallas_call(
            functools.partial(backward_kernel, False, scale),
            out_shape=[shape(flat, f32), shape(pq_shape, bf16), shape((16, width), f32)],
            in_specs=[VMEM, VMEM] + [ANY] * 7,
            out_specs=[ANY, ANY, VMEM],
            scratch_shapes=scratch,
            compiler_params=params(),
            cost_estimate=cost,
            name="backward",
        )(*operands)
        pq = jnp.moveaxis(pq.reshape(pairs, SLOTS, 3 * unit, LANES), 0, 2).reshape(SLOTS, 3 * unit, width)
        pg = pg.reshape(SLOTS, 9 * unit, width)
        partial = [
            unpack_columns(pq, 3),
            unpack_columns(pg[:, :unit], 1),
            unpack_columns(pg[:, unit : 5 * unit], blocks),
            pg[:, 5 * unit :].reshape(hidden, width),
            vg[:12].reshape(-1),
        ]
        grads = [
            lax.psum_scatter(g.astype(f32), AXES, scatter_dimension=0, tiled=True) for g in partial
        ]
        totals = lax.psum(vg[12, :4], AXES)
        root_means = jnp.sqrt(totals[1:] / totals[0])
        made = [adam(*four) for four in zip(weights, grads, firsts, seconds, RATES)]
        renewed, updated = ([m[k] for m in made] for k in range(2))
    return (stream_out, dual_out, stream_grad, root_means, *grads, *renewed, *updated)


def solution(mesh):
    sizes = dict(mesh.shape)
    comm = sizes["dp"] == 4 and sizes["fsdp"] == 8
    matrix, line = P(AXES, None), P(AXES)
    five = (matrix, matrix, matrix, matrix, line)
    in_specs = (matrix,) * 3 + five * 3 + (matrix, matrix)
    out_specs = (matrix,) * 3 + (P(),) + five * 3
    return jax.shard_map(
        functools.partial(per_device, comm),
        mesh=mesh,
        in_specs=in_specs,
        out_specs=out_specs,
        check_vma=False,
    )
```

```python
import functools

import jax
import jax.numpy as jnp
from jax import lax
from jax.experimental import pallas as pl
from jax.experimental.pallas import tpu as pltpu
from jax.sharding import PartitionSpec as P

HEAD = 64
STEP = 10
NORM_EPS = 1e-05
BETA_FIRST = 0.5
BETA_SECOND = 0.5
ADAM_EPS = 1e-08
RATES = ((0.04, 0.1), (0.15, 0.1), (0.04, 0.1), (0.03, 0.1), (0.2, 0.0))

AXES = ("dp", "fsdp")
MESH = pl.DeviceIdType.MESH
bf16 = jnp.bfloat16
f32 = jnp.float32
ANY = pl.BlockSpec(memory_space=pl.ANY)
VMEM = pl.BlockSpec(memory_space=pltpu.VMEM)

SLOTS = 32
NEG = -1e30
QB = 256
LANES = 128


def nn(a, b):
    return jnp.dot(a, b, preferred_element_type=f32)


def nt(a, b):
    return lax.dot_general(a, b, (((1,), (1,)), ((), ())), preferred_element_type=f32)


def tn(a, b):
    return lax.dot_general(a, b, (((0,), (0,)), ((), ())), preferred_element_type=f32)


def merged(packed):
    return packed.reshape(-1, packed.shape[-1])


def half_rows():
    lane = lax.broadcasted_iota(jnp.int32, (1, LANES), 1)
    low = jnp.where(lane < HEAD, 1.0, 0.0)
    return low.astype(bf16), (1.0 - low).astype(bf16)


def segment_columns(seg_row):
    length = seg_row.shape[-1]
    place = lax.rem(lax.broadcasted_iota(jnp.int32, (LANES, length), 0), HEAD)
    ids = jnp.broadcast_to(seg_row, (LANES, length))
    same = (place == ids) & (place < 16)
    ones = jnp.where(same, 1.0, 0.0)
    against = jnp.where(place < 16, jnp.where(same, 0.0, NEG), jnp.where(place < 19, 1.0, 0.0))
    return jnp.transpose(ones).astype(bf16), jnp.transpose(against).astype(bf16)


def in_parts(value):
    first = value.astype(bf16).astype(f32)
    rest = value - first
    second = rest.astype(bf16).astype(f32)
    return first, second, rest - second


def part_columns(value, other):
    first, second, third = in_parts(value)
    lane = lax.rem(lax.broadcasted_iota(jnp.int32, value.shape, 1), HEAD)
    return jnp.where(
        lane == 16, first, jnp.where(lane == 17, second, jnp.where(lane == 18, third, other))
    )


class Place:
    def __init__(self):
        self.dp = lax.axis_index("dp")
        self.fs = lax.axis_index("fsdp")
        self.c = lax.rem(self.fs, 2)
        self.z = self.fs // 2
        x = lax.rem(self.dp, 2)
        y = self.dp // 2
        self.dpx = 2 * y + 1 - x
        self.dpy = 2 - 2 * y + x
        self.a = self.dpx + self.c * (self.dpy - self.dpx)
        self.b = self.dpy + self.c * (self.dpx - self.dpy)
        self.ab = 3 - self.dp
        self.zs = [lax.rem(self.z + k, 4) for k in range(4)]
        self.to_a = (self.a, self.fs)
        self.to_b = (self.b, self.fs)
        self.to_x = (self.dpx, self.fs)
        self.to_y = (self.dpy, self.fs)
        self.to_ab = (self.ab, self.fs)
        self.to_core = (self.dp, self.fs + 1 - 2 * self.c)
        self.to_z = [None] + [(self.dp, 2 * self.zs[k] + self.c) for k in range(1, 4)]

    def greet(self):
        friends = [self.to_a, self.to_b, self.to_ab, self.to_core] + self.to_z[1:]
        for friend in friends:
            pl.semaphore_signal(
                pltpu.get_barrier_semaphore(), inc=1, device_id=friend, device_id_type=MESH
            )

    def greeted(self):
        pl.semaphore_wait(pltpu.get_barrier_semaphore(), 7)


def remote(src, dst, send_sem, recv_sem, device):
    return pltpu.make_async_remote_copy(
        src_ref=src,
        dst_ref=dst,
        send_sem=send_sem,
        recv_sem=recv_sem,
        device_id=device,
        device_id_type=MESH,
    )


class Gather:
    def __init__(self, here, buf, columns, send_sem, recv_sem, straight):
        self.here, self.buf, self.columns = here, buf, columns
        self.send_sem, self.recv_sem, self.straight = send_sem, recv_sem, straight
        self.sent = []

    def slot_copy(self, number, z, device):
        slot = self.buf.at[self.here.dp, z, self.here.c, :, self.columns]
        return remote(slot, slot, self.send_sem.at[number], self.recv_sem.at[z], device)

    def line_copy(self, number, d, c, device):
        line = self.buf.at[d, :, c, :, self.columns]
        base = 4 if device is not self.here.to_core else 8
        return remote(line, line, self.send_sem.at[number], self.recv_sem.at[base + d], device)

    def send(self, d, *devices):
        for device in devices:
            number = 3 + len(self.sent)
            self.sent.append((d, device))
            self.line_copy(number, d, self.here.c, device).start()

    def arrive(self, d):
        self.line_copy(0, d, self.here.c, self.here.to_a).wait_recv()

    def step(self, number):
        me = self.here
        if number == 0:
            for k in range(1, 4):
                self.slot_copy(k - 1, me.z, me.to_z[k]).start()
        elif number == 1:
            for k in range(1, 4):
                self.slot_copy(0, me.zs[k], me.to_z[k]).wait_recv()
            if self.straight:
                self.send(me.dp, me.to_ab, me.to_a, me.to_b, me.to_core)
            else:
                self.send(me.dp, me.to_a, me.to_b, me.to_core)
        elif number == 2:
            self.arrive(me.a)
            self.send(me.a, *([me.to_core] if self.straight else [me.to_b, me.to_core]))
        elif number == 3:
            for d in (me.b, me.ab):
                self.arrive(d)
                self.send(d, me.to_core)
        else:
            for d in range(4):
                self.line_copy(0, d, 1 - me.c, me.to_core).wait_recv()

    def finish(self):
        me = self.here
        for k in range(1, 4):
            self.slot_copy(k - 1, me.z, me.to_z[k]).wait_send()
        for number, (d, device) in enumerate(self.sent):
            self.line_copy(3 + number, d, me.c, device).wait_send()


def forward_kernel(comm, scale, *refs):
    if comm:
        (x_hbm, seg, wqkv, wp, wu, wd, vec, qkv_o, mix_o, feat_o, vec_o, ga_o, gb_o, gc_o) = refs[:14]
        (x_v, *qkv_p, mix_v, feat_v, fq, fk, ga, gb, gc) = refs[14:26]
        (loc, sa, ra, sb, rb, sc, rc) = refs[26:]
    else:
        (x_hbm, seg, ga_hbm, qkv_o, mix_o, feat_o, vec_o) = refs[:7]
        (x_v, *qkv_p, mix_v, feat_v, fq, fk, ga) = refs[7:17]
        (loc,) = refs[17:]
    rows, length = seg.shape
    width = x_v.shape[1]
    pairs = width // LANES
    step_rows = width // SLOTS

    x_copy = pltpu.make_async_copy(x_hbm, x_v, loc.at[0])
    count = SLOTS * 6
    if comm:
        here = Place()
        here.greet()
        own = (here.dp, here.z, here.c)
        for p in range(pairs):
            for j in range(3):
                begin = j * width + p * LANES
                ga[(p,) + own + (slice(None), slice(j * LANES, (j + 1) * LANES))] = wqkv[
                    :, begin : begin + LANES
                ].astype(bf16)
        rest = jnp.concatenate([vec[:, LANES:], jnp.zeros((1, 2 * LANES - count), f32)], axis=1)
        row = lax.broadcasted_iota(jnp.int32, (step_rows, LANES), 0)
        tile = jnp.where(row == 0, vec[:, :LANES], jnp.where(row == 1, rest, 0.0))
        ga[(0,) + own + (slice(None), slice(3 * LANES, 4 * LANES))] = tile.astype(bf16)
        gathers = [
            Gather(here, ga.at[p], slice(0, 4 * LANES if p == 0 else 3 * LANES), sa.at[p], ra.at[p], True)
            for p in range(pairs)
        ]
        every = slice(0, width)
        gathers.append(Gather(here, gb, every, sb, rb, False))
        gathers.append(Gather(here, gc, every, sc, rc, False))
        here.greeted()
        gathers[0].step(0)
        x_copy.start()
        for p in range(1, pairs):
            gathers[p].step(0)
        gb[own + (slice(0, step_rows),)] = wp[...].astype(bf16)
        for j in range(4):
            gb[own + (slice((j + 1) * step_rows, (j + 2) * step_rows),)] = wu[
                :, j * width : (j + 1) * width
            ].astype(bf16)
        gc[own] = wd[...].astype(bf16)
    else:
        x_copy.start()
        ga_copy = pltpu.make_async_copy(ga_hbm, ga, loc.at[1])
        ga_copy.start()

    def marks_of(r):
        ones, against = segment_columns(seg[r : r + 1, :])
        fq[r] = ones
        fk[r] = against

    def transfer(*steps):
        for group, number in steps:
            gathers[group].step(number)

    if comm:
        transfer((0, 1), (4, 0), (1, 1))
        marks_of(0)
        transfer((0, 2), (0, 3), (2, 1), (5, 0))
        for r in range(1, rows):
            marks_of(r)
        transfer((0, 4))
    else:
        for r in range(rows):
            marks_of(r)
        ga_copy.wait()
    x_copy.wait()

    lane = lax.broadcasted_iota(jnp.int32, (1, LANES), 1)

    def half_of(number, upper):
        part = number % 3
        row = part // 2
        i = number // 3
        tile = ga[0, i // 8, i % 8 // 2, i % 2, :, 3 * LANES : 4 * LANES].astype(f32)
        tile = tile if upper == (part == 1) else pltpu.roll(tile, HEAD, 1)
        return tile[row : row + 1, :]

    def assemble(first, last):
        for t in range(first, last):
            line = jnp.where(lane < HEAD, half_of(2 * t, False), half_of(2 * t + 1, True))
            vec_o[t // 4 : t // 4 + 1, t % 4 * LANES : (t % 4 + 1) * LANES] = line

    assemble(4 * pairs, 6 * pairs)

    def project(p, part):
        lin = nn(x_v[part, :], merged(ga[p, :, :, :, :, : 3 * LANES]))
        columns = slice(p * LANES, (p + 1) * LANES)
        query = (lin[:, :LANES] + vec_o[4:5, columns]).astype(bf16).astype(f32) * scale
        qkv_p[p][0, part, :] = query.astype(bf16)
        qkv_p[p][1, part, :] = lin[:, LANES : 2 * LANES].astype(bf16)
        qkv_p[p][2, part, :] = (lin[:, 2 * LANES :] + vec_o[5:6, columns]).astype(bf16)

    for t in range(rows * length // 512):
        project(0, slice(t * 512, (t + 1) * 512))
    if comm:
        transfer((1, 2), (1, 3))
    assemble(0, 4 * pairs)
    assemble(6 * pairs, 12 * pairs)
    vec_o[12:16, :] = jnp.zeros((4, width), f32)
    low_half, high_half = half_rows()
    half = lax.broadcasted_iota(jnp.int32, (QB, LANES), 1) < HEAD

    def attend(p, r):
        span = slice(r * length, (r + 1) * length)
        columns = slice(p * LANES, (p + 1) * LANES)
        keys = qkv_p[p][1, span, :]
        values = qkv_p[p][2, span, :]
        keys_in = (keys * low_half + fk[r] * high_half, keys * high_half + fk[r] * low_half)
        one_low = jnp.broadcast_to(low_half, values.shape)
        one_high = jnp.broadcast_to(high_half, values.shape)
        values_in = (
            jnp.concatenate([values * low_half, one_low], axis=1),
            jnp.concatenate([values * high_half, one_high], axis=1),
        )

        def scores(j, h):
            part = slice(r * length + j * QB, r * length + (j + 1) * QB)
            query = qkv_p[p][0, part, :]
            marks = fq[r, j * QB : (j + 1) * QB, :]
            mine, other = (low_half, high_half) if h == 0 else (high_half, low_half)
            return nt(query * mine + marks * other, keys_in[h])

        blocks = [(j, h) for j in range(length // QB) for h in range(2)]
        following = scores(*blocks[0])
        kept = []
        for number, (j, h) in enumerate(blocks):
            current = following
            if number + 1 < len(blocks):
                following = scores(*blocks[number + 1])
            part = slice(r * length + j * QB, r * length + (j + 1) * QB)
            if r == rows - 1 and p + 1 < pairs:
                share = rows * length // len(blocks)
                project(p + 1, slice(number * share, (number + 1) * share))
            peak = jnp.max(current, axis=1, keepdims=True)
            soft = jnp.exp(current - peak).astype(bf16)
            kept.append((peak, nn(soft, values_in[h])))
            if h == 1:
                both = kept[0][1] + kept[1][1]
                total = both[:, LANES:]
                mix_v[part, columns] = (both[:, :LANES] / total).astype(bf16)
                logs = jnp.where(half, kept[0][0], kept[1][0]) + jnp.log(total)
                logs = pltpu.roll(logs, HEAD, 1)
                marks = fq[r, j * QB : (j + 1) * QB, :].astype(f32)
                feat_v[part, columns] = part_columns(-logs, marks).astype(bf16)
                kept = []

    copies = []

    def copy_out(src, dst):
        copies.append(pltpu.make_async_copy(src, dst, loc.at[2 + len(copies)]))
        copies[-1].start()

    schedule = (
        ((1, 4), (2, 2), (2, 3), (3, 1)),
        ((4, 1), (3, 2), (3, 3), (5, 1)),
        ((2, 4),),
        ((4, 2),),
        ((3, 4), (5, 2)),
        ((4, 3),),
        ((5, 3),),
        ((4, 4), (5, 4)),
    )
    for p in range(pairs):
        for r in range(rows):
            attend(p, r)
            if comm:
                transfer(*schedule[rows * p + r])
        columns = slice(p * LANES, (p + 1) * LANES)
        copy_out(qkv_p[p], qkv_o.at[p])
        copy_out(mix_v.at[:, columns], mix_o.at[:, columns])
        copy_out(feat_v.at[:, columns], feat_o.at[:, columns])
        if comm:
            copy_out(ga.at[p], ga_o.at[p])
    if comm:
        copy_out(gb, gb_o)
        copy_out(gc, gc_o)
        for group in gathers:
            group.finish()
    for copy in copies:
        copy.wait()


def row_mean(value):
    return jnp.mean(value, axis=-1, keepdims=True)


def column_sum(value):
    return jnp.sum(value, axis=0, keepdims=True)


def middle_kernel(
    seg, vec, x_hbm, mix_hbm, dual_hbm, cs_hbm, cd_hbm, gb_hbm, gc_hbm,
    so_o, do_o, one_o, gm_o, pg_o, vg_o,
    x_v, mix_v, dual_v, cs_v, cd_v, gb, gc, low_v, spread_v, two_v, ffn_v, hid_v, slope_v, pg_v,
    attn_v, sum_v,
    in_sem, out_sem, w_sem,
):
    rows, length = seg.shape
    tokens, width = x_v.shape
    blocks = hid_v.shape[0]
    step_rows = width // SLOTS
    tile = 512
    tiles = tokens // tile
    per_row = length // tile

    def rows_of(t):
        return slice(t * tile, (t + 1) * tile)

    w_copies = [
        pltpu.make_async_copy(gb_hbm, gb, w_sem.at[0]),
        pltpu.make_async_copy(gc_hbm, gc, w_sem.at[1]),
    ]
    pairs_in = ((mix_hbm, mix_v), (x_hbm, x_v), (cs_hbm, cs_v), (cd_hbm, cd_v), (dual_hbm, dual_v))

    def in_copy(k, t):
        src, dst = pairs_in[k]
        return pltpu.make_async_copy(src.at[rows_of(t)], dst.at[rows_of(t)], in_sem.at[k, t])

    w_copies[0].start()
    for k in range(5):
        in_copy(k, 0).start()
    w_copies[1].start()
    for t in range(1, tiles):
        for k in range(5):
            in_copy(k, t).start()
    pairs_out = ((cs_v, so_o), (dual_v, do_o), (two_v, one_o), (ffn_v, gm_o))

    def out_copy(k, t):
        src, dst = pairs_out[k]
        return pltpu.make_async_copy(src.at[rows_of(t)], dst.at[rows_of(t)], out_sem.at[k, t])

    vg_o[...] = jnp.zeros_like(vg_o)
    gain_one, shift_one, gain_two, shift_two = (vec[k : k + 1, :] for k in range(4))
    bias_o, bias_d = vec[6:7, :], vec[7:8, :]
    w_copies[0].wait()
    w_copies[1].wait()
    lane = lax.broadcasted_iota(jnp.int32, (1, width), 1)

    def proj_weight():
        return merged(gb[:, :, :, 0:step_rows, :])

    def up_weight(f):
        return merged(gb[:, :, :, (f + 1) * step_rows : (f + 2) * step_rows, :])

    def down_weight(f):
        return merged(gc[f])

    def first_half(t):
        here = rows_of(t)
        attn = nn(mix_v[here, :], proj_weight()) + bias_o
        first_sum = x_v[here, :].astype(f32) + attn
        centred = first_sum - row_mean(first_sum)
        spread = lax.rsqrt(row_mean(centred * centred) + NORM_EPS)
        hat = centred * spread
        x_v[here, :] = hat.astype(bf16)
        spread_v[here, :] = jnp.broadcast_to(spread, (tile, LANES))
        first_norm = hat * gain_one + shift_one
        low_v[here, :] = first_norm.astype(bf16)
        two_v[here, :] = first_norm
        attn_v[t % 3] = attn

    def feed(t):
        here = rows_of(t)
        first_low = low_v[here, :]
        ffn = bias_d
        upper = nn(first_low, up_weight(0))
        for f in range(blocks):
            u = upper + vec[8 + f : 9 + f, :]
            if f + 1 < blocks:
                upper = nn(first_low, up_weight(f + 1))
            square = u * u
            inner = jnp.tanh(u * (0.7978845608028654 + 0.035677408136300125 * square))
            share = 0.5 + 0.5 * inner
            hidden = u * share
            slope = share + hidden * (1.0 - share) * (
                1.5957691216057308 + 0.21406444881780073 * square
            )
            hidden = hidden.astype(bf16)
            hid_v[f, here, :] = hidden
            slope_v[f, here, :] = slope.astype(bf16)
            ffn = ffn + nn(hidden, down_weight(f))
        sum_v[t % 2] = ffn

    def second_half(t):
        here = rows_of(t)
        attn = attn_v[t % 3]
        ffn = sum_v[t % 2]
        dual_v[here, :] = dual_v[here, :] + attn + ffn
        second_sum = two_v[here, :] + ffn
        centred = second_sum - row_mean(second_sum)
        spread = lax.rsqrt(row_mean(centred * centred) + NORM_EPS)
        hat = centred * spread
        second_norm = hat * gain_two + shift_two
        cot = cs_v[here, :].astype(f32)
        cs_v[here, :] = second_norm.astype(bf16)
        r = t // per_row
        begin = (t - r * per_row) * tile
        ids = seg[r : r + 1, begin : begin + tile]
        valid = jnp.where(ids != 0, 1.0, 0.0)
        valid = jnp.transpose(jnp.broadcast_to(valid, (LANES, tile)))[:, 0:1]
        counts = column_sum(valid) * width
        squares = [
            jnp.sum(column_sum(valid * (v * v)), axis=1, keepdims=True)
            for v in (second_norm, attn, ffn)
        ]
        line = jnp.where(lane == 0, counts, 0.0)
        for k in range(3):
            line = jnp.where(lane == k + 1, squares[k], line)
        vg_o[12:13, :] += line
        scaled = cot * gain_two
        grad = (scaled - row_mean(scaled) - hat * row_mean(scaled * hat)) * spread
        two_v[here, :] = grad
        vg_o[2:3, :] += column_sum(cot * hat)
        vg_o[3:4, :] += column_sum(cot)
        grad_low = (grad + cd_v[here, :].astype(f32)).astype(bf16)
        ffn_v[here, :] = grad_low
        vg_o[7:8, :] += column_sum(grad_low.astype(f32))

    for t in range(tiles + 2):
        if t < tiles:
            in_copy(0, t).wait()
            in_copy(1, t).wait()
        if t >= 2:
            for k in range(2, 5):
                in_copy(k, t - 2).wait()
            second_half(t - 2)
        if 1 <= t <= tiles:
            feed(t - 1)
        if t < tiles:
            first_half(t)
        if t >= 2:
            out_copy(0, t - 2).start()
            out_copy(1, t - 2).start()

    pg_copies = []

    def pg_out(*where):
        copy = pltpu.make_async_copy(pg_v.at[where], pg_o.at[where], w_sem.at[len(pg_copies) + 2])
        copy.start()
        pg_copies.append(copy)

    every = slice(None)
    for f in range(blocks):
        for t in range(tiles):
            here = rows_of(t)
            grad = nt(ffn_v[here, :], down_weight(f))
            grad_up = (slope_v[f, here, :].astype(f32) * grad).astype(bf16)
            slope_v[f, here, :] = grad_up
            vg_o[8 + f : 9 + f, :] += column_sum(grad_up.astype(f32))

    def weight_grads(f, carry):
        down = tn(hid_v[f], ffn_v[...])
        pg_v[f, :, :, 5 * step_rows :, :] = down.astype(bf16).reshape(4, 2, 4 * step_rows, width)
        up = tn(low_v[...], slope_v[f])
        rows_f = pl.ds(pl.multiple_of((f + 1) * step_rows, step_rows), step_rows)
        pg_v[:, :, :, rows_f, :] = up.astype(bf16).reshape(4, 4, 2, step_rows, width)
        return carry

    lax.fori_loop(0, blocks, weight_grads, 0)
    pg_out(every, every, every, slice(step_rows, 9 * step_rows))

    def grad_of_first(t):
        here = rows_of(t)
        grad = two_v[here, :]
        for f in range(blocks):
            grad = grad + nt(slope_v[f, here, :], up_weight(f))
        return grad

    def back_first(t, grad):
        here = rows_of(t)
        hat = x_v[here, :].astype(f32)
        vg_o[0:1, :] += column_sum(grad * hat)
        vg_o[1:2, :] += column_sum(grad)
        scaled = grad * gain_one
        spread = spread_v[here, 0:1]
        grad_one = (scaled - row_mean(scaled) - hat * row_mean(scaled * hat)) * spread
        two_v[here, :] = grad_one
        grad_low = (grad_one + cd_v[here, :].astype(f32)).astype(bf16)
        low_v[here, :] = grad_low
        vg_o[6:7, :] += column_sum(grad_low.astype(f32))
        ffn_v[here, :] = nt(grad_low, proj_weight()).astype(bf16)

    grad = grad_of_first(0)
    for t in range(tiles):
        current = grad
        if t + 1 < tiles:
            grad = grad_of_first(t + 1)
        back_first(t, current)
        out_copy(2, t).start()
        out_copy(3, t).start()
    proj = tn(mix_v[...], low_v[...])
    pg_v[:, :, :, 0:step_rows, :] = proj.astype(bf16).reshape(4, 4, 2, step_rows, width)
    pg_out(every, every, every, slice(0, step_rows))
    for t in range(tiles):
        for k in range(4):
            out_copy(k, t).wait()
    for copy in pg_copies:
        copy.wait()


class Scatter:
    def __init__(self, here, send, mine, bufs, send_sem, recv_sem):
        self.here, self.source, self.mine = here, send, mine
        self.from_core, self.from_b, self.from_a, self.from_z = bufs
        self.send_sem, self.recv_sem = send_sem, recv_sem

    def copies(self, phase):
        me, mine = self.here, self.mine
        if phase == 0:
            found = [(self.source, self.from_core, me.to_core)]
        elif phase == 1:
            found = [
                (mine.at[me.b], self.from_b.at[0], me.to_b),
                (mine.at[me.ab], self.from_b.at[1], me.to_b),
            ]
        elif phase == 2:
            found = [(mine.at[me.a], self.from_a, me.to_a)]
        else:
            found = [
                (mine.at[me.dp, me.zs[k]], self.from_z.at[k - 1], me.to_z[k]) for k in range(1, 4)
            ]
        base = (0, 1, 3, 4)[phase]
        return [
            remote(src, dst, self.send_sem.at[base + k], self.recv_sem.at[base + k], device)
            for k, (src, dst, device) in enumerate(found)
        ]

    def start(self, phase):
        for copy in self.copies(phase):
            copy.start()

    def add(self, phase):
        me, mine = self.here, self.mine
        for copy in self.copies(phase):
            copy.wait_recv()

        def into(where, part):
            mine[where] = (mine[where].astype(f32) + part.astype(f32)).astype(bf16)

        if phase == 0:
            for d in range(4):
                for z in range(4):
                    into((d, z), self.from_core[d, z])
        elif phase == 1:
            for z in range(4):
                into((me.dp, z), self.from_b[0, z])
                into((me.a, z), self.from_b[1, z])
        elif phase == 2:
            for z in range(4):
                into((me.dp, z), self.from_a[z])

    def result(self):
        for copy in self.copies(3):
            copy.wait_recv()
        total = self.mine[self.here.dp, self.here.z].astype(f32)
        for k in range(3):
            total = total + self.from_z[k].astype(f32)
        return total

    def finish(self):
        for phase in range(4):
            for copy in self.copies(phase):
                copy.wait_send()


class Total:
    def __init__(self, here, parts, bufs, send_sem, recv_sem):
        self.here, self.parts, self.bufs = here, parts, bufs
        self.send_sem, self.recv_sem = send_sem, recv_sem

    def copies(self, phase):
        me, parts, bufs = self.here, self.parts, self.bufs
        if phase < 3:
            device = (me.to_core, me.to_y, me.to_x)[phase]
            found = [(parts.at[phase], bufs.at[phase], device)]
        else:
            found = [(bufs.at[3 + me.z], bufs.at[3 + me.z], me.to_z[k]) for k in range(1, 4)]
        made = []
        for k, (src, dst, device) in enumerate(found):
            recv = self.recv_sem.at[phase] if phase < 3 else self.recv_sem.at[3 + me.z]
            made.append(remote(src, dst, self.send_sem.at[phase + k], recv, device))
        return made

    def start(self, phase):
        for copy in self.copies(phase):
            copy.start()

    def add(self, phase):
        for copy in self.copies(phase):
            copy.wait_recv()
        total = self.parts[phase] + self.bufs[phase]
        if phase < 2:
            self.parts[phase + 1] = total
        else:
            self.bufs[3 + self.here.z] = total

    def result(self):
        me = self.here
        for k in range(1, 4):
            slot = self.bufs.at[3 + me.zs[k]]
            remote(slot, slot, self.send_sem.at[0], self.recv_sem.at[3 + me.zs[k]], me.to_core).wait_recv()
        return self.bufs[3] + self.bufs[4] + self.bufs[5] + self.bufs[6]

    def finish(self):
        for phase in range(4):
            for copy in self.copies(phase):
                copy.wait_send()


def backward_kernel(comm, scale, *refs):
    (seg, vg, qkv_hbm, feat_hbm, mix_hbm, gm_hbm, one_hbm, x_hbm, ga_hbm) = refs[:9]
    if comm:
        (pg_hbm, sg_o, tot_o, totq_o, vg_o) = refs[9:14]
        refs = refs[14:]
    else:
        (sg_o, pq_o, vg_o) = refs[9:12]
        refs = refs[12:]
    (qkv_v, feat_v, mix_v, gm_v, one_v, x_v, ga, gq_v, fk, pq_v, in_sem, w_sem, out_sem) = refs[:13]
    rows, length = seg.shape
    tokens, width = x_v.shape
    pairs = width // LANES
    step_rows = width // SLOTS

    def pair_copies(p):
        columns = pl.ds(pl.multiple_of(p * LANES, LANES), LANES)
        found = [(qkv_hbm.at[p], qkv_v.at[p])]
        found += [
            (src.at[:, columns], dst.at[:, columns])
            for src, dst in ((gm_hbm, gm_v), (mix_hbm, mix_v), (feat_hbm, feat_v))
        ]
        return [
            pltpu.make_async_copy(src, dst, in_sem.at[p, k]) for k, (src, dst) in enumerate(found)
        ]

    late = [
        pltpu.make_async_copy(src, dst, w_sem.at[k])
        for k, (src, dst) in enumerate(((x_hbm, x_v), (ga_hbm, ga), (one_hbm, one_v)))
    ]
    if comm:
        (mine, fc, fb, fa, fz, mine_q, qc, qb, qa, qz, vp, vb, s1, r1, s2, r2, s3, r3) = refs[13:]
        here = Place()
        here.greet()
        weights = [
            Scatter(
                here,
                pg_hbm.at[:, :, 1 - here.c, pl.ds(g * 3 * step_rows, 3 * step_rows)],
                mine.at[g],
                (fc.at[g], fb.at[g], fa.at[g], fz.at[g]),
                s1.at[g],
                r1.at[g],
            )
            for g in range(3)
        ]
        columns_of = [
            Scatter(
                here,
                pq_v.at[p, :, :, 1 - here.c],
                mine_q.at[p],
                (qc.at[p], qb.at[p], qa.at[p], qz.at[p]),
                s2.at[p],
                r2.at[p],
            )
            for p in range(pairs)
        ]
        sums = Total(here, vp, vb, s3, r3)
        mine_copies = [
            pltpu.make_async_copy(
                pg_hbm.at[:, :, here.c, pl.ds(g * 3 * step_rows, 3 * step_rows)], mine.at[g], w_sem.at[3 + g]
            )
            for g in range(3)
        ]
    for copy in pair_copies(0):
        copy.start()
    if comm:
        for copy in mine_copies:
            copy.start()
    for p in range(1, pairs):
        for copy in pair_copies(p):
            copy.start()
    for copy in late:
        copy.start()
    for r in range(rows):
        fk[r] = segment_columns(seg[r : r + 1, :])[1]
    if comm:
        here.greeted()
        for group in weights:
            group.start(0)
    low_half, high_half = half_rows()

    def transfer(number):
        if number == 0:
            for copy in mine_copies:
                copy.wait()
        for group, steps in list(zip(weights, ((0, 2, 3), (1, 3, 4), (3, 5, 6)))) + [
            (columns_of[p], (rows * p + rows, rows * p + rows + 1, rows * p + rows + 2))
            for p in range(pairs)
        ]:
            for phase in range(3):
                if number == steps[phase]:
                    group.add(phase)
                    group.start(phase + 1)
        for p in range(pairs):
            if number == rows * (p + 1) - 1:
                mine_q[p] = pq_v[p, :, :, here.c]
                columns_of[p].start(0)

    def attend(i, carry):
        p = i // rows
        r = lax.rem(i, rows)
        span = pl.ds(pl.multiple_of(r * length, length), length)
        columns = pl.ds(pl.multiple_of(p * LANES, LANES), LANES)

        @pl.when(r == 0)
        def _():
            for copy in pair_copies(p):
                copy.wait()

        queries = qkv_v[p, 0, span, :]
        keys = qkv_v[p, 1, span, :]
        values = qkv_v[p, 2, span, :]
        grads = gm_v[span, columns]
        marks = feat_v[span, columns]
        product = grads.astype(f32) * mix_v[span, columns].astype(f32)
        is_low = lax.broadcasted_iota(jnp.int32, product.shape, 1) < HEAD
        for_low = jnp.sum(jnp.where(is_low, product, 0.0), axis=1, keepdims=True)
        for_high = jnp.sum(jnp.where(is_low, 0.0, product), axis=1, keepdims=True)
        deltas = part_columns(-jnp.where(is_low, for_high, for_low), 0.0).astype(bf16)
        place = lax.rem(lax.broadcasted_iota(jnp.int32, (1, LANES), 1), HEAD)
        ones = jnp.where((place >= 16) & (place < 19), 1.0, 0.0).astype(bf16)
        queries_t = jnp.transpose(queries)
        grads_t = jnp.transpose(grads)
        key_parts, value_parts = [], []
        query_grads = [None] * (length // QB)
        for h in range(2):
            mine_h, other_h = (low_half, high_half) if h == 0 else (high_half, low_half)
            half = slice(h * HEAD, (h + 1) * HEAD)
            key_own = keys * mine_h
            key_in = key_own + fk[r] * other_h
            value_in = values * mine_h + ones * other_h
            key_sum = value_sum = None
            for j in range(length // QB):
                part = slice(j * QB, (j + 1) * QB)
                soft = jnp.exp(nt(queries[part] * mine_h + marks[part] * other_h, key_in))
                wide = nt(grads[part] * mine_h + deltas[part] * other_h, value_in)
                back = (soft * wide).astype(bf16)
                soft = soft.astype(bf16)
                moved = nn(back, key_own)
                query_grads[j] = moved if h == 0 else query_grads[j] + moved
                value_part = nn(grads_t[half, part], soft)
                key_part = nn(queries_t[half, part], back)
                value_sum = value_part if j == 0 else value_sum + value_part
                key_sum = key_part if j == 0 else key_sum + key_part
            key_parts.append(key_sum)
            value_parts.append(value_sum)
        for j in range(length // QB):
            part = pl.ds(pl.multiple_of(r * length + j * QB, QB), QB)
            gq_v[0, part, columns] = (query_grads[j] * scale).astype(bf16)
        gq_v[1, span, columns] = jnp.transpose(jnp.concatenate(key_parts, axis=0)).astype(bf16)
        gq_v[2, span, columns] = jnp.transpose(jnp.concatenate(value_parts, axis=0)).astype(bf16)

        @pl.when(r == rows - 1)
        def _():
            @pl.when(p == 0)
            def _():
                late[0].wait()

            stacked = jnp.concatenate([gq_v[j, :, columns] for j in range(3)], axis=1)
            grad = tn(x_v[...], stacked).astype(bf16).reshape(4, 4, 2, step_rows, 3 * LANES)
            for j in range(3):
                pq_v[p, :, :, :, j * step_rows : (j + 1) * step_rows, :] = grad[
                    ..., j * LANES : (j + 1) * LANES
                ]

        if comm:
            for number in range(rows * pairs):
                pl.when(i == number)(functools.partial(transfer, number))
        return carry

    lax.fori_loop(0, rows * pairs, attend, 0)
    late[1].wait()
    late[2].wait()

    vg_sum = vg[...]
    row = lax.broadcasted_iota(jnp.int32, vg_sum.shape, 0)
    for k, j in ((4, 0), (5, 2)):
        vg_sum = jnp.where(row == k, column_sum(gq_v[j].astype(f32)), vg_sum)

    if comm:
        vp[0] = vg_sum
        sums.start(0)
    else:
        vg_o[...] = vg_sum
        pq_copy = pltpu.make_async_copy(pq_v, pq_o, out_sem.at[4])
        pq_copy.start()

    def out_copy(t):
        span = pl.ds(pl.multiple_of(t * 512, 512), 512)
        return pltpu.make_async_copy(one_v.at[span, :], sg_o.at[span, :], out_sem.at[t])

    def stream(t):
        span = pl.ds(t * 512, 512)
        total = one_v[span, :]
        for j in range(3):
            total = total + nt(
                gq_v[j, span, :],
                jnp.concatenate(
                    [merged(ga[p, :, :, :, :, j * LANES : (j + 1) * LANES]) for p in range(pairs)],
                    axis=1,
                ),
            )
        one_v[span, :] = total
        out_copy(t).start()

    for t in range(tokens // 512):
        stream(t)
        if comm:
            transfer(rows * pairs + t)
            if t < 3:
                sums.add(t)
                sums.start(t + 1)
    if comm:
        for g in range(3):
            tot_o[g * 3 * step_rows : (g + 1) * 3 * step_rows, :] = weights[g].result()
        for p in range(pairs):
            totq_o[p] = columns_of[p].result()
        vg_o[...] = sums.result()
        for group in columns_of + weights + [sums]:
            group.finish()
    else:
        pq_copy.wait()
    for t in range(tokens // 512):
        out_copy(t).wait()


def adam(weight, gradient, first_old, second, rates):
    step_rate, decay_rate = rates
    first_new = BETA_FIRST * first_old + (1.0 - BETA_FIRST) * gradient
    second_new = BETA_SECOND * second + (1.0 - BETA_SECOND) * gradient * gradient
    first_hat = first_new / (1.0 - BETA_FIRST**STEP)
    second_hat = second_new / (1.0 - BETA_SECOND**STEP)
    updated = weight - step_rate * (
        first_hat / (jnp.sqrt(second_hat) + ADAM_EPS) + decay_rate * weight
    )
    return second_new, updated


def update_kernel(tot, totq, vg, sg_hbm, *refs):
    weights, firsts, seconds = refs[0:5], refs[5:10], refs[10:15]
    sg_o, root, grads, renewed, updated = refs[15], refs[16], refs[17:22], refs[22:27], refs[27:32]
    sg_v, sem = refs[32:]
    size = sg_hbm.shape[0] // 8
    copies = []
    for t in range(8):
        span = pl.ds(t * size, size)
        copies.append(pltpu.make_async_copy(sg_hbm.at[span], sg_v.at[span], sem.at[0, t]))
        copies.append(pltpu.make_async_copy(sg_v.at[span], sg_o.at[span], sem.at[1, t]))
    for copy in copies[0::2]:
        copy.start()
    width = tot.shape[1]
    step_rows = width // SLOTS
    pairs = width // LANES

    def apply(k, columns, gradient):
        where = (slice(None), columns)
        grads[k][where] = gradient
        renewed[k][where], updated[k][where] = adam(
            weights[k][where], gradient, firsts[k][where], seconds[k][where], RATES[k]
        )

    for j in range(3):
        for p in range(pairs):
            begin = j * width + p * LANES
            apply(0, slice(begin, begin + LANES), totq[p, j * step_rows : (j + 1) * step_rows, :])
    apply(1, slice(None), tot[0:step_rows, :])
    for j in range(4):
        apply(2, slice(j * width, (j + 1) * width), tot[(j + 1) * step_rows : (j + 2) * step_rows, :])
    apply(3, slice(None), tot[5 * step_rows :, :])
    for t in range(8):
        copies[2 * t].wait()
        copies[2 * t + 1].start()
    count = weights[4].shape[1]
    begin = (lax.axis_index("dp") * 8 + lax.axis_index("fsdp")) * count
    top = begin // width
    shift = begin - top * width
    row = lax.broadcasted_iota(jnp.int32, vg.shape, 0)
    lane = lax.broadcasted_iota(jnp.int32, vg.shape, 1)
    kept = ((row == top) & (lane >= shift)) | ((row == top + 1) & (lane < shift))
    line = column_sum(jnp.where(kept, vg[...], 0.0))
    line = pltpu.roll(jnp.broadcast_to(line, (8, width)), lax.rem(width - shift, width), 1)
    apply(4, slice(None), line[0:1, :count])
    sums = vg[12:13, 0:LANES]
    means = jnp.sqrt(sums / sums[:, 0:1])
    lane = lax.broadcasted_iota(jnp.int32, means.shape, 1)
    for k in range(3):
        root[k] = jnp.sum(jnp.where(lane == k + 1, means, 0.0))
    for copy in copies[1::2]:
        copy.wait()


def params(**more):
    return pltpu.CompilerParams(vmem_limit_bytes=62 * 2**20, **more)


def shape(dims, kind):
    return jax.ShapeDtypeStruct(dims, kind)


def pack_columns(full, blocks):
    width = full.shape[0]
    parts = full.reshape(SLOTS, width // SLOTS, blocks, width)
    return jnp.swapaxes(parts, 1, 2).reshape(SLOTS, -1, width)


def unpack_columns(packed, blocks):
    width = packed.shape[-1]
    parts = packed.reshape(SLOTS, blocks, width // SLOTS, width)
    return jnp.swapaxes(parts, 1, 2).reshape(width, blocks * width)


def per_device(comm, *args):
    (stream_in, dual_in, segment_ids) = args[:3]
    weights, firsts, seconds = args[3:8], args[8:13], args[13:18]
    cot_stream, cot_dual = args[18:]
    tokens, width = stream_in.shape
    rows, length = segment_ids.shape
    pairs = width // LANES
    hidden = weights[2].shape[1]
    blocks = hidden // width
    unit = width // SLOTS
    scale = HEAD**-0.5
    slots = (4, 4, 2)
    dma = pltpu.SemaphoreType.DMA
    sem_gather = [dma((10,)), dma((12,))]
    ga_shape = (pairs,) + slots + (unit, 4 * LANES)
    gb_shape, gc_shape = (slots + (n, width) for n in (5 * unit, 4 * unit))

    def vm(dims, kind=bf16):
        return pltpu.VMEM(dims, kind)

    flat = (tokens, width)
    common_out = [
        shape((pairs, 3, tokens, LANES), bf16),
        shape(flat, bf16),
        shape(flat, bf16),
        shape((16, width), f32),
    ]
    common_scratch = [
        vm(flat),
        *[vm((3, tokens, LANES)) for _ in range(pairs)],
        vm(flat),
        vm(flat),
        vm((rows, length, LANES)),
        vm((rows, length, LANES)),
        vm(ga_shape),
    ]
    cost = pl.CostEstimate(flops=8 * 10**9, bytes_accessed=2 * 10**7, transcendentals=2 * 10**7)
    if comm:
        masters = [w if w.ndim == 2 else w.reshape(1, -1) for w in weights]
        qkv, mix, feat, vec, ga, gb, gc = pl.pallas_call(
            functools.partial(forward_kernel, True, scale),
            out_shape=common_out + [shape(s, bf16) for s in (ga_shape, gb_shape, gc_shape)],
            in_specs=[ANY] + [VMEM] * 6,
            out_specs=[ANY] * 3 + [VMEM] + [ANY] * 3,
            scratch_shapes=common_scratch
            + [vm(gb_shape), vm(gc_shape), dma((20,))]
            + [dma((pairs, 10)), dma((pairs, 12))]
            + sem_gather * 2,
            compiler_params=params(collective_id=0, has_side_effects=True),
            cost_estimate=cost,
            name="gather_forward",
        )(stream_in, segment_ids, *masters)
    else:
        full = [lax.all_gather(w.astype(bf16), AXES, axis=0, tiled=True) for w in weights]
        packed = pack_columns(full[0], 3).reshape(SLOTS, 3, unit, pairs, LANES)
        packed = packed.transpose(3, 0, 2, 1, 4).reshape(pairs, SLOTS, unit, 3 * LANES)
        vec_pad = jnp.pad(full[4].reshape(SLOTS, -1), ((0, 0), (0, HEAD))).reshape(SLOTS, 2, LANES)
        vec_pad = jnp.pad(vec_pad[None], ((0, pairs - 1), (0, 0), (0, unit - 2), (0, 0)))
        ga = jnp.concatenate([packed, vec_pad], axis=3).reshape(ga_shape)
        gb = jnp.concatenate(
            [pack_columns(full[1], 1), pack_columns(full[2], blocks)], axis=1
        ).reshape(gb_shape)
        gc = full[3].reshape(gc_shape)
        qkv, mix, feat, vec = pl.pallas_call(
            functools.partial(forward_kernel, False, scale),
            out_shape=common_out,
            in_specs=[ANY, VMEM, ANY],
            out_specs=[ANY] * 3 + [VMEM],
            scratch_shapes=common_scratch + [dma((20,))],
            compiler_params=params(),
            cost_estimate=cost,
            name="forward",
        )(stream_in, segment_ids, ga)

    pg_shape = slots + (9 * unit, width)
    tiles = tokens // 512
    stream_out, dual_out, grad_one, grad_mixed, pg, vg = pl.pallas_call(
        middle_kernel,
        out_shape=[
            shape(flat, bf16),
            shape(flat, f32),
            shape(flat, f32),
            shape(flat, bf16),
            shape(pg_shape, bf16),
            shape((16, width), f32),
        ],
        in_specs=[VMEM, VMEM] + [ANY] * 7,
        out_specs=[ANY] * 5 + [VMEM],
        scratch_shapes=[
            vm(flat),
            vm(flat),
            vm(flat, f32),
            vm(flat),
            vm(flat),
            vm(gb_shape),
            vm(gc_shape),
            vm(flat),
            vm((tokens, LANES), f32),
            vm(flat, f32),
            vm(flat),
            vm((blocks, tokens, width)),
            vm((blocks, tokens, width)),
            vm(pg_shape),
            vm((3, 512, width), f32),
            vm((2, 512, width), f32),
            dma((5, tiles)),
            dma((4, tiles)),
            dma((12,)),
        ],
        compiler_params=params(),
        cost_estimate=pl.CostEstimate(
            flops=3 * 10**10, bytes_accessed=4 * 10**7, transcendentals=4 * 10**6
        ),
        name="feed_forward",
    )(segment_ids, vec, stream_in, mix, dual_in, cot_stream, cot_dual, gb, gc)

    pq_shape = (pairs,) + slots + (3 * unit, LANES)
    scratch = [
        vm((pairs, 3, tokens, LANES)),
        vm(flat),
        vm(flat),
        vm(flat),
        vm(flat, f32),
        vm(flat),
        vm(ga_shape),
        vm((3,) + flat),
        vm((rows, length, LANES)),
        vm(pq_shape),
        dma((pairs, 4)),
        dma((6,)),
        dma((8,)),
    ]
    operands = (segment_ids, vg, qkv, feat, mix, grad_mixed, grad_one, stream_in, ga)
    cost = pl.CostEstimate(flops=2 * 10**10, bytes_accessed=3 * 10**7, transcendentals=2 * 10**7)
    if comm:
        tail = (9 * unit, width)
        tail_q = (3 * unit, LANES)
        stream_grad, tot, totq, vg = pl.pallas_call(
            functools.partial(backward_kernel, True, scale),
            out_shape=[
                shape(flat, f32),
                shape(tail, f32),
                shape((pairs,) + tail_q, f32),
                shape((16, width), f32),
            ],
            in_specs=[VMEM, VMEM] + [ANY] * 8,
            out_specs=[ANY] + [VMEM] * 3,
            scratch_shapes=scratch
            + [vm((3,) + s + (3 * unit, width)) for s in ((4, 4), (4, 4), (2, 4), (4,), (3,))]
            + [vm((pairs,) + s + tail_q) for s in ((4, 4), (4, 4), (2, 4), (4,), (3,))]
            + [vm((3, 16, width), f32), vm((7, 16, width), f32)]
            + [dma((3, 7)), dma((3, 7)), dma((pairs, 7)), dma((pairs, 7)), dma((6,)), dma((7,))],
            compiler_params=params(collective_id=1, has_side_effects=True),
            cost_estimate=cost,
            name="backward_scatter",
        )(*operands, pg)
        outs = pl.pallas_call(
            update_kernel,
            out_shape=[shape(flat, f32), shape((3,), f32)]
            + [shape(w.shape, f32) for _ in range(3) for w in masters],
            in_specs=[VMEM] * 3 + [ANY] + [VMEM] * 15,
            out_specs=[ANY, pl.BlockSpec(memory_space=pltpu.SMEM)] + [VMEM] * 15,
            scratch_shapes=[vm(flat, f32), dma((2, 8))],
            compiler_params=params(),
            name="update",
        )(tot, totq, vg, stream_grad, *masters, *firsts[:4], firsts[4].reshape(1, -1), *seconds[:4], seconds[4].reshape(1, -1))
        stream_grad, root_means = outs[:2]
        grads, renewed, updated = (
            [v.reshape(w.shape) for v, w in zip(outs[k : k + 5], weights)] for k in (2, 7, 12)
        )
    else:
        stream_grad, pq, vg = pl.pallas_call(
            functools.partial(backward_kernel, False, scale),
            out_shape=[shape(flat, f32), shape(pq_shape, bf16), shape((16, width), f32)],
            in_specs=[VMEM, VMEM] + [ANY] * 7,
            out_specs=[ANY, ANY, VMEM],
            scratch_shapes=scratch,
            compiler_params=params(),
            cost_estimate=cost,
            name="backward",
        )(*operands)
        pq = jnp.moveaxis(pq.reshape(pairs, SLOTS, 3 * unit, LANES), 0, 2).reshape(SLOTS, 3 * unit, width)
        pg = pg.reshape(SLOTS, 9 * unit, width)
        partial = [
            unpack_columns(pq, 3),
            unpack_columns(pg[:, :unit], 1),
            unpack_columns(pg[:, unit : 5 * unit], blocks),
            pg[:, 5 * unit :].reshape(hidden, width),
            vg[:12].reshape(-1),
        ]
        grads = [
            lax.psum_scatter(g.astype(f32), AXES, scatter_dimension=0, tiled=True) for g in partial
        ]
        totals = lax.psum(vg[12, :4], AXES)
        root_means = jnp.sqrt(totals[1:] / totals[0])
        made = [adam(*four) for four in zip(weights, grads, firsts, seconds, RATES)]
        renewed, updated = ([m[k] for m in made] for k in range(2))
    return (stream_out, dual_out, stream_grad, root_means, *grads, *renewed, *updated)


def solution(mesh):
    sizes = dict(mesh.shape)
    comm = sizes["dp"] == 4 and sizes["fsdp"] == 8
    matrix, line = P(AXES, None), P(AXES)
    five = (matrix, matrix, matrix, matrix, line)
    in_specs = (matrix,) * 3 + five * 3 + (matrix, matrix)
    out_specs = (matrix,) * 3 + (P(),) + five * 3
    return jax.shard_map(
        functools.partial(per_device, comm),
        mesh=mesh,
        in_specs=in_specs,
        out_specs=out_specs,
        check_vma=False,
    )
```

```python
import functools

import jax
import jax.numpy as jnp
from jax import lax
from jax.experimental import pallas as pl
from jax.experimental.pallas import tpu as pltpu
from jax.sharding import PartitionSpec as P

HEAD = 64
STEP = 10
NORM_EPS = 1e-05
BETA_FIRST = 0.5
BETA_SECOND = 0.5
ADAM_EPS = 1e-08
RATES = ((0.04, 0.1), (0.15, 0.1), (0.04, 0.1), (0.03, 0.1), (0.2, 0.0))

AXES = ("dp", "fsdp")
MESH = pl.DeviceIdType.MESH
bf16 = jnp.bfloat16
f32 = jnp.float32
ANY = pl.BlockSpec(memory_space=pl.ANY)
VMEM = pl.BlockSpec(memory_space=pltpu.VMEM)

SLOTS = 32
NEG = -1e30
QB = 256
LANES = 128


def nn(a, b):
    return jnp.dot(a, b, preferred_element_type=f32)


def nt(a, b):
    return lax.dot_general(a, b, (((1,), (1,)), ((), ())), preferred_element_type=f32)


def tn(a, b):
    return lax.dot_general(a, b, (((0,), (0,)), ((), ())), preferred_element_type=f32)


def merged(packed):
    return packed.reshape(-1, packed.shape[-1])


def half_rows():
    lane = lax.broadcasted_iota(jnp.int32, (1, LANES), 1)
    low = jnp.where(lane < HEAD, 1.0, 0.0)
    return low.astype(bf16), (1.0 - low).astype(bf16)


def segment_columns(seg_row):
    length = seg_row.shape[-1]
    place = lax.rem(lax.broadcasted_iota(jnp.int32, (LANES, length), 0), HEAD)
    ids = jnp.broadcast_to(seg_row, (LANES, length))
    same = (place == ids) & (place < 16)
    ones = jnp.where(same, 1.0, 0.0)
    against = jnp.where(place < 16, jnp.where(same, 0.0, NEG), jnp.where(place < 19, 1.0, 0.0))
    return jnp.transpose(ones).astype(bf16), jnp.transpose(against).astype(bf16)


def in_parts(value):
    first = value.astype(bf16).astype(f32)
    rest = value - first
    second = rest.astype(bf16).astype(f32)
    return first, second, rest - second


def part_columns(value, other):
    first, second, third = in_parts(value)
    lane = lax.rem(lax.broadcasted_iota(jnp.int32, value.shape, 1), HEAD)
    return jnp.where(
        lane == 16, first, jnp.where(lane == 17, second, jnp.where(lane == 18, third, other))
    )


class Place:
    def __init__(self):
        self.dp = lax.axis_index("dp")
        self.fs = lax.axis_index("fsdp")
        self.c = lax.rem(self.fs, 2)
        self.z = self.fs // 2
        x = lax.rem(self.dp, 2)
        y = self.dp // 2
        self.dpx = 2 * y + 1 - x
        self.dpy = 2 - 2 * y + x
        self.a = self.dpx + self.c * (self.dpy - self.dpx)
        self.b = self.dpy + self.c * (self.dpx - self.dpy)
        self.ab = 3 - self.dp
        self.zs = [lax.rem(self.z + k, 4) for k in range(4)]
        self.to_a = (self.a, self.fs)
        self.to_b = (self.b, self.fs)
        self.to_x = (self.dpx, self.fs)
        self.to_y = (self.dpy, self.fs)
        self.to_ab = (self.ab, self.fs)
        self.to_core = (self.dp, self.fs + 1 - 2 * self.c)
        self.to_z = [None] + [(self.dp, 2 * self.zs[k] + self.c) for k in range(1, 4)]

    def greet(self):
        friends = [self.to_a, self.to_b, self.to_ab, self.to_core] + self.to_z[1:]
        for friend in friends:
            pl.semaphore_signal(
                pltpu.get_barrier_semaphore(), inc=1, device_id=friend, device_id_type=MESH
            )

    def greeted(self):
        pl.semaphore_wait(pltpu.get_barrier_semaphore(), 7)


def remote(src, dst, send_sem, recv_sem, device):
    return pltpu.make_async_remote_copy(
        src_ref=src,
        dst_ref=dst,
        send_sem=send_sem,
        recv_sem=recv_sem,
        device_id=device,
        device_id_type=MESH,
    )


class Gather:
    def __init__(self, here, buf, columns, send_sem, recv_sem, straight):
        self.here, self.buf, self.columns = here, buf, columns
        self.send_sem, self.recv_sem, self.straight = send_sem, recv_sem, straight
        self.sent = []

    def slot_copy(self, number, z, device):
        slot = self.buf.at[self.here.dp, z, self.here.c, :, self.columns]
        return remote(slot, slot, self.send_sem.at[number], self.recv_sem.at[z], device)

    def line_copy(self, number, d, c, device):
        line = self.buf.at[d, :, c, :, self.columns]
        base = 4 if device is not self.here.to_core else 8
        return remote(line, line, self.send_sem.at[number], self.recv_sem.at[base + d], device)

    def send(self, d, *devices):
        for device in devices:
            number = 3 + len(self.sent)
            self.sent.append((d, device))
            self.line_copy(number, d, self.here.c, device).start()

    def arrive(self, d):
        self.line_copy(0, d, self.here.c, self.here.to_a).wait_recv()

    def step(self, number):
        me = self.here
        if number == 0:
            for k in range(1, 4):
                self.slot_copy(k - 1, me.z, me.to_z[k]).start()
        elif number == 1:
            for k in range(1, 4):
                self.slot_copy(0, me.zs[k], me.to_z[k]).wait_recv()
            if self.straight:
                self.send(me.dp, me.to_ab, me.to_a, me.to_b, me.to_core)
            else:
                self.send(me.dp, me.to_a, me.to_b, me.to_core)
        elif number == 2:
            self.arrive(me.a)
            self.send(me.a, *([me.to_core] if self.straight else [me.to_b, me.to_core]))
        elif number == 3:
            for d in (me.b, me.ab):
                self.arrive(d)
                self.send(d, me.to_core)
        else:
            for d in range(4):
                self.line_copy(0, d, 1 - me.c, me.to_core).wait_recv()

    def finish(self):
        me = self.here
        for k in range(1, 4):
            self.slot_copy(k - 1, me.z, me.to_z[k]).wait_send()
        for number, (d, device) in enumerate(self.sent):
            self.line_copy(3 + number, d, me.c, device).wait_send()


def forward_kernel(comm, scale, *refs):
    if comm:
        (x_hbm, seg, wqkv, wp, wu, wd, vec, qkv_o, mix_o, feat_o, vec_o, ga_o, gb_o, gc_o) = refs[:14]
        (x_v, now_v, next_v, mix_v, feat_v, fq, fk, ga, gb, gc) = refs[14:24]
        (loc, sa, ra, sb, rb, sc, rc) = refs[24:]
    else:
        (x_hbm, seg, ga_hbm, qkv_o, mix_o, feat_o, vec_o) = refs[:7]
        (x_v, now_v, next_v, mix_v, feat_v, fq, fk, ga) = refs[7:15]
        (loc,) = refs[15:]
    rows, length = seg.shape
    width = x_v.shape[1]
    pairs = width // LANES
    step_rows = width // SLOTS

    x_copy = pltpu.make_async_copy(x_hbm, x_v, loc.at[pairs, 0])
    count = SLOTS * 6
    if comm:
        here = Place()
        here.greet()
        own = (here.dp, here.z, here.c)
        for p in range(pairs):
            for j in range(3):
                begin = j * width + p * LANES
                ga[(p,) + own + (slice(None), slice(j * LANES, (j + 1) * LANES))] = wqkv[
                    :, begin : begin + LANES
                ].astype(bf16)
        rest = jnp.concatenate([vec[:, LANES:], jnp.zeros((1, 2 * LANES - count), f32)], axis=1)
        row = lax.broadcasted_iota(jnp.int32, (step_rows, LANES), 0)
        tile = jnp.where(row == 0, vec[:, :LANES], jnp.where(row == 1, rest, 0.0))
        ga[(0,) + own + (slice(None), slice(3 * LANES, 4 * LANES))] = tile.astype(bf16)
        gathers = [
            Gather(here, ga.at[p], slice(0, 4 * LANES if p == 0 else 3 * LANES), sa.at[p], ra.at[p], True)
            for p in range(pairs)
        ]
        every = slice(0, width)
        gathers.append(Gather(here, gb, every, sb, rb, False))
        gathers.append(Gather(here, gc, every, sc, rc, False))
        here.greeted()
        gathers[0].step(0)
        x_copy.start()
        for p in range(1, pairs):
            gathers[p].step(0)
        gb[own + (slice(0, step_rows),)] = wp[...].astype(bf16)
        for j in range(4):
            gb[own + (slice((j + 1) * step_rows, (j + 2) * step_rows),)] = wu[
                :, j * width : (j + 1) * width
            ].astype(bf16)
        gc[own] = wd[...].astype(bf16)
    else:
        x_copy.start()
        ga_copy = pltpu.make_async_copy(ga_hbm, ga, loc.at[pairs, 1])
        ga_copy.start()

    def marks_of(r):
        ones, against = segment_columns(seg[r : r + 1, :])
        fq[r] = ones
        fk[r] = against

    def transfer(*steps):
        for group, number in steps:
            gathers[group].step(number)

    if comm:
        transfer((0, 1), (4, 0), (1, 1))
        marks_of(0)
        transfer((0, 2), (0, 3), (2, 1), (5, 0))
        for r in range(1, rows):
            marks_of(r)
        transfer((0, 4))
    else:
        for r in range(rows):
            marks_of(r)
        ga_copy.wait()
    x_copy.wait()

    lane = lax.broadcasted_iota(jnp.int32, (1, LANES), 1)

    def half_of(number, upper):
        part = number % 3
        row = part // 2
        i = number // 3
        tile = ga[0, i // 8, i % 8 // 2, i % 2, :, 3 * LANES : 4 * LANES].astype(f32)
        tile = tile if upper == (part == 1) else pltpu.roll(tile, HEAD, 1)
        return tile[row : row + 1, :]

    def assemble(first, last):
        for t in range(first, last):
            line = jnp.where(lane < HEAD, half_of(2 * t, False), half_of(2 * t + 1, True))
            vec_o[t // 4 : t // 4 + 1, t % 4 * LANES : (t % 4 + 1) * LANES] = line

    assemble(4 * pairs, 6 * pairs)

    def columns_at(p):
        return pl.ds(pl.multiple_of(p * LANES, LANES), LANES)

    def project(p, part):
        lin = nn(x_v[part, :], merged(ga[p, :, :, :, :, : 3 * LANES]))
        query = (lin[:, :LANES] + vec_o[4:5, columns_at(p)]).astype(bf16).astype(f32) * scale
        next_v[0, part, :] = query.astype(bf16)
        next_v[1, part, :] = lin[:, LANES : 2 * LANES].astype(bf16)
        next_v[2, part, :] = (lin[:, 2 * LANES :] + vec_o[5:6, columns_at(p)]).astype(bf16)

    for t in range(rows * length // 512):
        project(0, slice(t * 512, (t + 1) * 512))
    if comm:
        transfer((1, 2), (1, 3))
    assemble(0, 4 * pairs)
    assemble(6 * pairs, 12 * pairs)
    vec_o[12:16, :] = jnp.zeros((4, width), f32)
    low_half, high_half = half_rows()
    half = lax.broadcasted_iota(jnp.int32, (QB, LANES), 1) < HEAD

    def attend(p, r):
        span = slice(r * length, (r + 1) * length)
        columns = columns_at(p)
        keys = now_v[1, span, :]
        values = now_v[2, span, :]
        keys_in = (keys * low_half + fk[r] * high_half, keys * high_half + fk[r] * low_half)
        one_low = jnp.broadcast_to(low_half, values.shape)
        one_high = jnp.broadcast_to(high_half, values.shape)
        values_in = (
            jnp.concatenate([values * low_half, one_low], axis=1),
            jnp.concatenate([values * high_half, one_high], axis=1),
        )

        def scores(j, h):
            part = slice(r * length + j * QB, r * length + (j + 1) * QB)
            query = now_v[0, part, :]
            marks = fq[r, j * QB : (j + 1) * QB, :]
            mine, other = (low_half, high_half) if h == 0 else (high_half, low_half)
            return nt(query * mine + marks * other, keys_in[h])

        blocks = [(j, h) for j in range(length // QB) for h in range(2)]
        following = scores(*blocks[0])
        kept = []
        for number, (j, h) in enumerate(blocks):
            current = following
            if number + 1 < len(blocks):
                following = scores(*blocks[number + 1])
            part = slice(r * length + j * QB, r * length + (j + 1) * QB)
            if r == rows - 1:
                share = rows * length // len(blocks)
                project(jnp.minimum(p + 1, pairs - 1), slice(number * share, (number + 1) * share))
            peak = jnp.max(current, axis=1, keepdims=True)
            soft = jnp.exp(current - peak).astype(bf16)
            kept.append((peak, nn(soft, values_in[h])))
            if h == 1:
                both = kept[0][1] + kept[1][1]
                total = both[:, LANES:]
                mix_v[part, columns] = (both[:, :LANES] / total).astype(bf16)
                logs = jnp.where(half, kept[0][0], kept[1][0]) + jnp.log(total)
                logs = pltpu.roll(logs, HEAD, 1)
                marks = fq[r, j * QB : (j + 1) * QB, :].astype(f32)
                feat_v[part, columns] = part_columns(-logs, marks).astype(bf16)
                kept = []

    schedule = (
        ((1, 4), (2, 2), (2, 3), (3, 1)),
        ((4, 1), (3, 2), (3, 3), (5, 1)),
        ((2, 4),),
        ((4, 2),),
        ((3, 4), (5, 2)),
        ((4, 3),),
        ((5, 3),),
        ((4, 4), (5, 4)),
    )
    def pair_out(p, which):
        columns = columns_at(p)
        found = [(now_v, qkv_o.at[p])] if which == 0 else [
            (mix_v.at[:, columns], mix_o.at[:, columns]),
            (feat_v.at[:, columns], feat_o.at[:, columns]),
        ]
        if comm and which == 1:
            found.append((ga.at[p], ga_o.at[p]))
        return [
            pltpu.make_async_copy(src, dst, loc.at[p, 3 * which + k])
            for k, (src, dst) in enumerate(found)
        ]

    def pair(p, carry):
        @pl.when(p > 0)
        def _():
            for copy in pair_out(p - 1, 0):
                copy.wait()

        now_v[...] = next_v[...]
        for copy in pair_out(p, 0):
            copy.start()
        for r in range(rows):
            attend(p, r)
            if comm:
                for number in range(pairs):
                    steps = schedule[rows * number + r]
                    pl.when(p == number)(functools.partial(transfer, *steps))
        for copy in pair_out(p, 1):
            copy.start()
        return carry

    lax.fori_loop(0, pairs, pair, 0)
    copies = pair_out(pairs - 1, 0)
    if comm:
        last = [
            pltpu.make_async_copy(src, dst, loc.at[pairs, 2 + k])
            for k, (src, dst) in enumerate(((gb, gb_o), (gc, gc_o)))
        ]
        for copy in last:
            copy.start()
        copies += last
        for group in gathers:
            group.finish()
    for p in range(pairs):
        copies += pair_out(p, 1)
    for copy in copies:
        copy.wait()


def row_mean(value):
    return jnp.mean(value, axis=-1, keepdims=True)


def column_sum(value):
    return jnp.sum(value, axis=0, keepdims=True)


def middle_kernel(
    seg, vec, x_hbm, mix_hbm, dual_hbm, cs_hbm, cd_hbm, gb_hbm, gc_hbm,
    so_o, do_o, one_o, gm_o, pg_o, vg_o,
    x_v, mix_v, dual_v, cs_v, cd_v, gb, gc, low_v, spread_v, two_v, ffn_v, hid_v, slope_v, pg_v,
    attn_v, sum_v,
    in_sem, out_sem, w_sem,
):
    rows, length = seg.shape
    tokens, width = x_v.shape
    blocks = hid_v.shape[0]
    step_rows = width // SLOTS
    tile = 512
    tiles = tokens // tile
    per_row = length // tile

    def rows_of(t, size=tile):
        return pl.ds(pl.multiple_of(t * size, size), size)

    w_copies = [
        pltpu.make_async_copy(gb_hbm, gb, w_sem.at[0]),
        pltpu.make_async_copy(gc_hbm, gc, w_sem.at[1]),
    ]
    pairs_in = ((mix_hbm, mix_v), (x_hbm, x_v), (cs_hbm, cs_v), (cd_hbm, cd_v), (dual_hbm, dual_v))

    def in_copy(k, t):
        src, dst = pairs_in[k]
        return pltpu.make_async_copy(src.at[rows_of(t)], dst.at[rows_of(t)], in_sem.at[k, t])

    w_copies[0].start()
    for k in range(5):
        in_copy(k, 0).start()
    w_copies[1].start()
    for t in range(1, tiles):
        for k in range(5):
            in_copy(k, t).start()
    pairs_out = ((cs_v, so_o), (dual_v, do_o), (dual_v, one_o), (ffn_v, gm_o))

    def out_copy(k, t):
        src, dst = pairs_out[k]
        return pltpu.make_async_copy(src.at[rows_of(t)], dst.at[rows_of(t)], out_sem.at[k, t])

    vg_o[...] = jnp.zeros_like(vg_o)
    gain_one, shift_one, gain_two, shift_two = (vec[k : k + 1, :] for k in range(4))
    bias_o, bias_d = vec[6:7, :], vec[7:8, :]
    w_copies[0].wait()
    w_copies[1].wait()
    lane = lax.broadcasted_iota(jnp.int32, (1, width), 1)

    def proj_weight():
        return merged(gb[:, :, :, 0:step_rows, :])

    def up_weight(f):
        return merged(gb[:, :, :, (f + 1) * step_rows : (f + 2) * step_rows, :])

    def down_weight(f):
        return merged(gc[f])

    def first_half(t):
        here = rows_of(t)
        attn = nn(mix_v[here, :], proj_weight()) + bias_o
        first_sum = x_v[here, :].astype(f32) + attn
        centred = first_sum - row_mean(first_sum)
        spread = lax.rsqrt(row_mean(centred * centred) + NORM_EPS)
        hat = centred * spread
        x_v[here, :] = hat.astype(bf16)
        spread_v[here, :] = jnp.broadcast_to(spread, (tile, LANES))
        first_norm = hat * gain_one + shift_one
        low_v[here, :] = first_norm.astype(bf16)
        two_v[here, :] = first_norm
        attn_v[...] = attn

    def feed(t):
        here = rows_of(t)
        first_low = low_v[here, :]
        ffn = bias_d
        upper = nn(first_low, up_weight(0))
        for f in range(blocks):
            u = upper + vec[8 + f : 9 + f, :]
            if f + 1 < blocks:
                upper = nn(first_low, up_weight(f + 1))
            square = u * u
            inner = jnp.tanh(u * (0.7978845608028654 + 0.035677408136300125 * square))
            share = 0.5 + 0.5 * inner
            hidden = u * share
            slope = share + hidden * (1.0 - share) * (
                1.5957691216057308 + 0.21406444881780073 * square
            )
            hidden = hidden.astype(bf16)
            hid_v[f, here, :] = hidden
            slope_v[f, here, :] = slope.astype(bf16)
            ffn = ffn + nn(hidden, down_weight(f))
        sum_v[...] = ffn

    def second_half(t):
        here = rows_of(t)
        attn = attn_v[...]
        ffn = sum_v[...]
        dual_v[here, :] = dual_v[here, :] + attn + ffn
        second_sum = two_v[here, :] + ffn
        centred = second_sum - row_mean(second_sum)
        spread = lax.rsqrt(row_mean(centred * centred) + NORM_EPS)
        hat = centred * spread
        second_norm = hat * gain_two + shift_two
        cot = cs_v[here, :].astype(f32)
        cs_v[here, :] = second_norm.astype(bf16)
        r = t // per_row
        ids = seg[pl.ds(r, 1), pl.ds(pl.multiple_of((t - r * per_row) * tile, tile), tile)]
        valid = jnp.where(ids != 0, 1.0, 0.0)
        valid = jnp.transpose(jnp.broadcast_to(valid, (LANES, tile)))[:, 0:1]
        counts = column_sum(valid) * width
        squares = [
            jnp.sum(column_sum(valid * (v * v)), axis=1, keepdims=True)
            for v in (second_norm, attn, ffn)
        ]
        line = jnp.where(lane == 0, counts, 0.0)
        for k in range(3):
            line = jnp.where(lane == k + 1, squares[k], line)
        vg_o[12:13, :] += line
        scaled = cot * gain_two
        grad = (scaled - row_mean(scaled) - hat * row_mean(scaled * hat)) * spread
        two_v[here, :] = grad
        vg_o[2:3, :] += column_sum(cot * hat)
        vg_o[3:4, :] += column_sum(cot)
        grad_low = (grad + cd_v[here, :].astype(f32)).astype(bf16)
        ffn_v[here, :] = grad_low
        vg_o[7:8, :] += column_sum(grad_low.astype(f32))

    def arrived(t, kinds):
        for k in kinds:
            in_copy(k, t).wait()

    def leave(t, kinds):
        for k in kinds:
            out_copy(k, t).start()

    def forward(t, carry):
        arrived(t, (0, 1, 2, 3, 4))
        first_half(t)
        feed(t)
        second_half(t)
        leave(t, (0, 1))
        return carry

    lax.fori_loop(0, tiles, forward, 0)

    pg_copies = []

    def pg_out(*where):
        copy = pltpu.make_async_copy(pg_v.at[where], pg_o.at[where], w_sem.at[len(pg_copies) + 2])
        copy.start()
        pg_copies.append(copy)

    every = slice(None)
    def back_hidden(f, carry):
        total = jnp.zeros((1, width), f32)
        for t in range(tokens // 512):
            here = slice(t * 512, (t + 1) * 512)
            grad = nt(ffn_v[here, :], down_weight(f))
            grad_up = (slope_v[f, here, :].astype(f32) * grad).astype(bf16)
            slope_v[f, here, :] = grad_up
            total = total + column_sum(grad_up.astype(f32))
        vg_o[pl.ds(8 + f, 1), :] = total
        return carry

    lax.fori_loop(0, blocks, back_hidden, 0)

    def weight_grads(f, carry):
        down = tn(hid_v[f], ffn_v[...])
        pg_v[f, :, :, 5 * step_rows :, :] = down.astype(bf16).reshape(4, 2, 4 * step_rows, width)
        up = tn(low_v[...], slope_v[f])
        rows_f = pl.ds(pl.multiple_of((f + 1) * step_rows, step_rows), step_rows)
        pg_v[:, :, :, rows_f, :] = up.astype(bf16).reshape(4, 4, 2, step_rows, width)
        return carry

    lax.fori_loop(0, blocks, weight_grads, 0)
    pg_out(every, every, every, slice(step_rows, 9 * step_rows))

    def grad_of_first(t):
        here = rows_of(t)
        grad = two_v[here, :]
        for f in range(blocks):
            grad = grad + nt(slope_v[f, here, :], up_weight(f))
        sum_v[...] = grad

    def back_first(t):
        here = rows_of(t)
        grad = sum_v[...]
        hat = x_v[here, :].astype(f32)
        scaled = grad * gain_one
        spread = spread_v[here, 0:1]
        grad_one = (scaled - row_mean(scaled) - hat * row_mean(scaled * hat)) * spread
        dual_v[here, :] = grad_one
        grad_low = (grad_one + cd_v[here, :].astype(f32)).astype(bf16)
        low_v[here, :] = grad_low
        ffn_v[here, :] = nt(grad_low, proj_weight()).astype(bf16)
        vg_o[0:1, :] += column_sum(grad * hat)
        vg_o[1:2, :] += column_sum(grad)
        vg_o[6:7, :] += column_sum(grad_low.astype(f32))

    for t in range(tiles):
        out_copy(1, t).wait()

    def backward(t, carry):
        grad_of_first(t)
        back_first(t)
        leave(t, (2, 3))
        return carry

    lax.fori_loop(0, tiles, backward, 0)
    proj = tn(mix_v[...], low_v[...])
    pg_v[:, :, :, 0:step_rows, :] = proj.astype(bf16).reshape(4, 4, 2, step_rows, width)
    pg_out(every, every, every, slice(0, step_rows))
    for t in range(tiles):
        for k in (0, 2, 3):
            out_copy(k, t).wait()
    for copy in pg_copies:
        copy.wait()


class Scatter:
    def __init__(self, here, send, mine, bufs, send_sem, recv_sem, straight):
        self.here, self.source, self.mine = here, send, mine
        self.from_core, self.from_b, self.from_a, self.from_z = bufs
        self.send_sem, self.recv_sem, self.straight = send_sem, recv_sem, straight
        self.last = 2 if straight else 3

    def copies(self, phase):
        me, mine = self.here, self.mine
        if phase == 0:
            base, found = 0, [(self.source, self.from_core, me.to_core)]
        elif phase == self.last:
            base = 4
            found = [
                (mine.at[me.dp, me.zs[k]], self.from_z.at[k - 1], me.to_z[k]) for k in range(1, 4)
            ]
        elif self.straight:
            base = 1
            found = [
                (mine.at[me.ab], self.from_a, me.to_ab),
                (mine.at[me.a], self.from_b.at[0], me.to_a),
                (mine.at[me.b], self.from_b.at[1], me.to_b),
            ]
        elif phase == 1:
            base = 1
            found = [
                (mine.at[me.b], self.from_b.at[0], me.to_b),
                (mine.at[me.ab], self.from_b.at[1], me.to_b),
            ]
        else:
            base, found = 3, [(mine.at[me.a], self.from_a, me.to_a)]
        return [
            remote(src, dst, self.send_sem.at[base + k], self.recv_sem.at[base + k], device)
            for k, (src, dst, device) in enumerate(found)
        ]

    def start(self, phase):
        for copy in self.copies(phase):
            copy.start()

    def add(self, phase):
        me, mine = self.here, self.mine
        for copy in self.copies(phase):
            copy.wait_recv()

        def into(where, *parts):
            if len(parts) == 1:
                mine[where] = mine[where] + parts[0]
            else:
                total = mine[where].astype(f32)
                for part in parts:
                    total = total + part.astype(f32)
                mine[where] = total.astype(bf16)

        for z in range(4):
            if phase == 0:
                for d in range(4):
                    into((d, z), self.from_core[d, z])
            elif self.straight:
                into((me.dp, z), self.from_a[z], self.from_b[0, z], self.from_b[1, z])
            elif phase == 1:
                into((me.dp, z), self.from_b[0, z])
                into((me.a, z), self.from_b[1, z])
            else:
                into((me.dp, z), self.from_a[z])

    def result(self):
        for copy in self.copies(self.last):
            copy.wait_recv()
        total = self.mine[self.here.dp, self.here.z].astype(f32)
        for k in range(3):
            total = total + self.from_z[k].astype(f32)
        return total

    def finish(self):
        for phase in range(self.last + 1):
            for copy in self.copies(phase):
                copy.wait_send()


class Total:
    def __init__(self, here, own, bufs, send_sem, recv_sem):
        self.here, self.own, self.bufs = here, own, bufs
        self.send_sem, self.recv_sem = send_sem, recv_sem

    def copies(self, phase):
        me, bufs = self.here, self.bufs
        if phase == 0:
            found = [(self.own, bufs.at[0], 0, me.to_core)]
        else:
            slot = 1 + me.dp if phase == 1 else 5 + me.z
            devices = [me.to_a, me.to_b, me.to_ab] if phase == 1 else me.to_z[1:]
            found = [(bufs.at[slot], bufs.at[slot], slot, device) for device in devices]
        return [
            remote(src, dst, self.send_sem.at[3 * phase + k], self.recv_sem.at[slot], device)
            for k, (src, dst, slot, device) in enumerate(found)
        ]

    def start(self, phase):
        for copy in self.copies(phase):
            copy.start()

    def arrive(self, *slots):
        for slot in slots:
            ref = self.bufs.at[slot]
            remote(ref, ref, self.send_sem.at[0], self.recv_sem.at[slot], self.here.to_core).wait_recv()

    def add(self, phase):
        me, bufs = self.here, self.bufs
        if phase == 0:
            self.arrive(0)
            bufs[1 + me.dp] = self.own[...] + bufs[0]
        else:
            self.arrive(1 + me.a, 1 + me.b, 1 + me.ab)
            bufs[5 + me.z] = bufs[1] + bufs[2] + bufs[3] + bufs[4]

    def result(self):
        self.arrive(*[5 + self.here.zs[k] for k in range(1, 4)])
        bufs = self.bufs
        return bufs[5] + bufs[6] + bufs[7] + bufs[8]

    def finish(self):
        for phase in range(3):
            for copy in self.copies(phase):
                copy.wait_send()


def backward_kernel(comm, scale, *refs):
    (seg, vg, qkv_hbm, feat_hbm, mix_hbm, gm_hbm, one_hbm, x_hbm, ga_hbm) = refs[:9]
    if comm:
        (pg_hbm, sg_o, tot_o, totq_o, vg_o) = refs[9:14]
        refs = refs[14:]
    else:
        (sg_o, pq_o, vg_o) = refs[9:12]
        refs = refs[12:]
    (qkv_v, feat_v, mix_v, gm_v, one_v, x_v, ga, gq_v, fk, pq_v, in_sem, w_sem, out_sem) = refs[:13]
    rows, length = seg.shape
    tokens, width = x_v.shape
    pairs = width // LANES
    step_rows = width // SLOTS

    def pair_copies(p):
        columns = pl.ds(pl.multiple_of(p * LANES, LANES), LANES)
        found = [(qkv_hbm.at[p], qkv_v.at[p])]
        found += [
            (src.at[:, columns], dst.at[:, columns])
            for src, dst in ((gm_hbm, gm_v), (mix_hbm, mix_v), (feat_hbm, feat_v))
        ]
        return [
            pltpu.make_async_copy(src, dst, in_sem.at[p, k]) for k, (src, dst) in enumerate(found)
        ]

    late = [
        pltpu.make_async_copy(src, dst, w_sem.at[k])
        for k, (src, dst) in enumerate(((x_hbm, x_v), (ga_hbm, ga), (one_hbm, one_v)))
    ]
    if comm:
        (mine, fc, fb, fa, fz, mine_q, qc, qb, qa, qz, vp, vb, s1, r1, s2, r2, s3, r3) = refs[13:]
        here = Place()
        here.greet()
        weights = [
            Scatter(
                here,
                pg_hbm.at[:, :, 1 - here.c, pl.ds(g * 3 * step_rows, 3 * step_rows)],
                mine.at[g],
                (fc.at[g], fb.at[g], fa.at[g], fz.at[g]),
                s1.at[g],
                r1.at[g],
                False,
            )
            for g in range(3)
        ]
        columns_of = [
            Scatter(
                here,
                pq_v.at[p, :, :, 1 - here.c],
                mine_q.at[p],
                (qc.at[p], qb.at[p], qa.at[p], qz.at[p]),
                s2.at[p],
                r2.at[p],
                True,
            )
            for p in range(pairs)
        ]
        sums = Total(here, vp, vb, s3, r3)
        vp[...] = vg[...]
        mine_copies = [
            pltpu.make_async_copy(
                pg_hbm.at[:, :, here.c, pl.ds(g * 3 * step_rows, 3 * step_rows)], mine.at[g], w_sem.at[3 + g]
            )
            for g in range(3)
        ]
    if not comm:
        vg_o[...] = vg[...]
    vector = vp if comm else vg_o
    for copy in pair_copies(0):
        copy.start()
    if comm:
        for copy in mine_copies:
            copy.start()
    for p in range(1, pairs):
        for copy in pair_copies(p):
            copy.start()
    for copy in late:
        copy.start()
    for r in range(rows):
        fk[r] = segment_columns(seg[r : r + 1, :])[1]
    if comm:
        here.greeted()
        for group in weights:
            group.start(0)
    low_half, high_half = half_rows()

    def transfer(number):
        if number == 0:
            for copy in mine_copies:
                copy.wait()
        for group, steps in list(zip(weights, ((0, 2, 3), (1, 3, 4), (3, 5, 6)))) + [
            (columns_of[p], (rows * p + rows, rows * p + rows + 1)) for p in range(pairs)
        ]:
            for phase in range(group.last):
                if number == steps[phase]:
                    group.add(phase)
                    group.start(phase + 1)
        for p in range(pairs):
            if number == rows * (p + 1) - 1:
                columns_of[p].start(0)
                mine_q[p] = pq_v[p, :, :, here.c]
        if number == rows * pairs - 1:
            sums.start(0)

    def attend(i, carry):
        p = i // rows
        r = lax.rem(i, rows)
        span = pl.ds(pl.multiple_of(r * length, length), length)
        columns = pl.ds(pl.multiple_of(p * LANES, LANES), LANES)

        @pl.when(r == 0)
        def _():
            for copy in pair_copies(p):
                copy.wait()

        queries = qkv_v[p, 0, span, :]
        keys = qkv_v[p, 1, span, :]
        values = qkv_v[p, 2, span, :]
        grads = gm_v[span, columns]
        marks = feat_v[span, columns]
        product = grads.astype(f32) * mix_v[span, columns].astype(f32)
        is_low = lax.broadcasted_iota(jnp.int32, product.shape, 1) < HEAD
        for_low = jnp.sum(jnp.where(is_low, product, 0.0), axis=1, keepdims=True)
        for_high = jnp.sum(jnp.where(is_low, 0.0, product), axis=1, keepdims=True)
        deltas = part_columns(-jnp.where(is_low, for_high, for_low), 0.0).astype(bf16)
        place = lax.rem(lax.broadcasted_iota(jnp.int32, (1, LANES), 1), HEAD)
        ones = jnp.where((place >= 16) & (place < 19), 1.0, 0.0).astype(bf16)
        queries_t = jnp.transpose(queries)
        grads_t = jnp.transpose(grads)
        key_parts, value_parts = [], []
        query_grads = [None] * (length // QB)
        for h in range(2):
            mine_h, other_h = (low_half, high_half) if h == 0 else (high_half, low_half)
            half = slice(h * HEAD, (h + 1) * HEAD)
            key_own = keys * mine_h
            key_in = key_own + fk[r] * other_h
            value_in = values * mine_h + ones * other_h
            key_sum = value_sum = None
            for j in range(length // QB):
                part = slice(j * QB, (j + 1) * QB)
                soft = jnp.exp(nt(queries[part] * mine_h + marks[part] * other_h, key_in))
                wide = nt(grads[part] * mine_h + deltas[part] * other_h, value_in)
                back = (soft * wide).astype(bf16)
                soft = soft.astype(bf16)
                moved = nn(back, key_own)
                query_grads[j] = moved if h == 0 else query_grads[j] + moved
                value_part = nn(grads_t[half, part], soft)
                key_part = nn(queries_t[half, part], back)
                value_sum = value_part if j == 0 else value_sum + value_part
                key_sum = key_part if j == 0 else key_sum + key_part
            key_parts.append(key_sum)
            value_parts.append(value_sum)
        for j in range(length // QB):
            part = pl.ds(pl.multiple_of(r * length + j * QB, QB), QB)
            gq_v[0, part, columns] = (query_grads[j] * scale).astype(bf16)
        gq_v[1, span, columns] = jnp.transpose(jnp.concatenate(key_parts, axis=0)).astype(bf16)
        gq_v[2, span, columns] = jnp.transpose(jnp.concatenate(value_parts, axis=0)).astype(bf16)

        @pl.when(r == rows - 1)
        def _():
            @pl.when(p == 0)
            def _():
                late[0].wait()

            stacked = jnp.concatenate([gq_v[j, :, columns] for j in range(3)], axis=1)
            for k, j in ((4, 0), (5, 2)):
                part = stacked[:, j * LANES : (j + 1) * LANES].astype(f32)
                vector[k : k + 1, columns] = column_sum(part)
            grad = tn(x_v[...], stacked).astype(bf16).reshape(4, 4, 2, step_rows, 3 * LANES)
            for j in range(3):
                pq_v[p, :, :, :, j * step_rows : (j + 1) * step_rows, :] = grad[
                    ..., j * LANES : (j + 1) * LANES
                ]

        if comm:
            for number in range(rows * pairs):
                pl.when(i == number)(functools.partial(transfer, number))
        return carry

    lax.fori_loop(0, rows * pairs, attend, 0)
    late[1].wait()
    late[2].wait()

    if not comm:
        pq_copy = pltpu.make_async_copy(pq_v, pq_o, out_sem.at[4])
        pq_copy.start()

    def out_copy(t):
        span = pl.ds(pl.multiple_of(t * 512, 512), 512)
        return pltpu.make_async_copy(one_v.at[span, :], sg_o.at[span, :], out_sem.at[t])

    def stream(t):
        span = pl.ds(t * 512, 512)
        total = one_v[span, :]
        for j in range(3):
            total = total + nt(
                gq_v[j, span, :],
                jnp.concatenate(
                    [merged(ga[p, :, :, :, :, j * LANES : (j + 1) * LANES]) for p in range(pairs)],
                    axis=1,
                ),
            )
        one_v[span, :] = total
        out_copy(t).start()

    for t in range(tokens // 512):
        stream(t)
        if comm:
            transfer(rows * pairs + t)
            if t < 2:
                sums.add(t)
                sums.start(t + 1)
    if comm:
        for g in range(3):
            tot_o[g * 3 * step_rows : (g + 1) * 3 * step_rows, :] = weights[g].result()
        for p in range(pairs):
            totq_o[p] = columns_of[p].result()
        vg_o[...] = sums.result()
        for group in columns_of + weights + [sums]:
            group.finish()
    else:
        pq_copy.wait()
    for t in range(tokens // 512):
        out_copy(t).wait()


def adam(weight, gradient, first_old, second, rates):
    step_rate, decay_rate = rates
    first_new = BETA_FIRST * first_old + (1.0 - BETA_FIRST) * gradient
    second_new = BETA_SECOND * second + (1.0 - BETA_SECOND) * gradient * gradient
    first_hat = first_new / (1.0 - BETA_FIRST**STEP)
    second_hat = second_new / (1.0 - BETA_SECOND**STEP)
    updated = weight - step_rate * (
        first_hat / (jnp.sqrt(second_hat) + ADAM_EPS) + decay_rate * weight
    )
    return second_new, updated


def update_kernel(tot, totq, vg, sg_hbm, *refs):
    weights, firsts, seconds = refs[0:5], refs[5:10], refs[10:15]
    sg_o, root, grads, renewed, updated = refs[15], refs[16], refs[17:22], refs[22:27], refs[27:32]
    sg_v, sem = refs[32:]
    size = sg_hbm.shape[0] // 8
    copies = []
    for t in range(8):
        span = pl.ds(t * size, size)
        copies.append(pltpu.make_async_copy(sg_hbm.at[span], sg_v.at[span], sem.at[0, t]))
        copies.append(pltpu.make_async_copy(sg_v.at[span], sg_o.at[span], sem.at[1, t]))
    for copy in copies[0::2]:
        copy.start()
    width = tot.shape[1]
    step_rows = width // SLOTS
    pairs = width // LANES

    def apply(k, columns, gradient):
        where = (slice(None), columns)
        grads[k][where] = gradient
        renewed[k][where], updated[k][where] = adam(
            weights[k][where], gradient, firsts[k][where], seconds[k][where], RATES[k]
        )

    for j in range(3):
        for p in range(pairs):
            begin = j * width + p * LANES
            apply(0, slice(begin, begin + LANES), totq[p, j * step_rows : (j + 1) * step_rows, :])
    apply(1, slice(None), tot[0:step_rows, :])
    for j in range(4):
        apply(2, slice(j * width, (j + 1) * width), tot[(j + 1) * step_rows : (j + 2) * step_rows, :])
    apply(3, slice(None), tot[5 * step_rows :, :])
    for t in range(8):
        copies[2 * t].wait()
        copies[2 * t + 1].start()
    count = weights[4].shape[1]
    begin = (lax.axis_index("dp") * 8 + lax.axis_index("fsdp")) * count
    top = begin // width
    shift = begin - top * width
    row = lax.broadcasted_iota(jnp.int32, vg.shape, 0)
    lane = lax.broadcasted_iota(jnp.int32, vg.shape, 1)
    kept = ((row == top) & (lane >= shift)) | ((row == top + 1) & (lane < shift))
    line = column_sum(jnp.where(kept, vg[...], 0.0))
    line = pltpu.roll(jnp.broadcast_to(line, (8, width)), lax.rem(width - shift, width), 1)
    apply(4, slice(None), line[0:1, :count])
    sums = vg[12:13, 0:LANES]
    means = jnp.sqrt(sums / sums[:, 0:1])
    lane = lax.broadcasted_iota(jnp.int32, means.shape, 1)
    for k in range(3):
        root[k] = jnp.sum(jnp.where(lane == k + 1, means, 0.0))
    for copy in copies[1::2]:
        copy.wait()


def params(**more):
    return pltpu.CompilerParams(vmem_limit_bytes=62 * 2**20, **more)


def shape(dims, kind):
    return jax.ShapeDtypeStruct(dims, kind)


def pack_columns(full, blocks):
    width = full.shape[0]
    parts = full.reshape(SLOTS, width // SLOTS, blocks, width)
    return jnp.swapaxes(parts, 1, 2).reshape(SLOTS, -1, width)


def unpack_columns(packed, blocks):
    width = packed.shape[-1]
    parts = packed.reshape(SLOTS, blocks, width // SLOTS, width)
    return jnp.swapaxes(parts, 1, 2).reshape(width, blocks * width)


def per_device(comm, *args):
    (stream_in, dual_in, segment_ids) = args[:3]
    weights, firsts, seconds = args[3:8], args[8:13], args[13:18]
    cot_stream, cot_dual = args[18:]
    tokens, width = stream_in.shape
    rows, length = segment_ids.shape
    pairs = width // LANES
    hidden = weights[2].shape[1]
    blocks = hidden // width
    unit = width // SLOTS
    scale = HEAD**-0.5
    slots = (4, 4, 2)
    dma = pltpu.SemaphoreType.DMA
    sem_gather = [dma((10,)), dma((12,))]
    ga_shape = (pairs,) + slots + (unit, 4 * LANES)
    gb_shape, gc_shape = (slots + (n, width) for n in (5 * unit, 4 * unit))

    def vm(dims, kind=bf16):
        return pltpu.VMEM(dims, kind)

    flat = (tokens, width)
    common_out = [
        shape((pairs, 3, tokens, LANES), bf16),
        shape(flat, bf16),
        shape(flat, bf16),
        shape((16, width), f32),
    ]
    common_scratch = [
        vm(flat),
        vm((3, tokens, LANES)),
        vm((3, tokens, LANES)),
        vm(flat),
        vm(flat),
        vm((rows, length, LANES)),
        vm((rows, length, LANES)),
        vm(ga_shape),
    ]
    cost = pl.CostEstimate(flops=8 * 10**9, bytes_accessed=2 * 10**7, transcendentals=2 * 10**7)
    if comm:
        masters = [w if w.ndim == 2 else w.reshape(1, -1) for w in weights]
        qkv, mix, feat, vec, ga, gb, gc = pl.pallas_call(
            functools.partial(forward_kernel, True, scale),
            out_shape=common_out + [shape(s, bf16) for s in (ga_shape, gb_shape, gc_shape)],
            in_specs=[ANY] + [VMEM] * 6,
            out_specs=[ANY] * 3 + [VMEM] + [ANY] * 3,
            scratch_shapes=common_scratch
            + [vm(gb_shape), vm(gc_shape), dma((pairs + 1, 6))]
            + [dma((pairs, 10)), dma((pairs, 12))]
            + sem_gather * 2,
            compiler_params=params(collective_id=0, has_side_effects=True),
            cost_estimate=cost,
            name="gather_forward",
        )(stream_in, segment_ids, *masters)
    else:
        full = [lax.all_gather(w.astype(bf16), AXES, axis=0, tiled=True) for w in weights]
        packed = pack_columns(full[0], 3).reshape(SLOTS, 3, unit, pairs, LANES)
        packed = packed.transpose(3, 0, 2, 1, 4).reshape(pairs, SLOTS, unit, 3 * LANES)
        vec_pad = jnp.pad(full[4].reshape(SLOTS, -1), ((0, 0), (0, HEAD))).reshape(SLOTS, 2, LANES)
        vec_pad = jnp.pad(vec_pad[None], ((0, pairs - 1), (0, 0), (0, unit - 2), (0, 0)))
        ga = jnp.concatenate([packed, vec_pad], axis=3).reshape(ga_shape)
        gb = jnp.concatenate(
            [pack_columns(full[1], 1), pack_columns(full[2], blocks)], axis=1
        ).reshape(gb_shape)
        gc = full[3].reshape(gc_shape)
        qkv, mix, feat, vec = pl.pallas_call(
            functools.partial(forward_kernel, False, scale),
            out_shape=common_out,
            in_specs=[ANY, VMEM, ANY],
            out_specs=[ANY] * 3 + [VMEM],
            scratch_shapes=common_scratch + [dma((pairs + 1, 6))],
            compiler_params=params(),
            cost_estimate=cost,
            name="forward",
        )(stream_in, segment_ids, ga)

    pg_shape = slots + (9 * unit, width)
    tiles = tokens // 512
    stream_out, dual_out, grad_one, grad_mixed, pg, vg = pl.pallas_call(
        middle_kernel,
        out_shape=[
            shape(flat, bf16),
            shape(flat, f32),
            shape(flat, f32),
            shape(flat, bf16),
            shape(pg_shape, bf16),
            shape((16, width), f32),
        ],
        in_specs=[VMEM, VMEM] + [ANY] * 7,
        out_specs=[ANY] * 5 + [VMEM],
        scratch_shapes=[
            vm(flat),
            vm(flat),
            vm(flat, f32),
            vm(flat),
            vm(flat),
            vm(gb_shape),
            vm(gc_shape),
            vm(flat),
            vm((tokens, LANES), f32),
            vm(flat, f32),
            vm(flat),
            vm((blocks, tokens, width)),
            vm((blocks, tokens, width)),
            vm(pg_shape),
            vm((512, width), f32),
            vm((512, width), f32),
            dma((5, tiles)),
            dma((4, tiles)),
            dma((12,)),
        ],
        compiler_params=params(),
        cost_estimate=pl.CostEstimate(
            flops=3 * 10**10, bytes_accessed=4 * 10**7, transcendentals=4 * 10**6
        ),
        name="feed_forward",
    )(segment_ids, vec, stream_in, mix, dual_in, cot_stream, cot_dual, gb, gc)

    pq_shape = (pairs,) + slots + (3 * unit, LANES)
    scratch = [
        vm((pairs, 3, tokens, LANES)),
        vm(flat),
        vm(flat),
        vm(flat),
        vm(flat, f32),
        vm(flat),
        vm(ga_shape),
        vm((3,) + flat),
        vm((rows, length, LANES)),
        vm(pq_shape),
        dma((pairs, 4)),
        dma((6,)),
        dma((8,)),
    ]
    operands = (segment_ids, vg, qkv, feat, mix, grad_mixed, grad_one, stream_in, ga)
    cost = pl.CostEstimate(flops=2 * 10**10, bytes_accessed=3 * 10**7, transcendentals=2 * 10**7)
    if comm:
        tail = (9 * unit, width)
        tail_q = (3 * unit, LANES)
        stream_grad, tot, totq, vg = pl.pallas_call(
            functools.partial(backward_kernel, True, scale),
            out_shape=[
                shape(flat, f32),
                shape(tail, f32),
                shape((pairs,) + tail_q, f32),
                shape((16, width), f32),
            ],
            in_specs=[VMEM, VMEM] + [ANY] * 8,
            out_specs=[ANY] + [VMEM] * 3,
            scratch_shapes=scratch
            + [vm((3,) + s + (3 * unit, width)) for s in ((4, 4), (4, 4), (2, 4), (4,), (3,))]
            + [vm((pairs,) + s + tail_q) for s in ((4, 4), (4, 4), (2, 4), (4,), (3,))]
            + [vm((16, width), f32), vm((9, 16, width), f32)]
            + [dma((3, 7)), dma((3, 7)), dma((pairs, 7)), dma((pairs, 7)), dma((9,)), dma((9,))],
            compiler_params=params(collective_id=1, has_side_effects=True),
            cost_estimate=cost,
            name="backward_scatter",
        )(*operands, pg)
        outs = pl.pallas_call(
            update_kernel,
            out_shape=[shape(flat, f32), shape((3,), f32)]
            + [shape(w.shape, f32) for _ in range(3) for w in masters],
            in_specs=[VMEM] * 3 + [ANY] + [VMEM] * 15,
            out_specs=[ANY, pl.BlockSpec(memory_space=pltpu.SMEM)] + [VMEM] * 15,
            scratch_shapes=[vm(flat, f32), dma((2, 8))],
            compiler_params=params(),
            name="update",
        )(tot, totq, vg, stream_grad, *masters, *firsts[:4], firsts[4].reshape(1, -1), *seconds[:4], seconds[4].reshape(1, -1))
        stream_grad, root_means = outs[:2]
        grads, renewed, updated = (
            [v.reshape(w.shape) for v, w in zip(outs[k : k + 5], weights)] for k in (2, 7, 12)
        )
    else:
        stream_grad, pq, vg = pl.pallas_call(
            functools.partial(backward_kernel, False, scale),
            out_shape=[shape(flat, f32), shape(pq_shape, bf16), shape((16, width), f32)],
            in_specs=[VMEM, VMEM] + [ANY] * 7,
            out_specs=[ANY, ANY, VMEM],
            scratch_shapes=scratch,
            compiler_params=params(),
            cost_estimate=cost,
            name="backward",
        )(*operands)
        pq = jnp.moveaxis(pq.reshape(pairs, SLOTS, 3 * unit, LANES), 0, 2).reshape(SLOTS, 3 * unit, width)
        pg = pg.reshape(SLOTS, 9 * unit, width)
        partial = [
            unpack_columns(pq, 3),
            unpack_columns(pg[:, :unit], 1),
            unpack_columns(pg[:, unit : 5 * unit], blocks),
            pg[:, 5 * unit :].reshape(hidden, width),
            vg[:12].reshape(-1),
        ]
        grads = [
            lax.psum_scatter(g.astype(f32), AXES, scatter_dimension=0, tiled=True) for g in partial
        ]
        totals = lax.psum(vg[12, :4], AXES)
        root_means = jnp.sqrt(totals[1:] / totals[0])
        made = [adam(*four) for four in zip(weights, grads, firsts, seconds, RATES)]
        renewed, updated = ([m[k] for m in made] for k in range(2))
    return (stream_out, dual_out, stream_grad, root_means, *grads, *renewed, *updated)


def solution(mesh):
    sizes = dict(mesh.shape)
    comm = sizes["dp"] == 4 and sizes["fsdp"] == 8
    matrix, line = P(AXES, None), P(AXES)
    five = (matrix, matrix, matrix, matrix, line)
    in_specs = (matrix,) * 3 + five * 3 + (matrix, matrix)
    out_specs = (matrix,) * 3 + (P(),) + five * 3
    return jax.shard_map(
        functools.partial(per_device, comm),
        mesh=mesh,
        in_specs=in_specs,
        out_specs=out_specs,
        check_vma=False,
    )
```

```python
import functools

import jax
import jax.numpy as jnp
from jax import lax
from jax.experimental import pallas as pl
from jax.experimental.pallas import tpu as pltpu
from jax.sharding import PartitionSpec as P

HEAD = 64
STEP = 10
NORM_EPS = 1e-05
BETA_FIRST = 0.5
BETA_SECOND = 0.5
ADAM_EPS = 1e-08
RATES = ((0.04, 0.1), (0.15, 0.1), (0.04, 0.1), (0.03, 0.1), (0.2, 0.0))

AXES = ("dp", "fsdp")
MESH = pl.DeviceIdType.MESH
bf16 = jnp.bfloat16
f32 = jnp.float32
ANY = pl.BlockSpec(memory_space=pl.ANY)
VMEM = pl.BlockSpec(memory_space=pltpu.VMEM)

SLOTS = 32
NEG = -1e30
QB = 256
LANES = 128


def nn(a, b):
    return jnp.dot(a, b, preferred_element_type=f32)


def nt(a, b):
    return lax.dot_general(a, b, (((1,), (1,)), ((), ())), preferred_element_type=f32)


def tn(a, b):
    return lax.dot_general(a, b, (((0,), (0,)), ((), ())), preferred_element_type=f32)


def merged(packed):
    return packed.reshape(-1, packed.shape[-1])


def half_rows():
    lane = lax.broadcasted_iota(jnp.int32, (1, LANES), 1)
    low = jnp.where(lane < HEAD, 1.0, 0.0)
    return low.astype(bf16), (1.0 - low).astype(bf16)


def segment_columns(seg_row):
    length = seg_row.shape[-1]
    place = lax.rem(lax.broadcasted_iota(jnp.int32, (LANES, length), 0), HEAD)
    ids = jnp.broadcast_to(seg_row, (LANES, length))
    same = (place == ids) & (place < 16)
    ones = jnp.where(same, 1.0, 0.0)
    against = jnp.where(place < 16, jnp.where(same, 0.0, NEG), jnp.where(place < 19, 1.0, 0.0))
    return jnp.transpose(ones).astype(bf16), jnp.transpose(against).astype(bf16)


def in_parts(value):
    first = value.astype(bf16).astype(f32)
    rest = value - first
    second = rest.astype(bf16).astype(f32)
    return first, second, rest - second


def part_columns(value, other):
    first, second, third = in_parts(value)
    lane = lax.rem(lax.broadcasted_iota(jnp.int32, value.shape, 1), HEAD)
    return jnp.where(
        lane == 16, first, jnp.where(lane == 17, second, jnp.where(lane == 18, third, other))
    )


class Place:
    def __init__(self):
        self.dp = lax.axis_index("dp")
        self.fs = lax.axis_index("fsdp")
        self.c = lax.rem(self.fs, 2)
        self.z = self.fs // 2
        x = lax.rem(self.dp, 2)
        y = self.dp // 2
        self.dpx = 2 * y + 1 - x
        self.dpy = 2 - 2 * y + x
        self.a = self.dpx + self.c * (self.dpy - self.dpx)
        self.b = self.dpy + self.c * (self.dpx - self.dpy)
        self.ab = 3 - self.dp
        self.zs = [lax.rem(self.z + k, 4) for k in range(4)]
        self.to_a = (self.a, self.fs)
        self.to_b = (self.b, self.fs)
        self.to_x = (self.dpx, self.fs)
        self.to_y = (self.dpy, self.fs)
        self.to_ab = (self.ab, self.fs)
        self.to_core = (self.dp, self.fs + 1 - 2 * self.c)
        self.to_z = [None] + [(self.dp, 2 * self.zs[k] + self.c) for k in range(1, 4)]

    def greet(self):
        friends = [self.to_a, self.to_b, self.to_ab, self.to_core] + self.to_z[1:]
        for friend in friends:
            pl.semaphore_signal(
                pltpu.get_barrier_semaphore(), inc=1, device_id=friend, device_id_type=MESH
            )

    def greeted(self):
        pl.semaphore_wait(pltpu.get_barrier_semaphore(), 7)


def remote(src, dst, send_sem, recv_sem, device):
    return pltpu.make_async_remote_copy(
        src_ref=src,
        dst_ref=dst,
        send_sem=send_sem,
        recv_sem=recv_sem,
        device_id=device,
        device_id_type=MESH,
    )


class Gather:
    def __init__(self, here, buf, columns, send_sem, recv_sem, straight):
        self.here, self.buf, self.columns = here, buf, columns
        self.send_sem, self.recv_sem, self.straight = send_sem, recv_sem, straight
        self.sent = []

    def slot_copy(self, number, z, device):
        slot = self.buf.at[self.here.dp, z, self.here.c, :, self.columns]
        return remote(slot, slot, self.send_sem.at[number], self.recv_sem.at[z], device)

    def line_copy(self, number, d, c, device):
        line = self.buf.at[d, :, c, :, self.columns]
        base = 4 if device is not self.here.to_core else 8
        return remote(line, line, self.send_sem.at[number], self.recv_sem.at[base + d], device)

    def send(self, d, *devices):
        for device in devices:
            number = 3 + len(self.sent)
            self.sent.append((d, device))
            self.line_copy(number, d, self.here.c, device).start()

    def arrive(self, d):
        self.line_copy(0, d, self.here.c, self.here.to_a).wait_recv()

    def step(self, number):
        me = self.here
        if number == 0:
            for k in range(1, 4):
                self.slot_copy(k - 1, me.z, me.to_z[k]).start()
        elif number == 1:
            for k in range(1, 4):
                self.slot_copy(0, me.zs[k], me.to_z[k]).wait_recv()
            if self.straight:
                self.send(me.dp, me.to_ab, me.to_a, me.to_b, me.to_core)
            else:
                self.send(me.dp, me.to_a, me.to_b, me.to_core)
        elif number == 2:
            self.arrive(me.a)
            self.send(me.a, *([me.to_core] if self.straight else [me.to_b, me.to_core]))
        elif number == 3:
            for d in (me.b, me.ab):
                self.arrive(d)
                self.send(d, me.to_core)
        else:
            for d in range(4):
                self.line_copy(0, d, 1 - me.c, me.to_core).wait_recv()

    def finish(self):
        me = self.here
        for k in range(1, 4):
            self.slot_copy(k - 1, me.z, me.to_z[k]).wait_send()
        for number, (d, device) in enumerate(self.sent):
            self.line_copy(3 + number, d, me.c, device).wait_send()


def forward_kernel(comm, scale, *refs):
    if comm:
        (x_hbm, seg, wqkv, wp, wu, wd, vec, qkv_o, mix_o, feat_o, vec_o, ga_o, gb_o, gc_o) = refs[:14]
        (x_v, now_v, next_v, mix_v, feat_v, fq, fk, ga, gb, gc) = refs[14:24]
        (loc, sa, ra, sb, rb, sc, rc) = refs[24:]
    else:
        (x_hbm, seg, ga_hbm, qkv_o, mix_o, feat_o, vec_o) = refs[:7]
        (x_v, now_v, next_v, mix_v, feat_v, fq, fk, ga) = refs[7:15]
        (loc,) = refs[15:]
    rows, length = seg.shape
    width = x_v.shape[1]
    pairs = width // LANES
    step_rows = width // SLOTS

    x_copy = pltpu.make_async_copy(x_hbm, x_v, loc.at[pairs, 0])
    count = SLOTS * 6
    if comm:
        here = Place()
        here.greet()
        own = (here.dp, here.z, here.c)
        for p in range(pairs):
            for j in range(3):
                begin = j * width + p * LANES
                ga[(p,) + own + (slice(None), slice(j * LANES, (j + 1) * LANES))] = wqkv[
                    :, begin : begin + LANES
                ].astype(bf16)
        rest = jnp.concatenate([vec[:, LANES:], jnp.zeros((1, 2 * LANES - count), f32)], axis=1)
        row = lax.broadcasted_iota(jnp.int32, (step_rows, LANES), 0)
        tile = jnp.where(row == 0, vec[:, :LANES], jnp.where(row == 1, rest, 0.0))
        ga[(0,) + own + (slice(None), slice(3 * LANES, 4 * LANES))] = tile.astype(bf16)
        gathers = [
            Gather(here, ga.at[p], slice(0, 4 * LANES if p == 0 else 3 * LANES), sa.at[p], ra.at[p], True)
            for p in range(pairs)
        ]
        every = slice(0, width)
        gathers.append(Gather(here, gb, every, sb, rb, False))
        gathers.append(Gather(here, gc, every, sc, rc, False))
        here.greeted()
        gathers[0].step(0)
        x_copy.start()
        for p in range(1, pairs):
            gathers[p].step(0)
        gb[own + (slice(0, step_rows),)] = wp[...].astype(bf16)
        for j in range(4):
            gb[own + (slice((j + 1) * step_rows, (j + 2) * step_rows),)] = wu[
                :, j * width : (j + 1) * width
            ].astype(bf16)
        gc[own] = wd[...].astype(bf16)
    else:
        x_copy.start()
        ga_copy = pltpu.make_async_copy(ga_hbm, ga, loc.at[pairs, 1])
        ga_copy.start()

    def marks_of(r):
        ones, against = segment_columns(seg[r : r + 1, :])
        fq[r] = ones
        fk[r] = against

    def transfer(*steps):
        for group, number in steps:
            gathers[group].step(number)

    if comm:
        transfer((0, 1), (1, 1))
        marks_of(0)
        transfer((0, 2), (0, 3), (4, 0), (2, 1), (5, 0))
        for r in range(1, rows):
            marks_of(r)
        transfer((0, 4))
    else:
        for r in range(rows):
            marks_of(r)
        ga_copy.wait()
    x_copy.wait()

    lane = lax.broadcasted_iota(jnp.int32, (1, LANES), 1)

    def half_of(number, upper):
        part = number % 3
        row = part // 2
        i = number // 3
        tile = ga[0, i // 8, i % 8 // 2, i % 2, :, 3 * LANES : 4 * LANES].astype(f32)
        tile = tile if upper == (part == 1) else pltpu.roll(tile, HEAD, 1)
        return tile[row : row + 1, :]

    def assemble(first, last):
        for t in range(first, last):
            line = jnp.where(lane < HEAD, half_of(2 * t, False), half_of(2 * t + 1, True))
            vec_o[t // 4 : t // 4 + 1, t % 4 * LANES : (t % 4 + 1) * LANES] = line

    assemble(4 * pairs, 6 * pairs)

    def columns_at(p):
        return pl.ds(pl.multiple_of(p * LANES, LANES), LANES)

    def project(p, part):
        lin = nn(x_v[part, :], merged(ga[p, :, :, :, :, : 3 * LANES]))
        query = (lin[:, :LANES] + vec_o[4:5, columns_at(p)]).astype(bf16).astype(f32) * scale
        next_v[0, part, :] = query.astype(bf16)
        next_v[1, part, :] = lin[:, LANES : 2 * LANES].astype(bf16)
        next_v[2, part, :] = (lin[:, 2 * LANES :] + vec_o[5:6, columns_at(p)]).astype(bf16)

    for t in range(rows * length // 512):
        project(0, slice(t * 512, (t + 1) * 512))
    if comm:
        transfer((1, 2), (1, 3))
    assemble(0, 4 * pairs)
    assemble(6 * pairs, 12 * pairs)
    vec_o[12:16, :] = jnp.zeros((4, width), f32)
    low_half, high_half = half_rows()
    half = lax.broadcasted_iota(jnp.int32, (QB, LANES), 1) < HEAD

    def attend(p, r):
        span = slice(r * length, (r + 1) * length)
        columns = columns_at(p)
        keys = now_v[1, span, :]
        values = now_v[2, span, :]
        keys_in = (keys * low_half + fk[r] * high_half, keys * high_half + fk[r] * low_half)
        one_low = jnp.broadcast_to(low_half, values.shape)
        one_high = jnp.broadcast_to(high_half, values.shape)
        values_in = (
            jnp.concatenate([values * low_half, one_low], axis=1),
            jnp.concatenate([values * high_half, one_high], axis=1),
        )

        def scores(j, h):
            part = slice(r * length + j * QB, r * length + (j + 1) * QB)
            query = now_v[0, part, :]
            marks = fq[r, j * QB : (j + 1) * QB, :]
            mine, other = (low_half, high_half) if h == 0 else (high_half, low_half)
            return nt(query * mine + marks * other, keys_in[h])

        blocks = [(j, h) for j in range(length // QB) for h in range(2)]
        following = scores(*blocks[0])
        kept = []
        for number, (j, h) in enumerate(blocks):
            current = following
            if number + 1 < len(blocks):
                following = scores(*blocks[number + 1])
            part = slice(r * length + j * QB, r * length + (j + 1) * QB)
            if r == rows - 1:
                share = rows * length // len(blocks)
                project(jnp.minimum(p + 1, pairs - 1), slice(number * share, (number + 1) * share))
            peak = jnp.max(current, axis=1, keepdims=True)
            soft = jnp.exp(current - peak).astype(bf16)
            kept.append((peak, nn(soft, values_in[h])))
            if h == 1:
                both = kept[0][1] + kept[1][1]
                total = both[:, LANES:]
                mix_v[part, columns] = (both[:, :LANES] / total).astype(bf16)
                logs = jnp.where(half, kept[0][0], kept[1][0]) + jnp.log(total)
                logs = pltpu.roll(logs, HEAD, 1)
                marks = fq[r, j * QB : (j + 1) * QB, :].astype(f32)
                feat_v[part, columns] = part_columns(-logs, marks).astype(bf16)
                kept = []

    schedule = (
        ((1, 4), (2, 2), (2, 3), (3, 1)),
        ((4, 1), (3, 2), (3, 3)),
        ((2, 4), (5, 1)),
        ((4, 2),),
        ((3, 4),),
        ((5, 2),),
        ((4, 3),),
        ((5, 3), (4, 4), (5, 4)),
    )

    def pair_out(p, which):
        columns = columns_at(p)
        found = [(now_v, qkv_o.at[p])] if which == 0 else [
            (mix_v.at[:, columns], mix_o.at[:, columns]),
            (feat_v.at[:, columns], feat_o.at[:, columns]),
        ]
        if comm and which == 1:
            found.append((ga.at[p], ga_o.at[p]))
        return [
            pltpu.make_async_copy(src, dst, loc.at[p, 3 * which + k])
            for k, (src, dst) in enumerate(found)
        ]

    def pair(p, carry):
        @pl.when(p > 0)
        def _():
            for copy in pair_out(p - 1, 0):
                copy.wait()

        now_v[...] = next_v[...]
        for copy in pair_out(p, 0):
            copy.start()
        for r in range(rows):
            attend(p, r)
            if comm:
                for number in range(pairs):
                    steps = schedule[rows * number + r]
                    pl.when(p == number)(functools.partial(transfer, *steps))
        for copy in pair_out(p, 1):
            copy.start()
        return carry

    lax.fori_loop(0, pairs, pair, 0)
    copies = pair_out(pairs - 1, 0)
    if comm:
        last = [
            pltpu.make_async_copy(src, dst, loc.at[pairs, 2 + k])
            for k, (src, dst) in enumerate(((gb, gb_o), (gc, gc_o)))
        ]
        for copy in last:
            copy.start()
        copies += last
        for group in gathers:
            group.finish()
    for p in range(pairs):
        copies += pair_out(p, 1)
    for copy in copies:
        copy.wait()


def row_mean(value):
    return jnp.mean(value, axis=-1, keepdims=True)


def column_sum(value):
    return jnp.sum(value, axis=0, keepdims=True)


def middle_kernel(
    seg, vec, x_hbm, mix_hbm, dual_hbm, cs_hbm, cd_hbm, gb_hbm, gc_hbm,
    so_o, do_o, one_o, gm_o, pg_o, vg_o,
    x_v, mix_v, dual_v, cs_v, cd_v, gb, gc, low_v, spread_v, two_v, ffn_v, hid_v, slope_v, pg_v,
    attn_v, sum_v,
    in_sem, out_sem, w_sem,
):
    rows, length = seg.shape
    tokens, width = x_v.shape
    blocks = hid_v.shape[0]
    step_rows = width // SLOTS
    tile = 512
    tiles = tokens // tile
    per_row = length // tile

    def rows_of(t, size=tile):
        return pl.ds(pl.multiple_of(t * size, size), size)

    w_copies = [
        pltpu.make_async_copy(gb_hbm, gb, w_sem.at[0]),
        pltpu.make_async_copy(gc_hbm, gc, w_sem.at[1]),
    ]
    pairs_in = ((mix_hbm, mix_v), (x_hbm, x_v), (cs_hbm, cs_v), (cd_hbm, cd_v), (dual_hbm, dual_v))

    def in_copy(k, t):
        src, dst = pairs_in[k]
        return pltpu.make_async_copy(src.at[rows_of(t)], dst.at[rows_of(t)], in_sem.at[k, t])

    in_copy(0, 0).start()
    in_copy(1, 0).start()
    w_copies[0].start()
    w_copies[1].start()
    for k in range(2, 5):
        in_copy(k, 0).start()
    for t in range(1, tiles):
        for k in range(5):
            in_copy(k, t).start()
    pairs_out = ((cs_v, so_o), (dual_v, do_o), (dual_v, one_o), (ffn_v, gm_o))

    def out_copy(k, t):
        src, dst = pairs_out[k]
        return pltpu.make_async_copy(src.at[rows_of(t)], dst.at[rows_of(t)], out_sem.at[k, t])

    vg_o[...] = jnp.zeros_like(vg_o)
    gain_one, shift_one, gain_two, shift_two = (vec[k : k + 1, :] for k in range(4))
    bias_o, bias_d = vec[6:7, :], vec[7:8, :]
    w_copies[0].wait()
    lane = lax.broadcasted_iota(jnp.int32, (1, width), 1)

    def proj_weight():
        return merged(gb[:, :, :, 0:step_rows, :])

    def up_weight(f):
        return merged(gb[:, :, :, (f + 1) * step_rows : (f + 2) * step_rows, :])

    def down_weight(f):
        return merged(gc[f])

    def first_half(t):
        here = rows_of(t)
        attn = nn(mix_v[here, :], proj_weight()) + bias_o
        first_sum = x_v[here, :].astype(f32) + attn
        centred = first_sum - row_mean(first_sum)
        spread = lax.rsqrt(row_mean(centred * centred) + NORM_EPS)
        hat = centred * spread
        x_v[here, :] = hat.astype(bf16)
        spread_v[here, :] = jnp.broadcast_to(spread, (tile, LANES))
        first_norm = hat * gain_one + shift_one
        low_v[here, :] = first_norm.astype(bf16)
        two_v[here, :] = first_norm
        attn_v[...] = attn

    def feed(t):
        here = rows_of(t)
        first_low = low_v[here, :]
        ffn = bias_d
        upper = nn(first_low, up_weight(0))
        for f in range(blocks):
            u = upper + vec[8 + f : 9 + f, :]
            if f + 1 < blocks:
                upper = nn(first_low, up_weight(f + 1))
            square = u * u
            inner = jnp.tanh(u * (0.7978845608028654 + 0.035677408136300125 * square))
            share = 0.5 + 0.5 * inner
            hidden = u * share
            slope = share + hidden * (1.0 - share) * (
                1.5957691216057308 + 0.21406444881780073 * square
            )
            hidden = hidden.astype(bf16)
            hid_v[f, here, :] = hidden
            slope_v[f, here, :] = slope.astype(bf16)
            ffn = ffn + nn(hidden, down_weight(f))
        sum_v[...] = ffn

    def second_half(t):
        here = rows_of(t)
        attn = attn_v[...]
        ffn = sum_v[...]
        dual_v[here, :] = dual_v[here, :] + attn + ffn
        second_sum = two_v[here, :] + ffn
        centred = second_sum - row_mean(second_sum)
        spread = lax.rsqrt(row_mean(centred * centred) + NORM_EPS)
        hat = centred * spread
        second_norm = hat * gain_two + shift_two
        cot = cs_v[here, :].astype(f32)
        cs_v[here, :] = second_norm.astype(bf16)
        r = t // per_row
        ids = seg[pl.ds(r, 1), pl.ds(pl.multiple_of((t - r * per_row) * tile, tile), tile)]
        valid = jnp.where(ids != 0, 1.0, 0.0)
        valid = jnp.transpose(jnp.broadcast_to(valid, (LANES, tile)))[:, 0:1]
        counts = column_sum(valid) * width
        squares = [
            jnp.sum(column_sum(valid * (v * v)), axis=1, keepdims=True)
            for v in (second_norm, attn, ffn)
        ]
        line = jnp.where(lane == 0, counts, 0.0)
        for k in range(3):
            line = jnp.where(lane == k + 1, squares[k], line)
        vg_o[12:13, :] += line
        scaled = cot * gain_two
        grad = (scaled - row_mean(scaled) - hat * row_mean(scaled * hat)) * spread
        two_v[here, :] = grad
        vg_o[2:3, :] += column_sum(cot * hat)
        vg_o[3:4, :] += column_sum(cot)
        grad_low = (grad + cd_v[here, :].astype(f32)).astype(bf16)
        ffn_v[here, :] = grad_low
        vg_o[7:8, :] += column_sum(grad_low.astype(f32))

    def arrived(t, kinds):
        for k in kinds:
            in_copy(k, t).wait()

    def leave(t, kinds):
        for k in kinds:
            out_copy(k, t).start()

    def forward(t, carry):
        arrived(t, (0, 1))
        first_half(t)

        @pl.when(t == 0)
        def _():
            w_copies[1].wait()

        arrived(t, (2, 3, 4))
        feed(t)
        second_half(t)
        leave(t, (0, 1))
        return carry

    lax.fori_loop(0, tiles, forward, 0)

    pg_copies = []

    def pg_out(*where):
        copy = pltpu.make_async_copy(pg_v.at[where], pg_o.at[where], w_sem.at[len(pg_copies) + 2])
        copy.start()
        pg_copies.append(copy)

    every = slice(None)
    def back_hidden(f, carry):
        total = jnp.zeros((1, width), f32)
        for t in range(tokens // 512):
            here = slice(t * 512, (t + 1) * 512)
            grad = nt(ffn_v[here, :], down_weight(f))
            grad_up = (slope_v[f, here, :].astype(f32) * grad).astype(bf16)
            slope_v[f, here, :] = grad_up
            total = total + column_sum(grad_up.astype(f32))
        vg_o[pl.ds(8 + f, 1), :] = total
        return carry

    lax.fori_loop(0, blocks, back_hidden, 0)

    def weight_grads(f, carry):
        down = tn(hid_v[f], ffn_v[...])
        pg_v[f, :, :, 5 * step_rows :, :] = down.astype(bf16).reshape(4, 2, 4 * step_rows, width)
        up = tn(low_v[...], slope_v[f])
        rows_f = pl.ds(pl.multiple_of((f + 1) * step_rows, step_rows), step_rows)
        pg_v[:, :, :, rows_f, :] = up.astype(bf16).reshape(4, 4, 2, step_rows, width)
        return carry

    lax.fori_loop(0, blocks, weight_grads, 0)
    pg_out(every, every, every, slice(step_rows, 9 * step_rows))

    def grad_of_first(t):
        here = rows_of(t)
        grad = two_v[here, :]
        for f in range(blocks):
            grad = grad + nt(slope_v[f, here, :], up_weight(f))
        sum_v[...] = grad

    def back_first(t):
        here = rows_of(t)
        grad = sum_v[...]
        hat = x_v[here, :].astype(f32)
        scaled = grad * gain_one
        spread = spread_v[here, 0:1]
        grad_one = (scaled - row_mean(scaled) - hat * row_mean(scaled * hat)) * spread
        dual_v[here, :] = grad_one
        grad_low = (grad_one + cd_v[here, :].astype(f32)).astype(bf16)
        low_v[here, :] = grad_low
        ffn_v[here, :] = nt(grad_low, proj_weight()).astype(bf16)
        vg_o[0:1, :] += column_sum(grad * hat)
        vg_o[1:2, :] += column_sum(grad)
        vg_o[6:7, :] += column_sum(grad_low.astype(f32))

    for t in range(tiles):
        out_copy(1, t).wait()

    def backward(t, carry):
        grad_of_first(t)
        back_first(t)
        leave(t, (2, 3))
        return carry

    lax.fori_loop(0, tiles, backward, 0)
    proj = tn(mix_v[...], low_v[...])
    pg_v[:, :, :, 0:step_rows, :] = proj.astype(bf16).reshape(4, 4, 2, step_rows, width)
    pg_out(every, every, every, slice(0, step_rows))
    for t in range(tiles):
        for k in (0, 2, 3):
            out_copy(k, t).wait()
    for copy in pg_copies:
        copy.wait()


class Scatter:
    def __init__(self, here, send, mine, bufs, send_sem, recv_sem, straight):
        self.here, self.source, self.mine = here, send, mine
        self.from_core, self.from_b, self.from_a, self.from_z = bufs
        self.send_sem, self.recv_sem, self.straight = send_sem, recv_sem, straight
        self.last = 2 if straight else 3

    def copies(self, phase):
        me, mine = self.here, self.mine
        if phase == 0:
            base, found = 0, [(self.source, self.from_core, me.to_core)]
        elif phase == self.last:
            base = 4
            found = [
                (mine.at[me.dp, me.zs[k]], self.from_z.at[k - 1], me.to_z[k]) for k in range(1, 4)
            ]
        elif self.straight:
            base = 1
            found = [
                (mine.at[me.ab], self.from_a, me.to_ab),
                (mine.at[me.a], self.from_b.at[0], me.to_a),
                (mine.at[me.b], self.from_b.at[1], me.to_b),
            ]
        elif phase == 1:
            base = 1
            found = [
                (mine.at[me.b], self.from_b.at[0], me.to_b),
                (mine.at[me.ab], self.from_b.at[1], me.to_b),
            ]
        else:
            base, found = 3, [(mine.at[me.a], self.from_a, me.to_a)]
        return [
            remote(src, dst, self.send_sem.at[base + k], self.recv_sem.at[base + k], device)
            for k, (src, dst, device) in enumerate(found)
        ]

    def start(self, phase):
        for copy in self.copies(phase):
            copy.start()

    def add(self, phase):
        me, mine = self.here, self.mine
        for copy in self.copies(phase):
            copy.wait_recv()

        def into(where, *parts):
            if len(parts) == 1:
                mine[where] = mine[where] + parts[0]
            else:
                total = mine[where].astype(f32)
                for part in parts:
                    total = total + part.astype(f32)
                mine[where] = total.astype(bf16)

        for z in range(4):
            if phase == 0:
                for d in range(4):
                    into((d, z), self.from_core[d, z])
            elif self.straight:
                into((me.dp, z), self.from_a[z], self.from_b[0, z], self.from_b[1, z])
            elif phase == 1:
                into((me.dp, z), self.from_b[0, z])
                into((me.a, z), self.from_b[1, z])
            else:
                into((me.dp, z), self.from_a[z])

    def result(self):
        for copy in self.copies(self.last):
            copy.wait_recv()
        total = self.mine[self.here.dp, self.here.z].astype(f32)
        for k in range(3):
            total = total + self.from_z[k].astype(f32)
        return total

    def finish(self):
        for phase in range(self.last + 1):
            for copy in self.copies(phase):
                copy.wait_send()


class Total:
    def __init__(self, here, own, bufs, send_sem, recv_sem):
        self.here, self.own, self.bufs = here, own, bufs
        self.send_sem, self.recv_sem = send_sem, recv_sem

    def copies(self, phase):
        me, bufs = self.here, self.bufs
        if phase == 0:
            found = [(self.own, bufs.at[0], 0, me.to_core)]
        else:
            slot = 1 + me.dp if phase == 1 else 5 + me.z
            devices = [me.to_a, me.to_b, me.to_ab] if phase == 1 else me.to_z[1:]
            found = [(bufs.at[slot], bufs.at[slot], slot, device) for device in devices]
        return [
            remote(src, dst, self.send_sem.at[3 * phase + k], self.recv_sem.at[slot], device)
            for k, (src, dst, slot, device) in enumerate(found)
        ]

    def start(self, phase):
        for copy in self.copies(phase):
            copy.start()

    def arrive(self, *slots):
        for slot in slots:
            ref = self.bufs.at[slot]
            remote(ref, ref, self.send_sem.at[0], self.recv_sem.at[slot], self.here.to_core).wait_recv()

    def add(self, phase):
        me, bufs = self.here, self.bufs
        if phase == 0:
            self.arrive(0)
            bufs[1 + me.dp] = self.own[...] + bufs[0]
        else:
            self.arrive(1 + me.a, 1 + me.b, 1 + me.ab)
            bufs[5 + me.z] = bufs[1] + bufs[2] + bufs[3] + bufs[4]

    def result(self):
        self.arrive(*[5 + self.here.zs[k] for k in range(1, 4)])
        bufs = self.bufs
        return bufs[5] + bufs[6] + bufs[7] + bufs[8]

    def finish(self):
        for phase in range(3):
            for copy in self.copies(phase):
                copy.wait_send()


def backward_kernel(comm, scale, *refs):
    (seg, vg, qkv_hbm, feat_hbm, mix_hbm, gm_hbm, one_hbm, x_hbm, ga_hbm) = refs[:9]
    if comm:
        (pg_hbm, sg_o, tot_o, totq_o, vg_o) = refs[9:14]
        refs = refs[14:]
    else:
        (sg_o, pq_o, vg_o) = refs[9:12]
        refs = refs[12:]
    (qkv_v, feat_v, mix_v, gm_v, one_v, x_v, ga, gq_v, fk, pq_v, in_sem, w_sem, out_sem) = refs[:13]
    rows, length = seg.shape
    tokens, width = x_v.shape
    pairs = width // LANES
    step_rows = width // SLOTS

    def pair_copies(p):
        columns = pl.ds(pl.multiple_of(p * LANES, LANES), LANES)
        found = [(qkv_hbm.at[p], qkv_v.at[p])]
        found += [
            (src.at[:, columns], dst.at[:, columns])
            for src, dst in ((gm_hbm, gm_v), (mix_hbm, mix_v), (feat_hbm, feat_v))
        ]
        return [
            pltpu.make_async_copy(src, dst, in_sem.at[p, k]) for k, (src, dst) in enumerate(found)
        ]

    late = [
        pltpu.make_async_copy(src, dst, w_sem.at[k])
        for k, (src, dst) in enumerate(((x_hbm, x_v), (ga_hbm, ga), (one_hbm, one_v)))
    ]
    if comm:
        (mine, fc, fb, fa, fz, mine_q, qc, qb, qa, qz, vp, vb, s1, r1, s2, r2, s3, r3) = refs[13:]
        here = Place()
        here.greet()
        weights = [
            Scatter(
                here,
                pg_hbm.at[:, :, 1 - here.c, pl.ds(g * 3 * step_rows, 3 * step_rows)],
                mine.at[g],
                (fc.at[g], fb.at[g], fa.at[g], fz.at[g]),
                s1.at[g],
                r1.at[g],
                False,
            )
            for g in range(3)
        ]
        columns_of = [
            Scatter(
                here,
                pq_v.at[p, :, :, 1 - here.c],
                mine_q.at[p],
                (qc.at[p], qb.at[p], qa.at[p], qz.at[p]),
                s2.at[p],
                r2.at[p],
                True,
            )
            for p in range(pairs)
        ]
        sums = Total(here, vp, vb, s3, r3)
        vp[...] = vg[...]
        mine_copies = [
            pltpu.make_async_copy(
                pg_hbm.at[:, :, here.c, pl.ds(g * 3 * step_rows, 3 * step_rows)], mine.at[g], w_sem.at[3 + g]
            )
            for g in range(3)
        ]
    if not comm:
        vg_o[...] = vg[...]
    vector = vp if comm else vg_o
    for copy in pair_copies(0):
        copy.start()
    if comm:
        for copy in mine_copies:
            copy.start()
    for p in range(1, pairs):
        for copy in pair_copies(p):
            copy.start()
    for copy in late:
        copy.start()
    for r in range(rows):
        fk[r] = segment_columns(seg[r : r + 1, :])[1]
    if comm:
        here.greeted()
        for group in weights:
            group.start(0)
    low_half, high_half = half_rows()

    def transfer(number):
        if number == 0:
            for copy in mine_copies:
                copy.wait()
        for group, steps in list(zip(weights, ((0, 2, 3), (1, 3, 4), (3, 5, 6)))) + [
            (columns_of[p], (rows * p + rows, rows * p + rows + 1)) for p in range(pairs)
        ]:
            for phase in range(group.last):
                if number == steps[phase]:
                    group.add(phase)
                    group.start(phase + 1)
        for p in range(pairs):
            if number == rows * (p + 1) - 1:
                columns_of[p].start(0)
                mine_q[p] = pq_v[p, :, :, here.c]
        if number == rows * pairs - 1:
            sums.start(0)

    def attend(i, carry):
        p = i // rows
        r = lax.rem(i, rows)
        span = pl.ds(pl.multiple_of(r * length, length), length)
        columns = pl.ds(pl.multiple_of(p * LANES, LANES), LANES)

        @pl.when(r == 0)
        def _():
            for copy in pair_copies(p):
                copy.wait()

        queries = qkv_v[p, 0, span, :]
        keys = qkv_v[p, 1, span, :]
        values = qkv_v[p, 2, span, :]
        grads = gm_v[span, columns]
        marks = feat_v[span, columns]
        product = grads.astype(f32) * mix_v[span, columns].astype(f32)
        is_low = lax.broadcasted_iota(jnp.int32, product.shape, 1) < HEAD
        for_low = jnp.sum(jnp.where(is_low, product, 0.0), axis=1, keepdims=True)
        for_high = jnp.sum(jnp.where(is_low, 0.0, product), axis=1, keepdims=True)
        deltas = part_columns(-jnp.where(is_low, for_high, for_low), 0.0).astype(bf16)
        place = lax.rem(lax.broadcasted_iota(jnp.int32, (1, LANES), 1), HEAD)
        ones = jnp.where((place >= 16) & (place < 19), 1.0, 0.0).astype(bf16)
        queries_t = jnp.transpose(queries)
        grads_t = jnp.transpose(grads)
        key_parts, value_parts = [], []
        query_grads = [None] * (length // QB)
        for h in range(2):
            mine_h, other_h = (low_half, high_half) if h == 0 else (high_half, low_half)
            half = slice(h * HEAD, (h + 1) * HEAD)
            key_own = keys * mine_h
            key_in = key_own + fk[r] * other_h
            value_in = values * mine_h + ones * other_h
            key_sum = value_sum = None
            for j in range(length // QB):
                part = slice(j * QB, (j + 1) * QB)
                soft = jnp.exp(nt(queries[part] * mine_h + marks[part] * other_h, key_in))
                wide = nt(grads[part] * mine_h + deltas[part] * other_h, value_in)
                back = (soft * wide).astype(bf16)
                soft = soft.astype(bf16)
                moved = nn(back, key_own)
                query_grads[j] = moved if h == 0 else query_grads[j] + moved
                value_part = nn(grads_t[half, part], soft)
                key_part = nn(queries_t[half, part], back)
                value_sum = value_part if j == 0 else value_sum + value_part
                key_sum = key_part if j == 0 else key_sum + key_part
            key_parts.append(key_sum)
            value_parts.append(value_sum)
        for j in range(length // QB):
            part = pl.ds(pl.multiple_of(r * length + j * QB, QB), QB)
            gq_v[0, part, columns] = (query_grads[j] * scale).astype(bf16)
        gq_v[1, span, columns] = jnp.transpose(jnp.concatenate(key_parts, axis=0)).astype(bf16)
        gq_v[2, span, columns] = jnp.transpose(jnp.concatenate(value_parts, axis=0)).astype(bf16)

        @pl.when(r == rows - 1)
        def _():
            @pl.when(p == 0)
            def _():
                late[0].wait()

            stacked = jnp.concatenate([gq_v[j, :, columns] for j in range(3)], axis=1)
            for k, j in ((4, 0), (5, 2)):
                part = stacked[:, j * LANES : (j + 1) * LANES].astype(f32)
                vector[k : k + 1, columns] = column_sum(part)
            grad = tn(x_v[...], stacked).astype(bf16).reshape(4, 4, 2, step_rows, 3 * LANES)
            for j in range(3):
                pq_v[p, :, :, :, j * step_rows : (j + 1) * step_rows, :] = grad[
                    ..., j * LANES : (j + 1) * LANES
                ]

        if comm:
            for number in range(rows * pairs):
                pl.when(i == number)(functools.partial(transfer, number))
        return carry

    lax.fori_loop(0, rows * pairs, attend, 0)
    late[1].wait()
    late[2].wait()

    if not comm:
        pq_copy = pltpu.make_async_copy(pq_v, pq_o, out_sem.at[4])
        pq_copy.start()

    def out_copy(t):
        span = pl.ds(pl.multiple_of(t * 512, 512), 512)
        return pltpu.make_async_copy(one_v.at[span, :], sg_o.at[span, :], out_sem.at[t])

    def stream(t):
        span = pl.ds(t * 512, 512)
        total = one_v[span, :]
        for j in range(3):
            total = total + nt(
                gq_v[j, span, :],
                jnp.concatenate(
                    [merged(ga[p, :, :, :, :, j * LANES : (j + 1) * LANES]) for p in range(pairs)],
                    axis=1,
                ),
            )
        one_v[span, :] = total
        out_copy(t).start()

    for t in range(tokens // 512):
        stream(t)
        if comm:
            transfer(rows * pairs + t)
            if t < 2:
                sums.add(t)
                sums.start(t + 1)
    if comm:
        for g in range(3):
            tot_o[g * 3 * step_rows : (g + 1) * 3 * step_rows, :] = weights[g].result()
        for p in range(pairs):
            totq_o[p] = columns_of[p].result()
        vg_o[...] = sums.result()
        for group in columns_of + weights + [sums]:
            group.finish()
    else:
        pq_copy.wait()
    for t in range(tokens // 512):
        out_copy(t).wait()


def adam(weight, gradient, first_old, second, rates):
    step_rate, decay_rate = rates
    first_new = BETA_FIRST * first_old + (1.0 - BETA_FIRST) * gradient
    second_new = BETA_SECOND * second + (1.0 - BETA_SECOND) * gradient * gradient
    first_hat = first_new / (1.0 - BETA_FIRST**STEP)
    second_hat = second_new / (1.0 - BETA_SECOND**STEP)
    updated = weight - step_rate * (
        first_hat / (jnp.sqrt(second_hat) + ADAM_EPS) + decay_rate * weight
    )
    return second_new, updated


def update_kernel(tot, totq, vg, sg_hbm, *refs):
    weights, firsts, seconds = refs[0:5], refs[5:10], refs[10:15]
    sg_o, root, grads, renewed, updated = refs[15], refs[16], refs[17:22], refs[22:27], refs[27:32]
    sg_v, sem = refs[32:]
    size = sg_hbm.shape[0] // 8
    copies = []
    for t in range(8):
        span = pl.ds(t * size, size)
        copies.append(pltpu.make_async_copy(sg_hbm.at[span], sg_v.at[span], sem.at[0, t]))
        copies.append(pltpu.make_async_copy(sg_v.at[span], sg_o.at[span], sem.at[1, t]))
    for copy in copies[0::2]:
        copy.start()
    width = tot.shape[1]
    step_rows = width // SLOTS
    pairs = width // LANES

    def apply(k, columns, gradient):
        where = (slice(None), columns)
        grads[k][where] = gradient
        renewed[k][where], updated[k][where] = adam(
            weights[k][where], gradient, firsts[k][where], seconds[k][where], RATES[k]
        )

    for j in range(3):
        for p in range(pairs):
            begin = j * width + p * LANES
            apply(0, slice(begin, begin + LANES), totq[p, j * step_rows : (j + 1) * step_rows, :])
    apply(1, slice(None), tot[0:step_rows, :])
    for j in range(4):
        apply(2, slice(j * width, (j + 1) * width), tot[(j + 1) * step_rows : (j + 2) * step_rows, :])
    apply(3, slice(None), tot[5 * step_rows :, :])
    for t in range(8):
        copies[2 * t].wait()
        copies[2 * t + 1].start()
    count = weights[4].shape[1]
    begin = (lax.axis_index("dp") * 8 + lax.axis_index("fsdp")) * count
    top = begin // width
    shift = begin - top * width
    row = lax.broadcasted_iota(jnp.int32, vg.shape, 0)
    lane = lax.broadcasted_iota(jnp.int32, vg.shape, 1)
    kept = ((row == top) & (lane >= shift)) | ((row == top + 1) & (lane < shift))
    line = column_sum(jnp.where(kept, vg[...], 0.0))
    line = pltpu.roll(jnp.broadcast_to(line, (8, width)), lax.rem(width - shift, width), 1)
    apply(4, slice(None), line[0:1, :count])
    sums = vg[12:13, 0:LANES]
    means = jnp.sqrt(sums / sums[:, 0:1])
    lane = lax.broadcasted_iota(jnp.int32, means.shape, 1)
    for k in range(3):
        root[k] = jnp.sum(jnp.where(lane == k + 1, means, 0.0))
    for copy in copies[1::2]:
        copy.wait()


def params(**more):
    return pltpu.CompilerParams(vmem_limit_bytes=62 * 2**20, **more)


def shape(dims, kind):
    return jax.ShapeDtypeStruct(dims, kind)


def pack_columns(full, blocks):
    width = full.shape[0]
    parts = full.reshape(SLOTS, width // SLOTS, blocks, width)
    return jnp.swapaxes(parts, 1, 2).reshape(SLOTS, -1, width)


def unpack_columns(packed, blocks):
    width = packed.shape[-1]
    parts = packed.reshape(SLOTS, blocks, width // SLOTS, width)
    return jnp.swapaxes(parts, 1, 2).reshape(width, blocks * width)


def per_device(comm, *args):
    (stream_in, dual_in, segment_ids) = args[:3]
    weights, firsts, seconds = args[3:8], args[8:13], args[13:18]
    cot_stream, cot_dual = args[18:]
    tokens, width = stream_in.shape
    rows, length = segment_ids.shape
    pairs = width // LANES
    hidden = weights[2].shape[1]
    blocks = hidden // width
    unit = width // SLOTS
    scale = HEAD**-0.5
    slots = (4, 4, 2)
    dma = pltpu.SemaphoreType.DMA
    sem_gather = [dma((10,)), dma((12,))]
    ga_shape = (pairs,) + slots + (unit, 4 * LANES)
    gb_shape, gc_shape = (slots + (n, width) for n in (5 * unit, 4 * unit))

    def vm(dims, kind=bf16):
        return pltpu.VMEM(dims, kind)

    flat = (tokens, width)
    common_out = [
        shape((pairs, 3, tokens, LANES), bf16),
        shape(flat, bf16),
        shape(flat, bf16),
        shape((16, width), f32),
    ]
    common_scratch = [
        vm(flat),
        vm((3, tokens, LANES)),
        vm((3, tokens, LANES)),
        vm(flat),
        vm(flat),
        vm((rows, length, LANES)),
        vm((rows, length, LANES)),
        vm(ga_shape),
    ]
    cost = pl.CostEstimate(flops=8 * 10**9, bytes_accessed=2 * 10**7, transcendentals=2 * 10**7)
    if comm:
        masters = [w if w.ndim == 2 else w.reshape(1, -1) for w in weights]
        qkv, mix, feat, vec, ga, gb, gc = pl.pallas_call(
            functools.partial(forward_kernel, True, scale),
            out_shape=common_out + [shape(s, bf16) for s in (ga_shape, gb_shape, gc_shape)],
            in_specs=[ANY] + [VMEM] * 6,
            out_specs=[ANY] * 3 + [VMEM] + [ANY] * 3,
            scratch_shapes=common_scratch
            + [vm(gb_shape), vm(gc_shape), dma((pairs + 1, 6))]
            + [dma((pairs, 10)), dma((pairs, 12))]
            + sem_gather * 2,
            compiler_params=params(collective_id=0, has_side_effects=True),
            cost_estimate=cost,
            name="gather_forward",
        )(stream_in, segment_ids, *masters)
    else:
        full = [lax.all_gather(w.astype(bf16), AXES, axis=0, tiled=True) for w in weights]
        packed = pack_columns(full[0], 3).reshape(SLOTS, 3, unit, pairs, LANES)
        packed = packed.transpose(3, 0, 2, 1, 4).reshape(pairs, SLOTS, unit, 3 * LANES)
        vec_pad = jnp.pad(full[4].reshape(SLOTS, -1), ((0, 0), (0, HEAD))).reshape(SLOTS, 2, LANES)
        vec_pad = jnp.pad(vec_pad[None], ((0, pairs - 1), (0, 0), (0, unit - 2), (0, 0)))
        ga = jnp.concatenate([packed, vec_pad], axis=3).reshape(ga_shape)
        gb = jnp.concatenate(
            [pack_columns(full[1], 1), pack_columns(full[2], blocks)], axis=1
        ).reshape(gb_shape)
        gc = full[3].reshape(gc_shape)
        qkv, mix, feat, vec = pl.pallas_call(
            functools.partial(forward_kernel, False, scale),
            out_shape=common_out,
            in_specs=[ANY, VMEM, ANY],
            out_specs=[ANY] * 3 + [VMEM],
            scratch_shapes=common_scratch + [dma((pairs + 1, 6))],
            compiler_params=params(),
            cost_estimate=cost,
            name="forward",
        )(stream_in, segment_ids, ga)

    pg_shape = slots + (9 * unit, width)
    tiles = tokens // 512
    stream_out, dual_out, grad_one, grad_mixed, pg, vg = pl.pallas_call(
        middle_kernel,
        out_shape=[
            shape(flat, bf16),
            shape(flat, f32),
            shape(flat, f32),
            shape(flat, bf16),
            shape(pg_shape, bf16),
            shape((16, width), f32),
        ],
        in_specs=[VMEM, VMEM] + [ANY] * 7,
        out_specs=[ANY] * 5 + [VMEM],
        scratch_shapes=[
            vm(flat),
            vm(flat),
            vm(flat, f32),
            vm(flat),
            vm(flat),
            vm(gb_shape),
            vm(gc_shape),
            vm(flat),
            vm((tokens, LANES), f32),
            vm(flat, f32),
            vm(flat),
            vm((blocks, tokens, width)),
            vm((blocks, tokens, width)),
            vm(pg_shape),
            vm((512, width), f32),
            vm((512, width), f32),
            dma((5, tiles)),
            dma((4, tiles)),
            dma((12,)),
        ],
        compiler_params=params(),
        cost_estimate=pl.CostEstimate(
            flops=3 * 10**10, bytes_accessed=4 * 10**7, transcendentals=4 * 10**6
        ),
        name="feed_forward",
    )(segment_ids, vec, stream_in, mix, dual_in, cot_stream, cot_dual, gb, gc)

    pq_shape = (pairs,) + slots + (3 * unit, LANES)
    scratch = [
        vm((pairs, 3, tokens, LANES)),
        vm(flat),
        vm(flat),
        vm(flat),
        vm(flat, f32),
        vm(flat),
        vm(ga_shape),
        vm((3,) + flat),
        vm((rows, length, LANES)),
        vm(pq_shape),
        dma((pairs, 4)),
        dma((6,)),
        dma((8,)),
    ]
    operands = (segment_ids, vg, qkv, feat, mix, grad_mixed, grad_one, stream_in, ga)
    cost = pl.CostEstimate(flops=2 * 10**10, bytes_accessed=3 * 10**7, transcendentals=2 * 10**7)
    if comm:
        tail = (9 * unit, width)
        tail_q = (3 * unit, LANES)
        stream_grad, tot, totq, vg = pl.pallas_call(
            functools.partial(backward_kernel, True, scale),
            out_shape=[
                shape(flat, f32),
                shape(tail, f32),
                shape((pairs,) + tail_q, f32),
                shape((16, width), f32),
            ],
            in_specs=[VMEM, VMEM] + [ANY] * 8,
            out_specs=[ANY] + [VMEM] * 3,
            scratch_shapes=scratch
            + [vm((3,) + s + (3 * unit, width)) for s in ((4, 4), (4, 4), (2, 4), (4,), (3,))]
            + [vm((pairs,) + s + tail_q) for s in ((4, 4), (4, 4), (2, 4), (4,), (3,))]
            + [vm((16, width), f32), vm((9, 16, width), f32)]
            + [dma((3, 7)), dma((3, 7)), dma((pairs, 7)), dma((pairs, 7)), dma((9,)), dma((9,))],
            compiler_params=params(collective_id=1, has_side_effects=True),
            cost_estimate=cost,
            name="backward_scatter",
        )(*operands, pg)
        outs = pl.pallas_call(
            update_kernel,
            out_shape=[shape(flat, f32), shape((3,), f32)]
            + [shape(w.shape, f32) for _ in range(3) for w in masters],
            in_specs=[VMEM] * 3 + [ANY] + [VMEM] * 15,
            out_specs=[ANY, pl.BlockSpec(memory_space=pltpu.SMEM)] + [VMEM] * 15,
            scratch_shapes=[vm(flat, f32), dma((2, 8))],
            compiler_params=params(),
            name="update",
        )(tot, totq, vg, stream_grad, *masters, *firsts[:4], firsts[4].reshape(1, -1), *seconds[:4], seconds[4].reshape(1, -1))
        stream_grad, root_means = outs[:2]
        grads, renewed, updated = (
            [v.reshape(w.shape) for v, w in zip(outs[k : k + 5], weights)] for k in (2, 7, 12)
        )
    else:
        stream_grad, pq, vg = pl.pallas_call(
            functools.partial(backward_kernel, False, scale),
            out_shape=[shape(flat, f32), shape(pq_shape, bf16), shape((16, width), f32)],
            in_specs=[VMEM, VMEM] + [ANY] * 7,
            out_specs=[ANY, ANY, VMEM],
            scratch_shapes=scratch,
            compiler_params=params(),
            cost_estimate=cost,
            name="backward",
        )(*operands)
        pq = jnp.moveaxis(pq.reshape(pairs, SLOTS, 3 * unit, LANES), 0, 2).reshape(SLOTS, 3 * unit, width)
        pg = pg.reshape(SLOTS, 9 * unit, width)
        partial = [
            unpack_columns(pq, 3),
            unpack_columns(pg[:, :unit], 1),
            unpack_columns(pg[:, unit : 5 * unit], blocks),
            pg[:, 5 * unit :].reshape(hidden, width),
            vg[:12].reshape(-1),
        ]
        grads = [
            lax.psum_scatter(g.astype(f32), AXES, scatter_dimension=0, tiled=True) for g in partial
        ]
        totals = lax.psum(vg[12, :4], AXES)
        root_means = jnp.sqrt(totals[1:] / totals[0])
        made = [adam(*four) for four in zip(weights, grads, firsts, seconds, RATES)]
        renewed, updated = ([m[k] for m in made] for k in range(2))
    return (stream_out, dual_out, stream_grad, root_means, *grads, *renewed, *updated)


def solution(mesh):
    sizes = dict(mesh.shape)
    comm = sizes["dp"] == 4 and sizes["fsdp"] == 8
    matrix, line = P(AXES, None), P(AXES)
    five = (matrix, matrix, matrix, matrix, line)
    in_specs = (matrix,) * 3 + five * 3 + (matrix, matrix)
    out_specs = (matrix,) * 3 + (P(),) + five * 3
    return jax.shard_map(
        functools.partial(per_device, comm),
        mesh=mesh,
        in_specs=in_specs,
        out_specs=out_specs,
        check_vma=False,
    )
```
